128 devices in a mesh: grp: 4 (over x_lo, core), dom: 32 (over x_hi, z, y).
Axes of the slice: x: 4 (x_hi: 2, x_lo: 2; x = x_hi * 2 + x_lo), y: 4, z: 4, core: 2. Of those that a mesh axis runs over, the one named last changes fastest.
Arguments:
- ice_depth: float32 [131072], P('dom'), may hold values from 1 to 3
- heat_state: float32 [20, 131072], P(None, 'dom'), may hold values from -1 to 1
- elevation_slope_components: float32 [2, 131072], P(None, 'dom'), may hold values from -3 to 3
- sliding_drag: float32 [131072], P('dom'), may hold values from 0.1 to 1
- adjacent_polygons: int32 [6, 131072], P(None, 'dom'), may hold values from 0 to 131071, as said below
- edge_timing_ratio: float32 [6, 131072], P(None, 'dom'), may hold values from 0.02 to 0.15
- edge_average_normal_speed: float32 [6, 131072], P(None, 'dom'), may hold values from -4 to 4
- tier_edge_normal_speed: float32 [20, 6, 131072], P('grp', None, 'dom'), may hold values from -4 to 4
- position_donor_polygons: int32 [32, 4, 32, 64], P('dom'), may hold values from -1 to 4095, as said below
- shaft_holding_position: int32 [128, 512], P('dom', 'grp'), may hold values from 0 to 2047, as said below
- prior_node_motion: float32 [2, 21, 128, 512], P(None, None, 'dom', 'grp'), may hold values from -3 to 3
Outputs:
- transported_ice_depth: float32 [131072], P('dom')
- transported_heat_state: float32 [20, 131072], P('grp', 'dom')
- node_velocity: float32 [2, 21, 128, 512], P(None, None, 'dom', 'grp')
- polygon_tier_motion: float32 [2, 20, 131072], P(None, 'grp', 'dom')
The draws below stay inside these ranges and needn't reach their ends.
Inputs may be any that keep to these rules, and one draw needn't show every extreme that they name: `adjacent_polygons`: each entry is the index of another cell at most 1024 positions away from its own cell in the global order; the distance 1024 occurs. `shaft_holding_position`: slot block p of a device's buffer (slots p * 64 to p * 64 + 63) holds data of owner partition p. The columns of one device take distinct slots; for each device one owner's block is full and the others hold at most 64 columns of it. `position_donor_polygons`: cells are numbered within partition p. An entry is -1 exactly when no column of device (g, d) uses that slot; a cell may be named by several slots or by none.
All inputs are finite; a program needn't handle non-finite values.
Results may differ from the reference program's by a relative error of at most 0.00002.
Values sent between devices are 32-bit elements; how exact they have to be, the bound alone decides.
No kernel may reach another device: no remote copies, remote signals or barrier semaphores. Data moves between devices by JAX's collectives and lax.ppermute only.
A program may use at most 64 MiB of HBM per device.

```python
import math
import jax
import jax.numpy as jnp
import numpy as np
from jax import lax

TIER_TOTAL = 20
K = 6
PICARD = 2
SWEEPS = 1
CELL_DEV = 4096
HX = 4
HY = 128
BLK = 64
RIM = 1024
POLYGON_TOTAL = 131072
NX = 128
NY = 512
N_GRP = 4
N_DOM = 32


def slot_routing(key):
    columns = HX * HY
    slot_count = N_DOM * BLK

    def per_device(device_key):
        full_key, order_key, other_key, cell_key = jax.random.split(device_key, 4)
        full_owner = jax.random.randint(full_key, (), 0, N_DOM)
        col_order = jax.random.permutation(order_key, columns).astype(jnp.int32)
        others = jax.random.permutation(other_key, (N_DOM - 1) * BLK)[:columns - BLK].astype(jnp.int32)
        owner_rank = others // BLK
        owner_real = owner_rank + (owner_rank >= full_owner).astype(jnp.int32)
        slot_taken = jnp.concatenate([full_owner * BLK + jnp.arange(BLK, dtype=jnp.int32), owner_real * BLK + others % BLK])
        column_slot = jnp.zeros((columns,), jnp.int32).at[col_order].set(slot_taken)
        slot_used = jnp.zeros((slot_count,), jnp.int32).at[slot_taken].set(1)
        cell_pick = jax.random.randint(cell_key, (slot_count,), 0, CELL_DEV)
        return (column_slot, jnp.where(slot_used > 0, cell_pick, -1).astype(jnp.int32))
    device_keys = jax.random.split(key, N_GRP * N_DOM)
    column_slot, slot_cell = jax.vmap(per_device)(device_keys)
    return (column_slot.reshape(N_GRP, N_DOM, HX, HY), slot_cell.reshape(N_GRP, N_DOM, N_DOM, BLK))


def draw_shaft_holding_position(key, part):
    column_slot, slot_cell = slot_routing(key)
    return jnp.transpose(column_slot, (1, 2, 0, 3)).reshape(NX, NY).astype(jnp.int32)


def draw_position_donor_polygons(key, part):
    column_slot, slot_cell = slot_routing(key)
    return jnp.transpose(slot_cell, (2, 0, 1, 3)).astype(jnp.int32)


def draw_adjacent_polygons(key, part):
    key = jax.random.fold_in(key, 11)
    offset_key, flip_key, anchor_key = jax.random.split(key, 3)
    cell_index = jnp.arange(POLYGON_TOTAL, dtype=jnp.int32)
    offsets = jax.random.randint(offset_key, (K, POLYGON_TOTAL), 1, RIM + 1)
    anchor = jax.random.randint(anchor_key, (), 0, RIM)
    offsets = offsets.at[0].set(jnp.where(cell_index % RIM == anchor, RIM, offsets[0]))
    sign_flip = jax.random.randint(flip_key, (K, POLYGON_TOTAL), 0, 2) * 2 - 1
    target = cell_index[None, :] + sign_flip * offsets
    target = jnp.where((target < 0) | (target >= POLYGON_TOTAL), cell_index[None, :] - sign_flip * offsets, target)
    return target.astype(jnp.int32)


def block_scale(key, extent, cuts, low, top_value):
    def one(position, shards_of):
        steps = jax.random.uniform(jax.random.fold_in(jax.random.fold_in(key, 6), position), (shards_of,), jnp.float32, low / len(cuts), top_value / len(cuts))
        return jnp.repeat(jnp.exp(steps), extent[position] // shards_of).reshape((-1,) + (1,) * (len(extent) - position - 1))

    gain = one(*cuts[0])
    for cut in cuts[1:]:
        gain = gain * one(*cut)
    return gain


def centred(rng, extent, spread, most, cuts=(), kind=jnp.bfloat16):
    factor_of = block_scale(rng, extent, cuts, -0.22, 0.18) if cuts else 1.0
    entries = jax.random.normal(rng, extent, jnp.float32) * spread * factor_of
    return jnp.minimum(jnp.maximum(entries, -most), most).astype(kind)


def setup_inputs(seed: int = 0) -> dict:
    splits = jax.random.split(jax.random.key(seed), 12)
    ice_depth = jnp.clip(1.0 + 2.0 * jax.random.uniform(splits[0], (POLYGON_TOTAL,), jnp.float32) ** block_scale(splits[0], (POLYGON_TOTAL,), ((0, 32),), -0.2, 0.2), 1.0, 3.0)
    heat_state = jnp.clip(jax.random.uniform(splits[1], (TIER_TOTAL, POLYGON_TOTAL), jnp.float32, -1.0, 1.0) * block_scale(splits[1], (TIER_TOTAL, POLYGON_TOTAL), ((1, 32),), -0.4, 0.0), -1.0, 1.0)
    elevation_slope_components = centred(splits[2], (2, POLYGON_TOTAL), 0.5, 3.0, ((1, 32),), jnp.float32)
    sliding_drag = jnp.clip(jnp.exp(math.log(1.0) - 2.3025851 * jax.random.uniform(splits[3], (POLYGON_TOTAL,), jnp.float32) ** block_scale(splits[3], (POLYGON_TOTAL,), ((0, 32),), -0.2, 0.2)), 0.1, 1.0)
    adjacent_polygons = draw_adjacent_polygons(jax.random.fold_in(splits[11], 71), 0)
    edge_timing_ratio = jnp.clip(jnp.exp(math.log(0.15) - 2.014903 * jax.random.uniform(splits[5], (K, POLYGON_TOTAL), jnp.float32) ** block_scale(splits[5], (K, POLYGON_TOTAL), ((1, 32),), -0.2, 0.2)), 0.02, 0.15)
    edge_average_normal_speed = centred(splits[6], (K, POLYGON_TOTAL), 1.0, 4.0, ((1, 32),), jnp.float32)
    tier_edge_normal_speed = centred(splits[7], (TIER_TOTAL, K, POLYGON_TOTAL), 1.0, 4.0, ((0, 4), (2, 32)), jnp.float32)
    position_donor_polygons = draw_position_donor_polygons(jax.random.fold_in(splits[11], 71), 0)
    shaft_holding_position = draw_shaft_holding_position(jax.random.fold_in(splits[11], 71), 0)
    prior_node_motion = centred(splits[10], (2, TIER_TOTAL + 1, NX, NY), 0.5, 3.0, ((2, 32), (3, 4)), jnp.float32)
    return {"ice_depth": ice_depth, "heat_state": heat_state, "elevation_slope_components": elevation_slope_components, "sliding_drag": sliding_drag, "adjacent_polygons": adjacent_polygons, "edge_timing_ratio": edge_timing_ratio, "edge_average_normal_speed": edge_average_normal_speed, "tier_edge_normal_speed": tier_edge_normal_speed, "position_donor_polygons": position_donor_polygons, "shaft_holding_position": shaft_holding_position, "prior_node_motion": prior_node_motion}


HSTEP = 0.25
OMEGA = 0.5
EPS_RATE = 0.01

def basis_tables():
    lower_point = 0.5 - 0.5 / math.sqrt(3.0)
    points = (lower_point, 1.0 - lower_point)
    table_x = np.zeros((8, 8))
    table_y = np.zeros((8, 8))
    table_z = np.zeros((8, 8))
    for qpoint in range(8):
        point_z, point_x, point_y = (points[qpoint // 4], points[qpoint // 2 % 2], points[qpoint % 2])
        for corner in range(8):
            upper_z, upper_x, upper_y = (corner // 4, corner // 2 % 2, corner % 2)
            value_z = point_z if upper_z else 1.0 - point_z
            value_x = point_x if upper_x else 1.0 - point_x
            value_y = point_y if upper_y else 1.0 - point_y
            slope_z = 1.0 if upper_z else -1.0
            slope_x = 1.0 if upper_x else -1.0
            slope_y = 1.0 if upper_y else -1.0
            table_x[qpoint, corner] = slope_x * value_y * value_z
            table_y[qpoint, corner] = value_x * slope_y * value_z
            table_z[qpoint, corner] = value_x * value_y * slope_z
    return (table_x, table_y, table_z)

def corner_sum(array):
    return array[..., :-1, :-1] + array[..., 1:, :-1] + array[..., :-1, 1:] + array[..., 1:, 1:]

def element_geometry(geometry_ext):
    tier_pile = geometry_ext.shape[0] - 1
    layer_depth = corner_sum(geometry_ext[0]) * (0.25 / tier_pile)
    hardness = jnp.exp(-0.25 * corner_sum(geometry_ext[1:]))
    return (layer_depth, hardness)

def corner_views(field_ext, tier_pile):
    span_x = field_ext.shape[2] - 1
    span_y = field_ext.shape[3] - 1
    corner_list = []
    for corner in range(8):
        upper_z, upper_x, upper_y = (corner // 4, corner // 2 % 2, corner % 2)
        corner_list.append(field_ext[:, upper_z:upper_z + tier_pile, upper_x:upper_x + span_x, upper_y:upper_y + span_y])
    return corner_list

def point_gradients(corner_list, tables, qpoint, layer_depth):
    table_x, table_y, table_z = tables
    grad_x = float(table_x[qpoint, 0]) * corner_list[0]
    grad_y = float(table_y[qpoint, 0]) * corner_list[0]
    grad_z = float(table_z[qpoint, 0]) * corner_list[0]
    for corner in range(1, 8):
        grad_x = grad_x + float(table_x[qpoint, corner]) * corner_list[corner]
        grad_y = grad_y + float(table_y[qpoint, corner]) * corner_list[corner]
        grad_z = grad_z + float(table_z[qpoint, corner]) * corner_list[corner]
    return (grad_x / HSTEP, grad_y / HSTEP, grad_z / layer_depth)

def effective_viscosity(corner_list, tables, layer_depth, hardness):
    result = []
    for qpoint in range(8):
        grad_x, grad_y, grad_z = point_gradients(corner_list, tables, qpoint, layer_depth)
        shear = grad_y[0] + grad_x[1]
        strain_rate = grad_x[0] * grad_x[0] + grad_y[1] * grad_y[1] + grad_x[0] * grad_y[1] + 0.25 * shear * shear + 0.25 * (grad_z[0] * grad_z[0] + grad_z[1] * grad_z[1]) + EPS_RATE
        result.append(0.5 * hardness * strain_rate ** (-1.0 / 3.0))
    return result

def element_forces(corner_list, tables, layer_depth, viscous):
    table_x, table_y, table_z = tables
    weight = layer_depth * (HSTEP * HSTEP / 8.0) / HSTEP
    forces = [jnp.zeros_like(corner_list[0]) for corner in range(8)]
    for qpoint in range(8):
        grad_x, grad_y, grad_z = point_gradients(corner_list, tables, qpoint, layer_depth)
        visc_point = viscous[qpoint]
        shear = visc_point * (grad_y[0] + grad_x[1])
        flux_x = jnp.stack([visc_point * (4.0 * grad_x[0] + 2.0 * grad_y[1]), shear]) * weight
        flux_y = jnp.stack([shear, visc_point * (4.0 * grad_y[1] + 2.0 * grad_x[0])]) * weight
        flux_z = jnp.stack([visc_point * grad_z[0], visc_point * grad_z[1]]) * (HSTEP * HSTEP / 8.0)
        for corner in range(8):
            forces[corner] = forces[corner] + float(table_x[qpoint, corner]) * flux_x + float(table_y[qpoint, corner]) * flux_y + float(table_z[qpoint, corner]) * flux_z
    return forces

def element_diagonal(tables, layer_depth, viscous):
    table_x, table_y, table_z = tables
    weight = layer_depth * (HSTEP * HSTEP / 8.0) / (HSTEP * HSTEP)
    vertical = HSTEP * HSTEP / 8.0 / layer_depth
    parts = [None] * 8
    for qpoint in range(8):
        visc_point = viscous[qpoint]
        for corner in range(8):
            along_x = float(table_x[qpoint, corner]) ** 2 * visc_point * weight
            along_y = float(table_y[qpoint, corner]) ** 2 * visc_point * weight
            along_z = float(table_z[qpoint, corner]) ** 2 * visc_point * vertical
            term = jnp.stack([4.0 * along_x + along_y + along_z, along_x + 4.0 * along_y + along_z])
            parts[corner] = term if parts[corner] is None else parts[corner] + term
    return parts

def gather_nodes(parts):
    span_x = parts[0].shape[2] - 1
    span_y = parts[0].shape[3] - 1
    summed = None
    for corner in range(8):
        upper_z, upper_x, upper_y = (corner // 4, corner // 2 % 2, corner % 2)
        padded = jnp.pad(parts[corner], ((0, 0), (upper_z, 1 - upper_z), (0, 0), (0, 0)))
        node_part = padded[:, :, 1 - upper_x:1 - upper_x + span_x, 1 - upper_y:1 - upper_y + span_y]
        summed = node_part if summed is None else summed + node_part
    return summed

def reference(ice_depth, heat_state, elevation_slope_components, sliding_drag, adjacent_polygons, edge_timing_ratio, edge_average_normal_speed, tier_edge_normal_speed, position_donor_polygons, shaft_holding_position, prior_node_motion):
    beside_thick = ice_depth[adjacent_polygons]
    transported_ice_depth = ice_depth - lax.optimization_barrier(jnp.sum(edge_timing_ratio * (jnp.maximum(edge_average_normal_speed, 0.0) * ice_depth[None] + jnp.minimum(edge_average_normal_speed, 0.0) * beside_thick), 0))
    adjacent_heat_state = heat_state[:, adjacent_polygons]
    transported_heat_state = heat_state - lax.optimization_barrier(jnp.sum(edge_timing_ratio[None] * (jnp.maximum(tier_edge_normal_speed, 0.0) * heat_state[:, None] + jnp.minimum(tier_edge_normal_speed, 0.0) * adjacent_heat_state), 1))
    shaft_fields = jnp.concatenate([ice_depth[None], elevation_slope_components, sliding_drag[None], heat_state], 0)
    owner_dom = shaft_holding_position // BLK
    slot_place = shaft_holding_position % BLK
    row_domain = jnp.arange(NX, dtype=jnp.int32) // HX
    col_group = jnp.arange(NY, dtype=jnp.int32) // HY
    local_cell = position_donor_polygons[owner_dom, col_group[None, :], row_domain[:, None], slot_place]
    cell_of_column = (owner_dom * CELL_DEV + local_cell).astype(jnp.int32)
    column = shaft_fields[:, cell_of_column]
    column_thick = column[0]
    column_slope = column[1:3]
    column_friction = column[3]
    geometry = jnp.concatenate([column[0:1], column[4:]], 0)
    geometry_ext = jnp.pad(geometry, ((0, 0), (1, 1), (1, 1)))
    layer_depth, hardness = element_geometry(geometry_ext)
    tables = basis_tables()
    driving = -(column_thick[None] * column_slope)[:, None]
    current_guess = prior_node_motion
    for picard_step in range(PICARD):
        for sweep_step in range(SWEEPS):
            field_ext = jnp.pad(current_guess, ((0, 0), (0, 0), (1, 1), (1, 1)))
            corner_list = corner_views(field_ext, TIER_TOTAL)
            if sweep_step == 0:
                viscous = effective_viscosity(corner_list, tables, layer_depth, hardness)
                diagonal = gather_nodes(element_diagonal(tables, layer_depth, viscous))
                diagonal = diagonal.at[:, 0].add(column_friction)
            forces = gather_nodes(element_forces(corner_list, tables, layer_depth, viscous))
            forces = forces.at[:, 0].add(column_friction * current_guess[:, 0])
            current_guess = current_guess + OMEGA * (driving - forces) / diagonal
    layer_mean = 0.5 * (current_guess[:, :-1] + current_guess[:, 1:])
    cell_ids = cell_of_column.reshape(-1)
    cell_sums = jax.vmap(lambda values_row: jax.ops.segment_sum(values_row, cell_ids, POLYGON_TOTAL))(layer_mean.reshape(2 * TIER_TOTAL, -1))
    counts = jax.ops.segment_sum(jnp.ones(cell_ids.shape, jnp.float32), cell_ids, POLYGON_TOTAL)
    polygon_tier_motion = (cell_sums / jnp.maximum(counts, 1.0)).reshape(2, TIER_TOTAL, POLYGON_TOTAL)
    return (transported_ice_depth, transported_heat_state, current_guess, polygon_tier_motion)
```

```python
import math

import jax
import jax.numpy as jnp
from jax import lax
from jax.experimental import pallas as pl
from jax.experimental.pallas import tpu as pltpu
from jax.sharding import PartitionSpec as P

KAPPA = 1.0 / math.sqrt(3.0)
EPS_RATE = 0.01
LOG2E = math.log2(math.e)
SCALE = 4096.0
LAYERS = 20
LEVELS = 21
FIELDS = 24
PAIRS = 12
BLOCK_ROWS = 40
MSG_ROWS = 136
SPLITS = 2
f32 = jnp.float32
bf16 = jnp.bfloat16
PARAMS = pltpu.CompilerParams(vmem_limit_bytes=32 * 1024 * 1024)


def lanes_of(table, index):
    return jnp.take_along_axis(table, index, axis=1, mode="promise_in_bounds")


def iota(shape, dim):
    return lax.broadcasted_iota(jnp.int32, shape, dim)


def row_of(ref, row, rows):
    return jnp.broadcast_to(ref[pl.ds(row, 1), :], (rows, 128))


def halves(first, second, lane):
    even = jnp.where(lane < 64, first, pltpu.roll(second, 64, 1))
    odd = jnp.where(lane < 64, pltpu.roll(first, 64, 1), second)
    return even, odd


def pack_kernel(ice, heat, slope, drag, donor, shaft, prior, out, near, far, own):
    g = lax.axis_index("grp")
    d = lax.axis_index("dom")
    ids = jnp.concatenate(
        [donor[0, g, pl.ds(0, 16, stride=2), :], donor[0, g, pl.ds(1, 16, stride=2), :]], axis=1
    )
    ids = jnp.maximum(ids, 0)
    high = ids >> 7
    low = ids & 127
    lane = iota((16, 128), 1)

    def table(field, k):
        if field == 0:
            part = ice[k : k + 1, :]
        elif field < 3:
            part = slope[field - 1 : field, 128 * k : 128 * k + 128]
        elif field == 3:
            part = drag[k : k + 1, :]
        else:
            part = heat[field - 4 : field - 3, 128 * k : 128 * k + 128]
        return jnp.broadcast_to(part, (16, 128))

    for pair0 in range(0, PAIRS, 3):
        pairs = range(pair0, pair0 + 3)
        fields = [p for p in pairs] + [p + PAIRS for p in pairs]
        found = {f: jnp.zeros((16, 128), f32) for f in fields}
        for k in range(32):
            here = high == k
            for f in fields:
                found[f] = jnp.where(here, lanes_of(table(f, k), low), found[f])
        for p in pairs:
            even, odd = halves(found[p], found[p + PAIRS], lane)
            out[pl.ds(12 + p, 16, stride=80), :] = even
            out[pl.ds(40 + p, 16, stride=80), :] = even
            out[pl.ds(64 + p, 15, stride=80), :] = even[1:]
            out[pl.ds(52 + p, 16, stride=80), :] = odd
            out[pl.ds(24 + p, 16, stride=80), :] = odd
            out[pl.ds(80 + p, 15, stride=80), :] = odd[:15]
    out[0:12, :] = jnp.zeros((12, 128), f32)
    out[31 * 40 + 24 : 31 * 40 + 36, :] = jnp.zeros((12, 128), f32)
    for k in range(32):
        out[40 * k + 36 : 40 * k + 40, :] = jnp.zeros((4, 128), f32)

    def message(msg, row0, chunk0):
        for c in range(2):
            for z in range(LEVELS):
                at = 2 * (c * LEVELS + z)
                msg[at : at + 2, :] = prior[c, z, row0 : row0 + 2, :]
        msg[84:86, :] = shaft[row0 : row0 + 2, :].astype(f32)
        msg[86:88, :] = jnp.zeros((2, 128), f32)
        for i in range(6):
            msg[88 + 8 * i : 96 + 8 * i, :] = own[i, chunk0 : chunk0 + 8, :]

    own[0] = ice[...]
    for part in range(4):

        @pl.when(g == part)
        def _():
            for i in range(5):
                layer = 5 * part + i
                for k in range(32):
                    own[i + 1, k : k + 1, :] = heat[layer : layer + 1, 128 * k : 128 * k + 128]

    even_device = d % 2 == 0

    @pl.when(even_device)
    def _():
        message(near, 2, 24)
        message(far, 0, 0)

    @pl.when(jnp.logical_not(even_device))
    def _():
        message(near, 0, 0)
        message(far, 2, 24)


def advect_kernel(own, adjacent, ratio, mean_speed, tier_speed, near, far, depth_out, heat_out, ext):
    d = lax.axis_index("dom")
    even_device = d % 2 == 0
    for i in range(6):
        a = near[88 + 8 * i : 96 + 8 * i, :]
        b = far[88 + 8 * i : 96 + 8 * i, :]
        ext[i, 0:8, :] = jnp.where(even_device, b, a)
        ext[i, 40:48, :] = jnp.where(even_device, a, b)
        ext[i, 8:40, :] = own[i]

    @pl.loop(0, 32)
    def _(k):
        span = pl.ds(pl.multiple_of(128 * k, 128), 128)
        cell = adjacent[:, span] - (d * 4096 - 1024)
        low = cell & 127
        turn = (cell >> 7) - k
        beside = [jnp.zeros((6, 128), f32) for _ in range(6)]
        for r in range(17):
            here = turn == r
            for i in range(6):
                rows = jnp.broadcast_to(ext[i, pl.ds(k + r, 1), :], (6, 128))
                beside[i] = jnp.where(here, lanes_of(rows, low), beside[i])
        weight = ratio[:, span]
        for i in range(6):
            here = ext[i, pl.ds(k + 8, 1), :]
            speed = mean_speed[:, span] if i == 0 else tier_speed[i - 1, :, span]
            flow = weight * (jnp.maximum(speed, 0.0) * here + jnp.minimum(speed, 0.0) * beside[i])
            result = here - jnp.sum(flow, axis=0, keepdims=True)
            if i == 0:
                depth_out[pl.ds(k, 1), :] = result
            else:
                heat_out[i - 1 : i, span] = result


def column_kernel(arrived, shaft, near, far, prior, geo, vext, edge, slots):
    d = lax.axis_index("dom")
    even_device = d % 2 == 0
    row = iota((8, 128), 0)
    lane = iota((8, 128), 1)

    def sides(start, count):
        a = near[start : start + count, :]
        b = far[start : start + count, :]
        return jnp.where(even_device, b, a), jnp.where(even_device, a, b)

    left, right = sides(84, 2)
    slots[0:2, :] = left.astype(jnp.int32)
    slots[2:6, :] = shaft[...]
    slots[6:8, :] = right.astype(jnp.int32)
    slot = slots[...]
    owner = slot >> 6
    low = slot & 63
    low2 = low + 64
    found = [jnp.zeros((8, 128), f32) for _ in range(FIELDS)]
    upper = row < 2
    middle = row < 6
    for p in range(32):
        here = owner == p
        for f in range(PAIRS):
            at = BLOCK_ROWS * p + f
            rows = jnp.where(
                upper,
                row_of(arrived, at, 8),
                jnp.where(middle, row_of(arrived, at + 12, 8), row_of(arrived, at + 24, 8)),
            )
            found[f] = jnp.where(here, lanes_of(rows, low), found[f])
            found[f + PAIRS] = jnp.where(here, lanes_of(rows, low2), found[f + PAIRS])
    first = jnp.where(d == 0, 2, 0)
    last = jnp.where(d == lax.axis_size("dom") - 1, 5, 7)
    inside = jnp.logical_and(row >= first, row <= last)
    found = [jnp.where(inside, value, 0.0) for value in found]
    load_u = -(found[0] * found[1]) * SCALE
    load_v = -(found[0] * found[2]) * SCALE
    friction = found[3] * SCALE
    geo[0] = found[0]
    geo[1] = load_u
    geo[2] = load_v
    geo[3] = friction
    for l in range(LAYERS):
        geo[4 + l] = found[4 + l]
    for cz in range(2 * LEVELS):
        left, right = sides(2 * cz, 2)
        vext[cz, 0:2, :] = left
        vext[cz, 2:6, :] = prior[cz // LEVELS, cz % LEVELS]
        vext[cz, 6:8, :] = right
    group = lane // LEVELS
    pick = jnp.where(group < 2, group, jnp.where(group < 4, 124 + group, 0))
    level = lane - group * LEVELS
    for c in range(2):
        value = jnp.zeros((8, 128), f32)
        for z in range(LEVELS):
            value = jnp.where(level == z, lanes_of(vext[c * LEVELS + z], pick), value)
        edge[8 * c : 8 * c + 8, :] = value
    value = jnp.zeros((8, 128), f32)
    for l in range(LAYERS):
        value = jnp.where(level == l, lanes_of(found[4 + l], pick), value)
    edge[16:24, :] = value
    edge[24:32, :] = lanes_of(found[0], pick)
    edge[32:40, :] = lanes_of(load_u, pick)
    edge[40:48, :] = lanes_of(load_v, pick)
    edge[48:56, :] = jnp.where(level == 0, lanes_of(friction, pick), 0.0)


def interpolate(a, b):
    diff = b - a
    total = a + b
    part = KAPPA * diff
    return diff, total - part, total + part


def spread(a, b):
    total = a + b
    part = KAPPA * (a - b)
    return total, part


def spread_square(a, b):
    total = (1.0 + KAPPA * KAPPA) * (a + b)
    part = (2.0 * KAPPA) * (a - b)
    return total + part, total - part


def up_x(value):
    return pltpu.roll(value, 7, 0)


def down_x(value):
    return pltpu.roll(value, 1, 0)


def level_terms(value, value_y):
    dy, ya, yb = interpolate(value, value_y)
    _, along_y0, along_y1 = interpolate(dy, up_x(dy))
    along_x0, z00, z10 = interpolate(ya, up_x(ya))
    along_x1, z01, z11 = interpolate(yb, up_x(yb))
    return [along_x0, along_x1, along_y0, along_y1, z00, z01, z10, z11]


def element(low_u, top_u, low_v, top_v, hardness, inverse2, keep=None):
    def gradients(low, top):
        x = [interpolate(low[q], top[q])[1:] for q in (0, 1)]
        y = [interpolate(low[2 + q], top[2 + q])[1:] for q in (0, 1)]
        z = [top[4 + q] - low[4 + q] for q in range(4)]
        return x, y, z

    ux, uy, uz = gradients(low_u, top_u)
    vx, vy, vz = gradients(low_v, top_v)
    vertical = [
        (uz[q] * uz[q] + vz[q] * vz[q]) * (0.25 * inverse2) + EPS_RATE for q in range(4)
    ]
    vy2 = [[vy[a][b] * vy[a][b] for b in (0, 1)] for a in (0, 1)]
    ex, ey, ez = {}, {}, {}
    ev, eu, wx, wy = {}, {}, {}, {}

    def put(store, key, value):
        store[key] = value if key not in store else store[key] + value

    for qx in (0, 1):
        for qy in (0, 1):
            for qz in (0, 1):
                a = ux[qy][qz]
                b = vy[qx][qz]
                shear = uy[qx][qz] + vx[qy][qz]
                rate = (
                    a * (a + b) + vy2[qx][qz] + 0.25 * (shear * shear) + vertical[2 * qx + qy]
                )
                eta = jnp.exp2(hardness - jnp.log2(rate) * (1.0 / 3.0))
                if keep is not None:
                    eta = jnp.where(keep, eta, 0.0)
                put(ex, (qy, qz), eta)
                put(ey, (qx, qz), eta)
                put(ez, 2 * qx + qy, eta)
                put(ev, (qy, qz), eta * b)
                put(eu, (qx, qz), eta * a)
                w = eta * shear
                put(wx, (qy, qz), w)
                put(wy, (qx, qz), w)
    ez = [ez[q] * inverse2 for q in range(4)]
    lows, tops = [], []

    def add_spread(a, b):
        total, part = spread(a, b)
        lows.append(total + part)
        tops.append(total - part)

    def flux(e, g, s):
        half = (g + g) * e + s
        return half + half

    for q in (0, 1):
        add_spread(*[flux(ex[q, z], ux[q][z], ev[q, z]) for z in (0, 1)])
    for q in (0, 1):
        add_spread(wy[q, 0], wy[q, 1])
    for q in range(4):
        value = ez[q] * uz[q]
        lows.append(-value)
        tops.append(value)
    for q in (0, 1):
        add_spread(wx[q, 0], wx[q, 1])
    for q in (0, 1):
        add_spread(*[flux(ey[q, z], vy[q][z], eu[q, z]) for z in (0, 1)])
    for q in range(4):
        value = ez[q] * vz[q]
        lows.append(-value)
        tops.append(value)
    for q in (0, 1):
        a, b = spread_square(ex[q, 0], ex[q, 1])
        lows.append(a)
        tops.append(b)
    for q in (0, 1):
        a, b = spread_square(ey[q, 0], ey[q, 1])
        lows.append(a)
        tops.append(b)
    lows += ez
    tops += ez
    return lows, tops


def node_parts(acc):
    results = []
    for c in (0, 1):
        x0, x1, y0, y1, z00, z01, z10, z11 = acc[8 * c : 8 * c + 8]
        total, part = spread(y0, y1)
        hd = (total + part) + down_x(total - part)
        both = []
        for along, a, b in ((x0, z00, z10), (x1, z01, z11)):
            total, part = spread(a, b)
            part = part - along
            both.append((total + part) + down_x(total - part))
        total, part = spread(both[0], both[1])
        part = part - hd
        results.append((total + part, total - part))
    x0, x1, y0, y1, z00, z01, z10, z11 = acc[16:24]
    hx = [x0 + down_x(x0), x1 + down_x(x1)]
    a, b = spread_square(y0, y1)
    hy = a + down_x(b)
    hz = []
    for za, zb in ((z00, z10), (z01, z11)):
        a, b = spread_square(za, zb)
        hz.append(a + down_x(b))
    a, b = spread_square(4.0 * hx[0] + hz[0], 4.0 * hx[1] + hz[1])
    results.append((a + hy, b + hy))
    hy4 = 4.0 * hy
    a, b = spread_square(hx[0] + hz[0], hx[1] + hz[1])
    results.append((a + hy4, b + hy4))
    return results


def ice_kernel(geo, vext, edges, shaft, out_v, send, hard, first, second, means):
    g = lax.axis_index("grp")
    d = lax.axis_index("dom")
    groups = lax.axis_size("grp")
    domains = lax.axis_size("dom")
    row = iota((8, 128), 0)
    lane = iota((8, 128), 1)
    group = lane // LEVELS
    level = lane - group * LEVELS

    def at_lane(value, index):
        return lanes_of(value, jnp.full((8, 128), index, jnp.int32))

    base = 56 * g
    before = pl.multiple_of(jnp.maximum(base - 56, 0), 8)
    after = pl.multiple_of(jnp.minimum(base + 56, 56 * (groups - 1)), 8)

    def edge_field(i):
        own = edges[pl.ds(pl.multiple_of(base + 8 * i, 8), 8), :]
        left = jnp.where(g > 0, edges[pl.ds(before + 8 * i, 8), :], 0.0)
        right = jnp.where(g < groups - 1, edges[pl.ds(after + 8 * i, 8), :], 0.0)
        return jnp.where(
            lane < 42,
            pltpu.roll(left, 86, 1),
            jnp.where(
                lane < 63,
                pltpu.roll(own, 42, 1),
                jnp.where(lane < 84, own, pltpu.roll(right, 84, 1)),
            ),
        )

    edge_u, edge_v, edge_t, edge_h, edge_fu, edge_fv, edge_b = [edge_field(i) for i in range(7)]

    def up_y(value, beyond):
        return jnp.where(lane == 127, beyond, pltpu.roll(value, 127, 1))

    def edge_up(value):
        return pltpu.roll(value, 107, 1)

    def corners(value, value_y):
        pair = value + value_y
        return pair + up_x(pair)

    def geometry(depth4):
        dz = depth4 * (0.25 / LAYERS)
        dz = jnp.where(dz > 0.0, dz, 1.0)
        inverse = 0.25 / dz
        return jnp.log2(dz * 16.0), inverse * inverse

    depth = geo[0]
    main_log, main_inv2 = geometry(corners(depth, up_y(depth, at_lane(edge_h, 84))))
    edge_log, edge_inv2 = geometry(corners(edge_h, edge_up(edge_h)))
    edge_hard = edge_log - (0.25 * LOG2E) * corners(edge_t, edge_up(edge_t))

    @pl.loop(0, LAYERS)
    def _(l):
        warm = geo[4 + l]
        hard[l] = main_log - (0.25 * LOG2E) * corners(warm, up_y(warm, at_lane(edge_t, 84 + l)))

    load_u = geo[1]
    load_v = geo[2]
    friction = geo[3]
    not_top = jnp.logical_and(level != LAYERS, lane < 6 * LEVELS)
    first_row = jnp.where(d == 0, 2, 1)
    last_row = jnp.where(d == domains - 1, 5, 6)
    inside = jnp.logical_and(row >= first_row, row <= last_row)
    edge_inside = jnp.logical_and(
        inside,
        jnp.logical_or(
            jnp.logical_and(group == 1, g > 0),
            jnp.logical_and(group == 4, g < groups - 1),
        ),
    )

    def edge_parts(u, v):
        low_u = level_terms(u, edge_up(u))
        low_v = level_terms(v, edge_up(v))
        top_u = [pltpu.roll(t, 127, 1) for t in low_u]
        top_v = [pltpu.roll(t, 127, 1) for t in low_v]
        lows, tops = element(low_u, top_u, low_v, top_v, edge_hard, edge_inv2, not_top)
        acc = [a + pltpu.roll(b, 1, 1) for a, b in zip(lows, tops)]
        return node_parts(acc)

    def stepped(value, load, force, diagonal, drag):
        return value + 0.5 * (load - force - drag * value) / (diagonal + drag)

    def sweep(source, target, eu, ev, parts, keep):
        beyond = [part[1] for part in parts]

        def node(z, acc, drag):
            results = node_parts(acc)
            fu, fv, du, dv = [
                a + jnp.where(lane == 0, at_lane(e, 42 - LEVELS + z), pltpu.roll(b, 1, 1))
                for (a, b), e in zip(results, beyond)
            ]
            u = stepped(source[z], load_u, fu, du, drag)
            v = stepped(source[LEVELS + z], load_v, fv, dv, drag)
            target[z] = jnp.where(keep, u, 0.0)
            target[LEVELS + z] = jnp.where(keep, v, 0.0)

        def terms(z):
            u = source[z]
            v = source[LEVELS + z]
            return level_terms(u, up_y(u, at_lane(eu, 84 + z))) + level_terms(
                v, up_y(v, at_lane(ev, 84 + z))
            )

        def body(z, carry):
            low, tops = carry[:16], carry[16:]
            top = terms(z + 1)
            lows, next_tops = element(low[:8], top[:8], low[8:], top[8:], hard[z], main_inv2)
            node(z, [a + b for a, b in zip(lows, tops)], jnp.where(z == 0, friction, 0.0))
            return (*top, *next_tops)

        zero = jnp.zeros((8, 128), f32)
        carry = lax.fori_loop(0, LAYERS, body, (*terms(0), *([zero] * 24)))
        node(LAYERS, list(carry[16:]), zero)

    parts = edge_parts(edge_u, edge_v)
    sweep(vext, first, edge_u, edge_v, parts, inside)

    def edge_final(c, value, load):
        (fa, fb), (da, db) = parts[c], parts[2 + c]
        force = fa + pltpu.roll(fb, LEVELS, 1)
        diagonal = da + pltpu.roll(db, LEVELS, 1)
        return jnp.where(edge_inside, stepped(value, load, force, diagonal, edge_b), 0.0)

    edge_u = edge_final(0, edge_u, edge_fu)
    edge_v = edge_final(1, edge_v, edge_fv)
    for z in range(LEVELS):
        here = lane == 42 + z
        edge_u = jnp.where(here, at_lane(first[z], 0), edge_u)
        edge_v = jnp.where(here, at_lane(first[LEVELS + z], 0), edge_v)
    parts = edge_parts(edge_u, edge_v)
    own_rows = jnp.logical_and(row >= 2, row < 6)
    sweep(first, second, edge_u, edge_v, parts, own_rows)
    for c in range(2):
        for z in range(LEVELS):
            out_v[c, z] = second[c * LEVELS + z, 2:6, :]
    for c in range(2):
        for l in range(LAYERS):
            at = c * LEVELS + l
            means[8 * (c * LAYERS + l) : 8 * (c * LAYERS + l) + 8, :] = 0.5 * (
                second[at] + second[at + 1]
            )

    slot_row = iota((16, 128), 0)
    place = iota((16, 128), 1).astype(f32)
    low_row = iota((128, 128), 0)
    where_from = jnp.zeros((32, 128), f32)
    for x in range(4):
        slot = shaft[x : x + 1, :]
        here = slot_row == jnp.broadcast_to(slot >> 7, (16, 128))
        left = jnp.concatenate(
            [jnp.where(here, float(x), 0.0), jnp.where(here, place, 0.0)], axis=0
        )
        right = jnp.where(low_row == jnp.broadcast_to(slot & 127, (128, 128)), 1.0, 0.0)
        where_from = where_from + lax.dot_general(
            left.astype(bf16),
            right.astype(bf16),
            (((1,), (1,)), ((), ())),
            preferred_element_type=f32,
        )
    from_x = where_from[0:16].astype(jnp.int32)
    from_y = where_from[16:32].astype(jnp.int32) & 127
    lane16 = iota((16, 128), 1)
    here = [from_x == x for x in range(4)]
    send[...] = jnp.zeros(send.shape, f32)
    for l in range(LAYERS):
        pair = []
        for c in range(2):
            at = 8 * (c * LAYERS + l) + 2
            value = lanes_of(row_of(means, at, 16), from_y)
            for x in range(1, 4):
                value = jnp.where(here[x], lanes_of(row_of(means, at + x, 16), from_y), value)
            pair.append(value)
        even, odd = halves(pair[0], pair[1], lane16)
        start = (l // 5) * 256 + l % 5
        send[pl.ds(start, 16, stride=16), :] = even
        send[pl.ds(start + 8, 16, stride=16), :] = odd


def total_kernel(arrived, donor, out, ids, left, right, sums):
    lane = iota((8, 128), 1)
    row = iota((8, 128), 0)
    row256 = iota((256, 128), 0)
    for g in range(4):
        ids[16 * g : 16 * g + 16, :] = jnp.concatenate(
            [donor[0, g, pl.ds(0, 16, stride=2), :], donor[0, g, pl.ds(1, 16, stride=2), :]],
            axis=1,
        )

    @pl.loop(0, 8)
    def _(step):
        for part in range(8):
            chunk = 8 * step + part
            span = slice(128 * part, 128 * part + 128)
            x = arrived[pl.ds(pl.multiple_of(16 * chunk, 16), 16), :]
            u, v = halves(x[:8], x[8:], lane)
            u = jnp.where(row < 5, u, jnp.where(row == 5, 1.0, 0.0))
            v = jnp.where(row < 5, v, 0.0)
            rest = jnp.concatenate([u, v], axis=0)
            values = []
            for s in range(SPLITS):
                piece = rest.astype(bf16)
                values.append(piece)
                rest = rest - piece.astype(f32)
            cell = ids[pl.ds(chunk, 1), :]
            high = jnp.broadcast_to(cell >> 8, (16, 128))
            low = jnp.broadcast_to(cell & 255, (256, 128))
            right[:, span] = jnp.where(row256 == low, 1.0, 0.0).astype(bf16)
            for h in range(16):
                here = jnp.where(high == h, 1.0, 0.0).astype(bf16)
                for s in range(SPLITS):
                    at = 16 * (SPLITS * h + s)
                    left[at : at + 16, span] = values[s] * here
        product = lax.dot_general(
            left[...], right[...], (((1,), (1,)), ((), ())), preferred_element_type=f32
        )

        @pl.when(step == 0)
        def _():
            sums[...] = product

        @pl.when(step > 0)
        def _():
            sums[...] += product

    for h in range(16):
        at = 16 * SPLITS * h
        total = sums[at : at + 16, :]
        for s in range(1, SPLITS):
            total = total + sums[at + 16 * s : at + 16 * s + 16, :]
        count = jnp.maximum(total[5:6, :], 1.0)
        span = slice(256 * h, 256 * h + 256)
        out[0, :, span] = total[0:5, :] / count
        out[1, :, span] = total[8:13, :] / count


def shape(*sizes):
    return jax.ShapeDtypeStruct(sizes, f32)


def near_pairs(count):
    even = [(i, i ^ 1) for i in range(count)]
    odd = []
    for i in range(1, count - 1, 2):
        odd += [(i, i + 1), (i + 1, i)]
    return even, odd


def shards(
    ice_depth,
    heat_state,
    elevation_slope_components,
    sliding_drag,
    adjacent_polygons,
    edge_timing_ratio,
    edge_average_normal_speed,
    tier_edge_normal_speed,
    position_donor_polygons,
    shaft_holding_position,
    prior_node_motion,
):
    ice = ice_depth.reshape(32, 128)
    drag = sliding_drag.reshape(32, 128)
    outgoing, near, far, own = pl.pallas_call(
        pack_kernel,
        out_shape=(
            shape(32 * BLOCK_ROWS, 128),
            shape(MSG_ROWS, 128),
            shape(MSG_ROWS, 128),
            shape(6, 32, 128),
        ),
        compiler_params=PARAMS,
        name="pack",
    )(
        ice,
        heat_state,
        elevation_slope_components,
        drag,
        position_donor_polygons,
        shaft_holding_position,
        prior_node_motion,
    )
    arrived = lax.all_to_all(outgoing, "dom", split_axis=0, concat_axis=0, tiled=True)
    even, odd = near_pairs(lax.axis_size("dom"))
    near = lax.ppermute(near, "dom", even)
    far = lax.ppermute(far, "dom", odd)
    geo, vext, edge = pl.pallas_call(
        column_kernel,
        out_shape=(shape(FIELDS, 8, 128), shape(2 * LEVELS, 8, 128), shape(56, 128)),
        scratch_shapes=[pltpu.VMEM((8, 128), jnp.int32)],
        compiler_params=PARAMS,
        name="columns",
    )(arrived, shaft_holding_position, near, far, prior_node_motion)
    edges = lax.all_gather(edge, "grp", axis=0, tiled=True)
    node_velocity, send = pl.pallas_call(
        ice_kernel,
        out_shape=(shape(2, LEVELS, 4, 128), shape(1024, 128)),
        scratch_shapes=[
            pltpu.VMEM((LAYERS, 8, 128), f32),
            pltpu.VMEM((2 * LEVELS, 8, 128), f32),
            pltpu.VMEM((2 * LEVELS, 8, 128), f32),
            pltpu.VMEM((2 * LAYERS * 8, 128), f32),
        ],
        compiler_params=PARAMS,
        name="velocity",
    )(geo, vext, edges, shaft_holding_position)
    back = lax.all_to_all(send, ("grp", "dom"), split_axis=0, concat_axis=0, tiled=True)
    depth, heat = pl.pallas_call(
        advect_kernel,
        out_shape=(shape(32, 128), shape(5, 4096)),
        scratch_shapes=[pltpu.VMEM((6, 48, 128), f32)],
        compiler_params=PARAMS,
        name="advect",
    )(
        own,
        adjacent_polygons,
        edge_timing_ratio,
        edge_average_normal_speed,
        tier_edge_normal_speed,
        near,
        far,
    )
    tier_motion = pl.pallas_call(
        total_kernel,
        out_shape=shape(2, 5, 4096),
        scratch_shapes=[
            pltpu.VMEM((64, 128), jnp.int32),
            pltpu.VMEM((256 * SPLITS, 1024), bf16),
            pltpu.VMEM((256, 1024), bf16),
            pltpu.VMEM((256 * SPLITS, 256), f32),
        ],
        compiler_params=PARAMS,
        name="totals",
    )(back, position_donor_polygons)
    return (depth.reshape(4096), heat, node_velocity, tier_motion)


def solution(mesh):
    in_specs = (
        P("dom"),
        P(None, "dom"),
        P(None, "dom"),
        P("dom"),
        P(None, "dom"),
        P(None, "dom"),
        P(None, "dom"),
        P("grp", None, "dom"),
        P("dom", None, None, None),
        P("dom", "grp"),
        P(None, None, "dom", "grp"),
    )
    out_specs = (P("dom"), P("grp", "dom"), P(None, None, "dom", "grp"), P(None, "grp", "dom"))
    return jax.shard_map(shards, mesh=mesh, in_specs=in_specs, out_specs=out_specs, check_vma=False)
```

```python
import math

import jax
import jax.numpy as jnp
from jax import lax
from jax.experimental import pallas as pl
from jax.experimental.pallas import tpu as pltpu
from jax.sharding import PartitionSpec as P

KAPPA = 1.0 / math.sqrt(3.0)
EPS_RATE = 0.01
LOG2E = math.log2(math.e)
SCALE = 4096.0
LAYERS = 20
LEVELS = 21
FIELDS = 24
PAIRS = 12
BLOCK_ROWS = 40
MSG_ROWS = 136
SPLITS = 2
STEPS = 4
UNROLL = 4
f32 = jnp.float32
bf16 = jnp.bfloat16
PARAMS = pltpu.CompilerParams(vmem_limit_bytes=32 * 1024 * 1024)
WIDE = pltpu.CompilerParams(vmem_limit_bytes=60 * 1024 * 1024)


def lanes_of(table, index):
    return jnp.take_along_axis(table, index, axis=1, mode="promise_in_bounds")


def iota(shape, dim):
    return lax.broadcasted_iota(jnp.int32, shape, dim)


def row_of(ref, row, rows):
    return jnp.broadcast_to(ref[pl.ds(row, 1), :], (rows, 128))


def halves(first, second, lane):
    even = jnp.where(lane < 64, first, pltpu.roll(second, 64, 1))
    odd = jnp.where(lane < 64, pltpu.roll(first, 64, 1), second)
    return even, odd


def joined_rows(rows):
    return jnp.concatenate([rows[pl.ds(0, 16, stride=2), :], rows[pl.ds(1, 16, stride=2), :]], axis=1)


def pack_kernel(
    ice_in, heat_in, slope_in, drag_in, donor_in, shaft_in, prior_in, out, near, far, own,
    ice, heat, slope, drag, donor, shaft, prior, arrivals,
):
    g = lax.axis_index("grp")
    d = lax.axis_index("dom")
    pairs = (
        (donor_in.at[0, g], donor),
        (ice_in, ice),
        (slope_in, slope),
        (drag_in, drag),
        (heat_in, heat),
        (shaft_in, shaft),
        (prior_in, prior),
    )
    copies = [pltpu.make_async_copy(a, b, arrivals.at[i]) for i, (a, b) in enumerate(pairs)]
    for copy in copies:
        copy.start()
    out[0:12, :] = jnp.zeros((12, 128), f32)
    out[31 * 40 + 24 : 31 * 40 + 36, :] = jnp.zeros((12, 128), f32)
    for k in range(32):
        out[40 * k + 36 : 40 * k + 40, :] = jnp.zeros((4, 128), f32)
    for copy in copies:
        copy.wait()
    ids = joined_rows(donor)
    ids = jnp.maximum(ids, 0)
    high = ids >> 7
    low = ids & 127
    lane = iota((16, 128), 1)

    def table(field, k):
        if field == 0:
            part = ice[k : k + 1, :]
        elif field < 3:
            part = slope[field - 1 : field, 128 * k : 128 * k + 128]
        elif field == 3:
            part = drag[k : k + 1, :]
        else:
            part = heat[field - 4 : field - 3, 128 * k : 128 * k + 128]
        return jnp.broadcast_to(part, (16, 128))

    for pair0 in range(0, PAIRS, 3):
        pairs = range(pair0, pair0 + 3)
        fields = [p for p in pairs] + [p + PAIRS for p in pairs]
        found = {f: jnp.zeros((16, 128), f32) for f in fields}
        for k in range(32):
            here = high == k
            for f in fields:
                found[f] = jnp.where(here, lanes_of(table(f, k), low), found[f])
        for p in pairs:
            even, odd = halves(found[p], found[p + PAIRS], lane)
            out[pl.ds(12 + p, 16, stride=80), :] = even
            out[pl.ds(40 + p, 16, stride=80), :] = even
            out[pl.ds(64 + p, 15, stride=80), :] = even[1:]
            out[pl.ds(52 + p, 16, stride=80), :] = odd
            out[pl.ds(24 + p, 16, stride=80), :] = odd
            out[pl.ds(80 + p, 15, stride=80), :] = odd[:15]

    def message(msg, row0, chunk0):
        for c in range(2):
            for z in range(LEVELS):
                at = 2 * (c * LEVELS + z)
                msg[at : at + 2, :] = prior[c, z, row0 : row0 + 2, :]
        msg[84:86, :] = shaft[row0 : row0 + 2, :].astype(f32)
        msg[86:88, :] = jnp.zeros((2, 128), f32)
        for i in range(6):
            msg[88 + 8 * i : 96 + 8 * i, :] = own[i, chunk0 : chunk0 + 8, :]

    own[0] = ice[...]
    for part in range(4):

        @pl.when(g == part)
        def _():
            for i in range(5):
                layer = 5 * part + i
                for k in range(32):
                    own[i + 1, k : k + 1, :] = heat[layer : layer + 1, 128 * k : 128 * k + 128]

    even_device = d % 2 == 0

    @pl.when(even_device)
    def _():
        message(near, 2, 24)
        message(far, 0, 0)

    @pl.when(jnp.logical_not(even_device))
    def _():
        message(near, 0, 0)
        message(far, 2, 24)


def advect_kernel(own, adjacent, ratio, mean_speed, tier_speed, near, far, depth_out, heat_out, ext):
    d = lax.axis_index("dom")
    even_device = d % 2 == 0
    for i in range(6):
        a = near[88 + 8 * i : 96 + 8 * i, :]
        b = far[88 + 8 * i : 96 + 8 * i, :]
        ext[i, 0:8, :] = jnp.where(even_device, b, a)
        ext[i, 40:48, :] = jnp.where(even_device, a, b)
        ext[i, 8:40, :] = own[i]

    @pl.loop(0, 32)
    def _(k):
        span = pl.ds(pl.multiple_of(128 * k, 128), 128)
        cell = adjacent[:, span] - (d * 4096 - 1024)
        low = cell & 127
        turn = (cell >> 7) - k
        beside = [jnp.zeros((6, 128), f32) for _ in range(6)]
        for r in range(17):
            here = turn == r
            for i in range(6):
                rows = jnp.broadcast_to(ext[i, pl.ds(k + r, 1), :], (6, 128))
                beside[i] = jnp.where(here, lanes_of(rows, low), beside[i])
        weight = ratio[:, span]
        for i in range(6):
            here = ext[i, pl.ds(k + 8, 1), :]
            speed = mean_speed[:, span] if i == 0 else tier_speed[i - 1, :, span]
            flow = weight * (jnp.maximum(speed, 0.0) * here + jnp.minimum(speed, 0.0) * beside[i])
            result = here - jnp.sum(flow, axis=0, keepdims=True)
            if i == 0:
                depth_out[pl.ds(k, 1), :] = result
            else:
                heat_out[i - 1 : i, span] = result


def column_kernel(arrived, shaft, near, far, prior, geo, vext, edge, slots):
    d = lax.axis_index("dom")
    even_device = d % 2 == 0
    row = iota((8, 128), 0)
    lane = iota((8, 128), 1)

    def sides(start, count):
        a = near[start : start + count, :]
        b = far[start : start + count, :]
        return jnp.where(even_device, b, a), jnp.where(even_device, a, b)

    left, right = sides(84, 2)
    slots[0:2, :] = left.astype(jnp.int32)
    slots[2:6, :] = shaft[...]
    slots[6:8, :] = right.astype(jnp.int32)
    slot = slots[...]
    owner = slot >> 6
    low = slot & 63
    low2 = low + 64
    found = [jnp.zeros((8, 128), f32) for _ in range(FIELDS)]
    upper = row < 2
    middle = row < 6
    for p in range(32):
        here = owner == p
        for f in range(PAIRS):
            at = BLOCK_ROWS * p + f
            rows = jnp.where(
                upper,
                row_of(arrived, at, 8),
                jnp.where(middle, row_of(arrived, at + 12, 8), row_of(arrived, at + 24, 8)),
            )
            found[f] = jnp.where(here, lanes_of(rows, low), found[f])
            found[f + PAIRS] = jnp.where(here, lanes_of(rows, low2), found[f + PAIRS])
    first = jnp.where(d == 0, 2, 0)
    last = jnp.where(d == lax.axis_size("dom") - 1, 5, 7)
    inside = jnp.logical_and(row >= first, row <= last)
    found = [jnp.where(inside, value, 0.0) for value in found]
    load_u = -(found[0] * found[1]) * SCALE
    load_v = -(found[0] * found[2]) * SCALE
    friction = found[3] * SCALE
    geo[0] = found[0]
    geo[1] = load_u
    geo[2] = load_v
    geo[3] = friction
    for l in range(LAYERS):
        geo[4 + l] = found[4 + l]
    for cz in range(2 * LEVELS):
        left, right = sides(2 * cz, 2)
        vext[cz, 0:2, :] = left
        vext[cz, 2:6, :] = prior[cz // LEVELS, cz % LEVELS]
        vext[cz, 6:8, :] = right
    group = lane // LEVELS
    pick = jnp.where(group < 2, group, jnp.where(group < 4, 124 + group, 0))
    level = lane - group * LEVELS
    for c in range(2):
        value = jnp.zeros((8, 128), f32)
        for z in range(LEVELS):
            value = jnp.where(level == z, lanes_of(vext[c * LEVELS + z], pick), value)
        edge[8 * c : 8 * c + 8, :] = value
    value = jnp.zeros((8, 128), f32)
    for l in range(LAYERS):
        value = jnp.where(level == l, lanes_of(found[4 + l], pick), value)
    edge[16:24, :] = value
    edge[24:32, :] = lanes_of(found[0], pick)
    edge[32:40, :] = lanes_of(load_u, pick)
    edge[40:48, :] = lanes_of(load_v, pick)
    edge[48:56, :] = jnp.where(level == 0, lanes_of(friction, pick), 0.0)


def interpolate(a, b):
    diff = b - a
    total = a + b
    part = KAPPA * diff
    return diff, total - part, total + part


def spread(a, b):
    total = a + b
    part = KAPPA * (a - b)
    return total, part


def spread_square(a, b):
    total = (1.0 + KAPPA * KAPPA) * (a + b)
    part = (2.0 * KAPPA) * (a - b)
    return total + part, total - part


def up_x(value):
    return pltpu.roll(value, 7, 0)


def down_x(value):
    return pltpu.roll(value, 1, 0)


def level_terms(value, value_y):
    dy, ya, yb = interpolate(value, value_y)
    _, along_y0, along_y1 = interpolate(dy, up_x(dy))
    along_x0, z00, z10 = interpolate(ya, up_x(ya))
    along_x1, z01, z11 = interpolate(yb, up_x(yb))
    return [along_x0, along_x1, along_y0, along_y1, z00, z01, z10, z11]


def element(low_u, top_u, low_v, top_v, hard, inverse2, keep=None):
    def gradients(low, top):
        x = [interpolate(low[q], top[q])[1:] for q in (0, 1)]
        y = [interpolate(low[2 + q], top[2 + q])[1:] for q in (0, 1)]
        z = [top[4 + q] - low[4 + q] for q in range(4)]
        return x, y, z

    ux, uy, uz = gradients(low_u, top_u)
    vx, vy, vz = gradients(low_v, top_v)
    vertical = [
        (uz[q] * uz[q] + vz[q] * vz[q]) * (0.25 * inverse2) + EPS_RATE for q in range(4)
    ]
    vy2 = [[vy[a][b] * vy[a][b] for b in (0, 1)] for a in (0, 1)]
    ex, ey, ez = {}, {}, {}
    ev, eu, wx, wy = {}, {}, {}, {}

    def put(store, key, value):
        store[key] = value if key not in store else store[key] + value

    for qx in (0, 1):
        for qy in (0, 1):
            for qz in (0, 1):
                a = ux[qy][qz]
                b = vy[qx][qz]
                shear = uy[qx][qz] + vx[qy][qz]
                rate = (
                    a * (a + b) + vy2[qx][qz] + 0.25 * (shear * shear) + vertical[2 * qx + qy]
                )
                eta = jnp.exp2(hard - jnp.log2(rate) * (1.0 / 3.0))
                if keep is not None:
                    eta = jnp.where(keep, eta, 0.0)
                put(ex, (qy, qz), eta)
                put(ey, (qx, qz), eta)
                put(ez, 2 * qx + qy, eta)
                put(ev, (qy, qz), eta * b)
                put(eu, (qx, qz), eta * a)
                w = eta * shear
                put(wx, (qy, qz), w)
                put(wy, (qx, qz), w)
    ez = [ez[q] * inverse2 for q in range(4)]
    lows, tops = [], []

    def add_spread(a, b):
        total, part = spread(a, b)
        lows.append(total + part)
        tops.append(total - part)

    def flux(e, g, s):
        half = (g + g) * e + s
        return half + half

    for q in (0, 1):
        add_spread(*[flux(ex[q, z], ux[q][z], ev[q, z]) for z in (0, 1)])
    for q in (0, 1):
        add_spread(wy[q, 0], wy[q, 1])
    for q in range(4):
        value = ez[q] * uz[q]
        lows.append(-value)
        tops.append(value)
    for q in (0, 1):
        add_spread(wx[q, 0], wx[q, 1])
    for q in (0, 1):
        add_spread(*[flux(ey[q, z], vy[q][z], eu[q, z]) for z in (0, 1)])
    for q in range(4):
        value = ez[q] * vz[q]
        lows.append(-value)
        tops.append(value)
    for q in (0, 1):
        a, b = spread_square(ex[q, 0], ex[q, 1])
        lows.append(a)
        tops.append(b)
    for q in (0, 1):
        a, b = spread_square(ey[q, 0], ey[q, 1])
        lows.append(a)
        tops.append(b)
    lows += ez
    tops += ez
    return lows, tops


def node_parts(acc):
    results = []
    for c in (0, 1):
        x0, x1, y0, y1, z00, z01, z10, z11 = acc[8 * c : 8 * c + 8]
        total, part = spread(y0, y1)
        hd = (total + part) + down_x(total - part)
        both = []
        for along, a, b in ((x0, z00, z10), (x1, z01, z11)):
            total, part = spread(a, b)
            part = part - along
            both.append((total + part) + down_x(total - part))
        total, part = spread(both[0], both[1])
        part = part - hd
        results.append((total + part, total - part))
    x0, x1, y0, y1, z00, z01, z10, z11 = acc[16:24]
    hx = [x0 + down_x(x0), x1 + down_x(x1)]
    a, b = spread_square(y0, y1)
    hy = a + down_x(b)
    hz = []
    for za, zb in ((z00, z10), (z01, z11)):
        a, b = spread_square(za, zb)
        hz.append(a + down_x(b))
    a, b = spread_square(4.0 * hx[0] + hz[0], 4.0 * hx[1] + hz[1])
    results.append((a + hy, b + hy))
    hy4 = 4.0 * hy
    a, b = spread_square(hx[0] + hz[0], hx[1] + hz[1])
    results.append((a + hy4, b + hy4))
    return results


def corners(value, value_y):
    pair = value + value_y
    return pair + up_x(pair)


def geometry(depth4):
    dz = depth4 * (0.25 / LAYERS)
    dz = jnp.where(dz > 0.0, dz, 1.0)
    inverse = 0.25 / dz
    return jnp.log2(dz * 16.0), inverse * inverse


def hardness(log_depth, warmth4):
    return log_depth - (0.25 * LOG2E) * warmth4


def at_lane(value, index):
    return lanes_of(value, jnp.full((8, 128), index, jnp.int32))


def up_y(value):
    return pltpu.roll(value, 127, 1)


def down_y(value):
    return pltpu.roll(value, 1, 1)


def levels(source, next_u, next_v, hard, inverse2, finish):
    def terms(z):
        u = source[z]
        v = source[LEVELS + z]
        return level_terms(u, next_u(z, u)) + level_terms(v, next_v(z, v))

    def body(z, carry):
        low, tops = carry[:16], carry[16:]
        top = terms(z + 1)
        lows, next_tops = element(low[:8], top[:8], low[8:], top[8:], hard(z), inverse2)
        finish(z, node_parts([a + b for a, b in zip(lows, tops)]))
        return (*top, *next_tops)

    zero = jnp.zeros((8, 128), f32)
    carry = lax.fori_loop(0, LAYERS, body, (*terms(0), *([zero] * 24)), unroll=UNROLL)
    finish(LAYERS, node_parts(list(carry[16:])))


def inner_kernel(geo, vext, partial):
    lane = iota((8, 128), 1)
    depth = geo[0]
    log_depth, inverse2 = geometry(corners(depth, up_y(depth)))

    def hard(z):
        warm = geo[4 + z]
        return hardness(log_depth, corners(warm, up_y(warm)))

    def beside(z, value):
        return up_y(value)

    def finish(z, results):
        for q, (a, b) in enumerate(results):
            partial[q * LEVELS + z] = jnp.where(lane == 127, 0.0, a) + jnp.where(
                lane == 0, 0.0, down_y(b)
            )

    levels(vext, beside, beside, hard, inverse2, finish)


def ice_kernel(geo, vext, partial, edge, edge_near, edge_far, origin, out_v, send, hard, first, second, means):
    g = lax.axis_index("grp")
    d = lax.axis_index("dom")
    groups = lax.axis_size("grp")
    domains = lax.axis_size("dom")
    row = iota((8, 128), 0)
    lane = iota((8, 128), 1)
    group = lane // LEVELS
    level = lane - group * LEVELS
    even_group = g % 2 == 0

    def edge_field(i):
        span = slice(8 * i, 8 * i + 8)
        own = edge[span, :]
        a = edge_near[span, :]
        b = edge_far[span, :]
        left = jnp.where(even_group, b, a)
        right = jnp.where(even_group, a, b)
        return jnp.where(
            lane < 42,
            pltpu.roll(left, 86, 1),
            jnp.where(
                lane < 63,
                pltpu.roll(own, 42, 1),
                jnp.where(lane < 84, own, pltpu.roll(right, 84, 1)),
            ),
        )

    edge_u, edge_v, edge_t, edge_h, edge_fu, edge_fv, edge_b = [edge_field(i) for i in range(7)]

    def edge_up(value):
        return pltpu.roll(value, 107, 1)

    def joined(value, beyond, index):
        return jnp.where(lane == 127, at_lane(beyond, index), up_y(value))

    edge_log, edge_inv2 = geometry(corners(edge_h, edge_up(edge_h)))
    edge_hard = hardness(edge_log, corners(edge_t, edge_up(edge_t)))
    depth = geo[0]
    main_log, main_inv2 = geometry(corners(depth, joined(depth, edge_h, 84)))
    for l in range(LAYERS):
        warm = geo[4 + l]
        hard[l] = hardness(main_log, corners(warm, joined(warm, edge_t, 84 + l)))

    load_u = geo[1]
    load_v = geo[2]
    friction = geo[3]
    keep = jnp.logical_and(level != LAYERS, lane < 6 * LEVELS)
    first_row = jnp.where(d == 0, 2, 1)
    last_row = jnp.where(d == domains - 1, 5, 6)
    inside = jnp.logical_and(row >= first_row, row <= last_row)
    edge_inside = jnp.logical_and(
        inside,
        jnp.logical_or(
            jnp.logical_and(group == 1, g > 0),
            jnp.logical_and(group == 4, g < groups - 1),
        ),
    )

    def edge_parts(u, v):
        low_u = level_terms(u, edge_up(u))
        low_v = level_terms(v, edge_up(v))
        top_u = [up_y(t) for t in low_u]
        top_v = [up_y(t) for t in low_v]
        lows, tops = element(low_u, top_u, low_v, top_v, edge_hard, edge_inv2, keep)
        return node_parts([a + down_y(b) for a, b in zip(lows, tops)])

    def stepped(value, load, force, diagonal, drag):
        return value + 0.5 * (load - force - drag * value) / (diagonal + drag)

    parts = edge_parts(edge_u, edge_v)
    for z in range(LEVELS):
        sums = []
        for q, (a, b) in enumerate(parts):
            rim = jnp.where(lane == 127, at_lane(a, 63 + z), 0.0)
            rim = jnp.where(lane == 0, at_lane(b, 21 + z), rim)
            sums.append(partial[q * LEVELS + z] + rim)
        fu, fv, du, dv = sums
        drag = friction if z == 0 else 0.0
        first[z] = jnp.where(inside, stepped(vext[z], load_u, fu, du, drag), 0.0)
        first[LEVELS + z] = jnp.where(inside, stepped(vext[LEVELS + z], load_v, fv, dv, drag), 0.0)

    def edge_final(c, value, load):
        (fa, fb), (da, db) = parts[c], parts[2 + c]
        force = fa + pltpu.roll(fb, LEVELS, 1)
        diagonal = da + pltpu.roll(db, LEVELS, 1)
        return jnp.where(edge_inside, stepped(value, load, force, diagonal, edge_b), 0.0)

    edge_u = edge_final(0, edge_u, edge_fu)
    edge_v = edge_final(1, edge_v, edge_fv)
    for z in range(LEVELS):
        here = lane == 42 + z
        edge_u = jnp.where(here, at_lane(first[z], 0), edge_u)
        edge_v = jnp.where(here, at_lane(first[LEVELS + z], 0), edge_v)
    beyond = [b for _, b in edge_parts(edge_u, edge_v)]

    def finish(z, results):
        fu, fv, du, dv = [
            a + jnp.where(lane == 0, at_lane(e, 21 + z), down_y(b))
            for (a, b), e in zip(results, beyond)
        ]
        drag = jnp.where(z == 0, friction, 0.0)
        second[z] = stepped(first[z], load_u, fu, du, drag)
        second[LEVELS + z] = stepped(first[LEVELS + z], load_v, fv, dv, drag)

    levels(
        first,
        lambda z, value: joined(value, edge_u, 84 + z),
        lambda z, value: joined(value, edge_v, 84 + z),
        lambda z: hard[z],
        main_inv2,
        finish,
    )
    for c in range(2):
        for z in range(LEVELS):
            out_v[c, z] = second[c * LEVELS + z, 2:6, :]
    for c in range(2):
        for l in range(LAYERS):
            at = c * LEVELS + l
            means[8 * (c * LAYERS + l) : 8 * (c * LAYERS + l) + 8, :] = 0.5 * (
                second[at] + second[at + 1]
            )

    from_x = origin[0:16]
    from_y = origin[16:32]
    lane16 = iota((16, 128), 1)
    here = [from_x == x for x in range(4)]
    send[...] = jnp.zeros(send.shape, f32)
    for l in range(LAYERS):
        pair = []
        for c in range(2):
            at = 8 * (c * LAYERS + l) + 2
            value = lanes_of(row_of(means, at, 16), from_y)
            for x in range(1, 4):
                value = jnp.where(here[x], lanes_of(row_of(means, at + x, 16), from_y), value)
            pair.append(value)
        even, odd = halves(pair[0], pair[1], lane16)
        start = (l // 5) * 256 + l % 5
        send[pl.ds(start, 16, stride=16), :] = even
        send[pl.ds(start + 8, 16, stride=16), :] = odd


def prepare_kernel(shaft, origin):
    slot_row = iota((16, 128), 0)
    place = iota((16, 128), 1).astype(f32)
    low_row = iota((128, 128), 0)
    where_from = jnp.zeros((32, 128), f32)
    for x in range(4):
        slot = shaft[x : x + 1, :]
        here = slot_row == jnp.broadcast_to(slot >> 7, (16, 128))
        left = jnp.concatenate(
            [jnp.where(here, float(x), 0.0), jnp.where(here, place, 0.0)], axis=0
        )
        right = jnp.where(low_row == jnp.broadcast_to(slot & 127, (128, 128)), 1.0, 0.0)
        where_from = where_from + lax.dot_general(
            left.astype(bf16),
            right.astype(bf16),
            (((1,), (1,)), ((), ())),
            preferred_element_type=f32,
        )
    origin[...] = where_from.astype(jnp.int32) & 127


def total_kernel(arrived, donor, out, left, hot):
    lane = iota((8, 128), 1)
    row = iota((8, 128), 0)
    row256 = iota((256, 128), 0).astype(bf16)
    one = jnp.ones((), bf16)
    zero = jnp.zeros((), bf16)
    ids = [joined_rows(donor.at[0, g]) for g in range(4)]
    sums = jnp.zeros((256 * SPLITS, 256), f32)
    for step in range(STEPS):
        for part in range(64 // STEPS):
            chunk = 64 // STEPS * step + part
            span = slice(128 * chunk, 128 * chunk + 128)
            x = arrived[16 * chunk : 16 * chunk + 16, :]
            u, v = halves(x[:8], x[8:], lane)
            u = jnp.where(row < 5, u, jnp.where(row == 5, 1.0, 0.0))
            v = jnp.where(row < 5, v, 0.0)
            rest = jnp.concatenate([u, v], axis=0)
            cell = ids[chunk // 16][chunk % 16 : chunk % 16 + 1]
            high = jnp.broadcast_to(cell >> 8, (16, 128)).astype(bf16)
            low = jnp.broadcast_to(cell & 255, (256, 128)).astype(bf16)
            hot[:, span] = jnp.where(row256 == low, one, zero)
            for s in range(SPLITS):
                piece = rest.astype(bf16)
                rest = rest - piece.astype(f32)
                for h in range(16):
                    at = 256 * s + 16 * h
                    left[at : at + 16, span] = jnp.where(high == h, piece, zero)
        span = slice(8192 // STEPS * step, 8192 // STEPS * (step + 1))
        sums = sums + lax.dot_general(
            left[:, span], hot[:, span], (((1,), (1,)), ((), ())), preferred_element_type=f32
        )
    for h in range(16):
        total = sums[16 * h : 16 * h + 16]
        for s in range(1, SPLITS):
            total = total + sums[256 * s + 16 * h : 256 * s + 16 * h + 16]
        count = jnp.maximum(total[5:6, :], 1.0)
        span = slice(256 * h, 256 * h + 256)
        u = total[0:5, :] / count
        v = total[8:13, :] / count
        for l in range(5):
            out[l, 0:1, span] = u[l : l + 1]
            out[l, 1:2, span] = v[l : l + 1]


def shape(*sizes):
    return jax.ShapeDtypeStruct(sizes, f32)


def near_pairs(count):
    even = [(i, i ^ 1) for i in range(count)]
    odd = []
    for i in range(1, count - 1, 2):
        odd += [(i, i + 1), (i + 1, i)]
    return even, odd


def shards(
    ice_depth,
    heat_state,
    elevation_slope_components,
    sliding_drag,
    adjacent_polygons,
    edge_timing_ratio,
    edge_average_normal_speed,
    tier_edge_normal_speed,
    position_donor_polygons,
    shaft_holding_position,
    prior_node_motion,
):
    ice = ice_depth.reshape(32, 128)
    drag = sliding_drag.reshape(32, 128)
    outgoing, near_out, far_out, own = pl.pallas_call(
        pack_kernel,
        out_shape=(
            shape(32 * BLOCK_ROWS, 128),
            shape(MSG_ROWS, 128),
            shape(MSG_ROWS, 128),
            shape(6, 32, 128),
        ),
        in_specs=[pl.BlockSpec(memory_space=pltpu.HBM)] * 7,
        scratch_shapes=[
            pltpu.VMEM((32, 128), f32),
            pltpu.VMEM((LAYERS, 4096), f32),
            pltpu.VMEM((2, 4096), f32),
            pltpu.VMEM((32, 128), f32),
            pltpu.VMEM((32, 64), jnp.int32),
            pltpu.VMEM((4, 128), jnp.int32),
            pltpu.VMEM((2, LEVELS, 4, 128), f32),
            pltpu.SemaphoreType.DMA((7,)),
        ],
        compiler_params=WIDE,
        name="pack",
    )(
        ice,
        heat_state,
        elevation_slope_components,
        drag,
        position_donor_polygons,
        shaft_holding_position,
        prior_node_motion,
    )
    arrived = lax.all_to_all(outgoing, "dom", split_axis=0, concat_axis=0, tiled=True)
    even, odd = near_pairs(lax.axis_size("dom"))
    near = lax.ppermute(near_out, "dom", even)
    far = lax.ppermute(far_out, "dom", odd)
    shaft, near_out = lax.optimization_barrier((shaft_holding_position, near_out))
    origin = pl.pallas_call(
        prepare_kernel,
        out_shape=jax.ShapeDtypeStruct((32, 128), jnp.int32),
        compiler_params=PARAMS,
        name="prepare",
    )(shaft)
    arrived, origin = lax.optimization_barrier((arrived, origin))
    geo, vext, edge = pl.pallas_call(
        column_kernel,
        out_shape=(shape(FIELDS, 8, 128), shape(2 * LEVELS, 8, 128), shape(56, 128)),
        scratch_shapes=[pltpu.VMEM((8, 128), jnp.int32)],
        compiler_params=PARAMS,
        name="columns",
    )(arrived, shaft_holding_position, near, far, prior_node_motion)
    even, odd = near_pairs(lax.axis_size("grp"))
    edge_near = lax.ppermute(edge, "grp", even)
    edge_far = lax.ppermute(edge, "grp", odd)
    partial = pl.pallas_call(
        inner_kernel,
        out_shape=shape(4 * LEVELS, 8, 128),
        compiler_params=PARAMS,
        name="inner",
    )(geo, vext)
    node_velocity, send = pl.pallas_call(
        ice_kernel,
        out_shape=(shape(2, LEVELS, 4, 128), shape(1024, 128)),
        scratch_shapes=[
            pltpu.VMEM((LAYERS, 8, 128), f32),
            pltpu.VMEM((2 * LEVELS, 8, 128), f32),
            pltpu.VMEM((2 * LEVELS, 8, 128), f32),
            pltpu.VMEM((2 * LAYERS * 8, 128), f32),
        ],
        compiler_params=PARAMS,
        name="velocity",
    )(geo, vext, partial, edge, edge_near, edge_far, origin)
    back = lax.all_to_all(send, ("grp", "dom"), split_axis=0, concat_axis=0, tiled=True)
    depth, heat = pl.pallas_call(
        advect_kernel,
        out_shape=(shape(32, 128), shape(5, 4096)),
        scratch_shapes=[pltpu.VMEM((6, 48, 128), f32)],
        compiler_params=PARAMS,
        name="advect",
    )(
        own,
        adjacent_polygons,
        edge_timing_ratio,
        edge_average_normal_speed,
        tier_edge_normal_speed,
        near,
        far,
    )
    tier_motion = pl.pallas_call(
        total_kernel,
        out_shape=shape(5, 2, 4096),
        scratch_shapes=[pltpu.VMEM((256 * SPLITS, 8192), bf16), pltpu.VMEM((256, 8192), bf16)],
        compiler_params=PARAMS,
        name="totals",
    )(back, position_donor_polygons)
    return (depth.reshape(4096), heat, node_velocity, jnp.transpose(tier_motion, (1, 0, 2)))


def solution(mesh):
    in_specs = (
        P("dom"),
        P(None, "dom"),
        P(None, "dom"),
        P("dom"),
        P(None, "dom"),
        P(None, "dom"),
        P(None, "dom"),
        P("grp", None, "dom"),
        P("dom", None, None, None),
        P("dom", "grp"),
        P(None, None, "dom", "grp"),
    )
    out_specs = (P("dom"), P("grp", "dom"), P(None, None, "dom", "grp"), P(None, "grp", "dom"))
    return jax.shard_map(shards, mesh=mesh, in_specs=in_specs, out_specs=out_specs, check_vma=False)
```

```python
import math

import jax
import jax.numpy as jnp
from jax import lax
from jax.experimental import pallas as pl
from jax.experimental.pallas import tpu as pltpu
from jax.sharding import PartitionSpec as P

KAPPA = 1.0 / math.sqrt(3.0)
EPS_RATE = 0.01
LOG2E = math.log2(math.e)
SCALE = 4096.0
LAYERS = 20
LEVELS = 21
FIELDS = 24
PAIRS = 12
BLOCK_ROWS = 40
MSG_ROWS = 136
STEPS = 4
f32 = jnp.float32
bf16 = jnp.bfloat16
PARAMS = pltpu.CompilerParams(vmem_limit_bytes=32 * 1024 * 1024)
WIDE = pltpu.CompilerParams(vmem_limit_bytes=60 * 1024 * 1024)


def lanes_of(table, index):
    return jnp.take_along_axis(table, index, axis=1, mode="promise_in_bounds")


def iota(shape, dim):
    return lax.broadcasted_iota(jnp.int32, shape, dim)


def row_of(ref, row, rows):
    return jnp.broadcast_to(ref[pl.ds(row, 1), :], (rows, 128))


def halves(first, second, lane):
    even = jnp.where(lane < 64, first, pltpu.roll(second, 64, 1))
    odd = jnp.where(lane < 64, pltpu.roll(first, 64, 1), second)
    return even, odd


def joined_rows(rows):
    return jnp.concatenate([rows[pl.ds(0, 16, stride=2), :], rows[pl.ds(1, 16, stride=2), :]], axis=1)


def pack_kernel(
    ice_in, heat_in, slope_in, drag_in, donor_in, shaft_in, prior_in,
    out_to, near_to, far_to, own_to,
    ice, heat, slope, drag, donor, shaft, prior, out, near, far, own, arrivals, leaves,
):
    g = lax.axis_index("grp")
    d = lax.axis_index("dom")
    pairs = (
        (heat_in, heat),
        (donor_in.at[0, g], donor),
        (ice_in, ice),
        (slope_in, slope),
        (drag_in, drag),
        (shaft_in, shaft),
        (prior_in, prior),
    )
    copies = [pltpu.make_async_copy(a, b, arrivals.at[i]) for i, (a, b) in enumerate(pairs)]
    for copy in copies:
        copy.start()
    out[0:12, :] = jnp.zeros((12, 128), f32)
    out[31 * 40 + 24 : 31 * 40 + 36, :] = jnp.zeros((12, 128), f32)
    for k in range(32):
        out[40 * k + 36 : 40 * k + 40, :] = jnp.zeros((4, 128), f32)
    for copy in copies:
        copy.wait()

    own[0] = ice[...]
    for part in range(4):

        @pl.when(g == part)
        def _():
            for i in range(5):
                layer = 5 * part + i
                for k in range(32):
                    own[i + 1, k : k + 1, :] = heat[layer : layer + 1, 128 * k : 128 * k + 128]

    def message(msg, row0, chunk0):
        for c in range(2):
            for z in range(LEVELS):
                at = 2 * (c * LEVELS + z)
                msg[at : at + 2, :] = prior[c, z, row0 : row0 + 2, :]
        msg[84:86, :] = shaft[row0 : row0 + 2, :].astype(f32)
        msg[86:88, :] = jnp.zeros((2, 128), f32)
        for i in range(6):
            msg[88 + 8 * i : 96 + 8 * i, :] = own[i, chunk0 : chunk0 + 8, :]

    even_device = d % 2 == 0

    @pl.when(even_device)
    def _():
        message(near, 2, 24)
        message(far, 0, 0)

    @pl.when(jnp.logical_not(even_device))
    def _():
        message(near, 0, 0)
        message(far, 2, 24)

    leaving = [
        pltpu.make_async_copy(near, near_to, leaves.at[0]),
        pltpu.make_async_copy(far, far_to, leaves.at[1]),
        pltpu.make_async_copy(own, own_to, leaves.at[2]),
    ]
    for copy in leaving:
        copy.start()

    ids = jnp.maximum(joined_rows(donor), 0)
    high = ids >> 7
    low = ids & 127
    lane = iota((8, 128), 1)
    highs = [high[:8], high[8:]]
    lows = [low[:8], low[8:]]

    def table(field, k):
        if field == 0:
            part = ice[k : k + 1, :]
        elif field < 3:
            part = slope[field - 1 : field, 128 * k : 128 * k + 128]
        elif field == 3:
            part = drag[k : k + 1, :]
        else:
            part = heat[field - 4 : field - 3, 128 * k : 128 * k + 128]
        return jnp.broadcast_to(part, (8, 128))

    for v in range(2):
        found = [jnp.zeros((8, 128), f32)] * FIELDS
        for k in range(32):
            here = highs[v] == k
            for f in range(FIELDS):
                found[f] = jnp.where(here, lanes_of(table(f, k), lows[v]), found[f])
        at = 640 * v
        for p in range(PAIRS):
            even, odd = halves(found[p], found[p + PAIRS], lane)
            out[pl.ds(at + 12 + p, 8, stride=80), :] = even
            out[pl.ds(at + 40 + p, 8, stride=80), :] = even
            if v == 0:
                out[pl.ds(64 + p, 7, stride=80), :] = even[1:]
                out[pl.ds(80 + p, 8, stride=80), :] = odd
            else:
                out[pl.ds(at - 16 + p, 8, stride=80), :] = even
                out[pl.ds(at + 80 + p, 7, stride=80), :] = odd[:7]
            out[pl.ds(at + 52 + p, 8, stride=80), :] = odd
            out[pl.ds(at + 24 + p, 8, stride=80), :] = odd
        span = slice(0, 600) if v == 0 else slice(600, 1280)
        copy = pltpu.make_async_copy(out.at[span], out_to.at[span], leaves.at[3 + v])
        copy.start()
        leaving.append(copy)
    for copy in leaving:
        copy.wait()


def advect_kernel(own, adjacent, ratio, mean_speed, tier_speed, near, far, depth_out, heat_out, ext):
    d = lax.axis_index("dom")
    even_device = d % 2 == 0
    for i in range(6):
        a = near[88 + 8 * i : 96 + 8 * i, :]
        b = far[88 + 8 * i : 96 + 8 * i, :]
        ext[i, 0:8, :] = jnp.where(even_device, b, a)
        ext[i, 40:48, :] = jnp.where(even_device, a, b)
        ext[i, 8:40, :] = own[i]

    @pl.loop(0, 32)
    def _(k):
        span = pl.ds(pl.multiple_of(128 * k, 128), 128)
        cell = adjacent[:, span] - (d * 4096 - 1024)
        low = cell & 127
        turn = (cell >> 7) - k
        beside = [jnp.zeros((6, 128), f32) for _ in range(6)]
        for r in range(17):
            here = turn == r
            for i in range(6):
                rows = jnp.broadcast_to(ext[i, pl.ds(k + r, 1), :], (6, 128))
                beside[i] = jnp.where(here, lanes_of(rows, low), beside[i])
        weight = ratio[:, span]
        for i in range(6):
            here = ext[i, pl.ds(k + 8, 1), :]
            speed = mean_speed[:, span] if i == 0 else tier_speed[i - 1, :, span]
            flow = weight * (jnp.maximum(speed, 0.0) * here + jnp.minimum(speed, 0.0) * beside[i])
            result = here - jnp.sum(flow, axis=0, keepdims=True)
            if i == 0:
                depth_out[pl.ds(k, 1), :] = result
            else:
                heat_out[i - 1 : i, span] = result


def column_kernel(arrived, shaft, near, far, prior, geo, vext, edge, slots):
    d = lax.axis_index("dom")
    even_device = d % 2 == 0
    row = iota((8, 128), 0)
    lane = iota((8, 128), 1)

    def sides(start, count):
        a = near[start : start + count, :]
        b = far[start : start + count, :]
        return jnp.where(even_device, b, a), jnp.where(even_device, a, b)

    left, right = sides(84, 2)
    slots[0:2, :] = left.astype(jnp.int32)
    slots[2:6, :] = shaft[...]
    slots[6:8, :] = right.astype(jnp.int32)
    slot = slots[...]
    owner = slot >> 6
    low = slot & 63
    low2 = low + 64
    found = [jnp.zeros((8, 128), f32) for _ in range(FIELDS)]
    upper = row < 2
    middle = row < 6
    for p in range(32):
        here = owner == p
        for f in range(PAIRS):
            at = BLOCK_ROWS * p + f
            rows = jnp.where(
                upper,
                row_of(arrived, at, 8),
                jnp.where(middle, row_of(arrived, at + 12, 8), row_of(arrived, at + 24, 8)),
            )
            found[f] = jnp.where(here, lanes_of(rows, low), found[f])
            found[f + PAIRS] = jnp.where(here, lanes_of(rows, low2), found[f + PAIRS])
    first = jnp.where(d == 0, 2, 0)
    last = jnp.where(d == lax.axis_size("dom") - 1, 5, 7)
    inside = jnp.logical_and(row >= first, row <= last)
    found = [jnp.where(inside, value, 0.0) for value in found]
    load_u = -(found[0] * found[1]) * SCALE
    load_v = -(found[0] * found[2]) * SCALE
    friction = found[3] * SCALE
    geo[0] = found[0]
    geo[1] = load_u
    geo[2] = load_v
    geo[3] = friction
    for l in range(LAYERS):
        geo[4 + l] = found[4 + l]
    for cz in range(2 * LEVELS):
        left, right = sides(2 * cz, 2)
        vext[cz, 0:2, :] = left
        vext[cz, 2:6, :] = prior[cz // LEVELS, cz % LEVELS]
        vext[cz, 6:8, :] = right
    group = lane // LEVELS
    pick = jnp.where(group < 2, group, jnp.where(group < 4, 124 + group, 0))
    level = lane - group * LEVELS
    for c in range(2):
        value = jnp.zeros((8, 128), f32)
        for z in range(LEVELS):
            value = jnp.where(level == z, lanes_of(vext[c * LEVELS + z], pick), value)
        edge[8 * c : 8 * c + 8, :] = value
    value = jnp.zeros((8, 128), f32)
    for l in range(LAYERS):
        value = jnp.where(level == l, lanes_of(found[4 + l], pick), value)
    edge[16:24, :] = value
    edge[24:32, :] = lanes_of(found[0], pick)
    edge[32:40, :] = lanes_of(load_u, pick)
    edge[40:48, :] = lanes_of(load_v, pick)
    edge[48:56, :] = jnp.where(level == 0, lanes_of(friction, pick), 0.0)


def interpolate(a, b):
    diff = b - a
    total = a + b
    part = KAPPA * diff
    return diff, total - part, total + part


def spread(a, b):
    total = a + b
    part = KAPPA * (a - b)
    return total, part


def spread_square(a, b):
    total = (1.0 + KAPPA * KAPPA) * (a + b)
    part = (2.0 * KAPPA) * (a - b)
    return total + part, total - part


def up_x(value):
    return pltpu.roll(value, 7, 0)


def down_x(value):
    return pltpu.roll(value, 1, 0)


def level_terms(value, value_y):
    dy, ya, yb = interpolate(value, value_y)
    _, along_y0, along_y1 = interpolate(dy, up_x(dy))
    along_x0, z00, z10 = interpolate(ya, up_x(ya))
    along_x1, z01, z11 = interpolate(yb, up_x(yb))
    return [along_x0, along_x1, along_y0, along_y1, z00, z01, z10, z11]


def element(low_u, top_u, low_v, top_v, hard, inverse2, keep=None):
    def gradients(low, top):
        x = [interpolate(low[q], top[q])[1:] for q in (0, 1)]
        y = [interpolate(low[2 + q], top[2 + q])[1:] for q in (0, 1)]
        z = [top[4 + q] - low[4 + q] for q in range(4)]
        return x, y, z

    ux, uy, uz = gradients(low_u, top_u)
    vx, vy, vz = gradients(low_v, top_v)
    vertical = [
        (uz[q] * uz[q] + vz[q] * vz[q]) * (0.25 * inverse2) + EPS_RATE for q in range(4)
    ]
    vy2 = [[vy[a][b] * vy[a][b] for b in (0, 1)] for a in (0, 1)]
    ex, ey, ez = {}, {}, {}
    ev, eu, wx, wy = {}, {}, {}, {}

    def put(store, key, value):
        store[key] = value if key not in store else store[key] + value

    for qx in (0, 1):
        for qy in (0, 1):
            for qz in (0, 1):
                a = ux[qy][qz]
                b = vy[qx][qz]
                shear = uy[qx][qz] + vx[qy][qz]
                rate = (
                    a * (a + b) + vy2[qx][qz] + 0.25 * (shear * shear) + vertical[2 * qx + qy]
                )
                eta = jnp.exp2(hard - jnp.log2(rate) * (1.0 / 3.0))
                if keep is not None:
                    eta = jnp.where(keep, eta, 0.0)
                put(ex, (qy, qz), eta)
                put(ey, (qx, qz), eta)
                put(ez, 2 * qx + qy, eta)
                put(ev, (qy, qz), eta * b)
                put(eu, (qx, qz), eta * a)
                w = eta * shear
                put(wx, (qy, qz), w)
                put(wy, (qx, qz), w)
    ez = [ez[q] * inverse2 for q in range(4)]
    lows, tops = [], []

    def add_spread(a, b):
        total, part = spread(a, b)
        lows.append(total + part)
        tops.append(total - part)

    def flux(e, g, s):
        half = (g + g) * e + s
        return half + half

    for q in (0, 1):
        add_spread(*[flux(ex[q, z], ux[q][z], ev[q, z]) for z in (0, 1)])
    for q in (0, 1):
        add_spread(wy[q, 0], wy[q, 1])
    for q in range(4):
        value = ez[q] * uz[q]
        lows.append(-value)
        tops.append(value)
    for q in (0, 1):
        add_spread(wx[q, 0], wx[q, 1])
    for q in (0, 1):
        add_spread(*[flux(ey[q, z], vy[q][z], eu[q, z]) for z in (0, 1)])
    for q in range(4):
        value = ez[q] * vz[q]
        lows.append(-value)
        tops.append(value)
    for q in (0, 1):
        a, b = spread_square(ex[q, 0], ex[q, 1])
        lows.append(a)
        tops.append(b)
    for q in (0, 1):
        a, b = spread_square(ey[q, 0], ey[q, 1])
        lows.append(a)
        tops.append(b)
    lows += ez
    tops += ez
    return lows, tops


def node_parts(acc):
    results = []
    for c in (0, 1):
        x0, x1, y0, y1, z00, z01, z10, z11 = acc[8 * c : 8 * c + 8]
        total, part = spread(y0, y1)
        hd = (total + part) + down_x(total - part)
        both = []
        for along, a, b in ((x0, z00, z10), (x1, z01, z11)):
            total, part = spread(a, b)
            part = part - along
            both.append((total + part) + down_x(total - part))
        total, part = spread(both[0], both[1])
        part = part - hd
        results.append((total + part, total - part))
    x0, x1, y0, y1, z00, z01, z10, z11 = acc[16:24]
    hx = [x0 + down_x(x0), x1 + down_x(x1)]
    a, b = spread_square(y0, y1)
    hy = a + down_x(b)
    hz = []
    for za, zb in ((z00, z10), (z01, z11)):
        a, b = spread_square(za, zb)
        hz.append(a + down_x(b))
    a, b = spread_square(4.0 * hx[0] + hz[0], 4.0 * hx[1] + hz[1])
    results.append((a + hy, b + hy))
    hy4 = 4.0 * hy
    a, b = spread_square(hx[0] + hz[0], hx[1] + hz[1])
    results.append((a + hy4, b + hy4))
    return results


def corners(value, value_y):
    pair = value + value_y
    return pair + up_x(pair)


def geometry(depth4):
    dz = depth4 * (0.25 / LAYERS)
    dz = jnp.where(dz > 0.0, dz, 1.0)
    inverse = 0.25 / dz
    return jnp.log2(dz * 16.0), inverse * inverse


def hardness(log_depth, warmth4):
    return log_depth - (0.25 * LOG2E) * warmth4


def at_lane(value, index):
    return lanes_of(value, jnp.full((8, 128), index, jnp.int32))


def up_y(value):
    return pltpu.roll(value, 127, 1)


def down_y(value):
    return pltpu.roll(value, 1, 1)


def levels(source, next_u, next_v, hard, inverse2, finish):
    def terms(z):
        u = source[z]
        v = source[LEVELS + z]
        return level_terms(u, next_u(z, u)) + level_terms(v, next_v(z, v))

    def body(z, carry):
        low, tops = carry[:16], carry[16:]
        top = terms(z + 1)
        lows, next_tops = element(low[:8], top[:8], low[8:], top[8:], hard(z), inverse2)
        finish(z, node_parts([a + b for a, b in zip(lows, tops)]))
        return (*top, *next_tops)

    zero = jnp.zeros((8, 128), f32)
    carry = (*terms(0), *([zero] * 24))
    for z in range(LAYERS):
        carry = body(z, carry)
    finish(LAYERS, node_parts(list(carry[16:])))


def inner_kernel(geo, vext, partial):
    lane = iota((8, 128), 1)
    depth = geo[0]
    log_depth, inverse2 = geometry(corners(depth, up_y(depth)))

    def hard(z):
        warm = geo[4 + z]
        return hardness(log_depth, corners(warm, up_y(warm)))

    def beside(z, value):
        return up_y(value)

    def finish(z, results):
        for q, (a, b) in enumerate(results):
            partial[q * LEVELS + z] = jnp.where(lane == 127, 0.0, a) + jnp.where(
                lane == 0, 0.0, down_y(b)
            )

    levels(vext, beside, beside, hard, inverse2, finish)


def ice_kernel(
    geo, vext, partial, edge, edge_near, edge_far, origin, out_v_to, send_to,
    hard, first, second, means, out_v, send, leaves,
):
    g = lax.axis_index("grp")
    d = lax.axis_index("dom")
    groups = lax.axis_size("grp")
    domains = lax.axis_size("dom")
    row = iota((8, 128), 0)
    lane = iota((8, 128), 1)
    group = lane // LEVELS
    level = lane - group * LEVELS
    even_group = g % 2 == 0

    def edge_field(i):
        span = slice(8 * i, 8 * i + 8)
        own = edge[span, :]
        a = edge_near[span, :]
        b = edge_far[span, :]
        left = jnp.where(even_group, b, a)
        right = jnp.where(even_group, a, b)
        return jnp.where(
            lane < 42,
            pltpu.roll(left, 86, 1),
            jnp.where(
                lane < 63,
                pltpu.roll(own, 42, 1),
                jnp.where(lane < 84, own, pltpu.roll(right, 84, 1)),
            ),
        )

    edge_u, edge_v, edge_t, edge_h, edge_fu, edge_fv, edge_b = [edge_field(i) for i in range(7)]

    def edge_up(value):
        return pltpu.roll(value, 107, 1)

    def joined(value, beyond, index):
        return jnp.where(lane == 127, pltpu.roll(beyond, 127 - index, 1), up_y(value))

    edge_log, edge_inv2 = geometry(corners(edge_h, edge_up(edge_h)))
    edge_hard = hardness(edge_log, corners(edge_t, edge_up(edge_t)))
    depth = geo[0]
    main_log, main_inv2 = geometry(corners(depth, joined(depth, edge_h, 84)))
    for l in range(LAYERS):
        warm = geo[4 + l]
        hard[l] = hardness(main_log, corners(warm, joined(warm, edge_t, 84 + l)))

    load_u = geo[1]
    load_v = geo[2]
    friction = geo[3]
    keep = jnp.logical_and(level != LAYERS, lane < 6 * LEVELS)
    first_row = jnp.where(d == 0, 2, 1)
    last_row = jnp.where(d == domains - 1, 5, 6)
    inside = jnp.logical_and(row >= first_row, row <= last_row)
    edge_inside = jnp.logical_and(
        inside,
        jnp.logical_or(
            jnp.logical_and(group == 1, g > 0),
            jnp.logical_and(group == 4, g < groups - 1),
        ),
    )

    def edge_parts(u, v):
        low_u = level_terms(u, edge_up(u))
        low_v = level_terms(v, edge_up(v))
        top_u = [up_y(t) for t in low_u]
        top_v = [up_y(t) for t in low_v]
        lows, tops = element(low_u, top_u, low_v, top_v, edge_hard, edge_inv2, keep)
        return node_parts([a + down_y(b) for a, b in zip(lows, tops)])

    def stepped(value, load, force, diagonal, drag):
        return value + 0.5 * (load - force - drag * value) / (diagonal + drag)

    parts = edge_parts(edge_u, edge_v)
    for z in range(LEVELS):
        sums = []
        for q, (a, b) in enumerate(parts):
            rim = jnp.where(lane == 127, pltpu.roll(a, 64 - z, 1), 0.0)
            rim = jnp.where(lane == 0, pltpu.roll(b, 107 - z, 1), rim)
            sums.append(partial[q * LEVELS + z] + rim)
        fu, fv, du, dv = sums
        drag = friction if z == 0 else 0.0
        first[z] = jnp.where(inside, stepped(vext[z], load_u, fu, du, drag), 0.0)
        first[LEVELS + z] = jnp.where(inside, stepped(vext[LEVELS + z], load_v, fv, dv, drag), 0.0)

    def edge_final(c, value, load):
        (fa, fb), (da, db) = parts[c], parts[2 + c]
        force = fa + pltpu.roll(fb, LEVELS, 1)
        diagonal = da + pltpu.roll(db, LEVELS, 1)
        return jnp.where(edge_inside, stepped(value, load, force, diagonal, edge_b), 0.0)

    edge_u = edge_final(0, edge_u, edge_fu)
    edge_v = edge_final(1, edge_v, edge_fv)
    for z in range(LEVELS):
        here = lane == 42 + z
        edge_u = jnp.where(here, pltpu.roll(first[z], 42 + z, 1), edge_u)
        edge_v = jnp.where(here, pltpu.roll(first[LEVELS + z], 42 + z, 1), edge_v)
    beyond = [b for _, b in edge_parts(edge_u, edge_v)]

    def finish(z, results):
        fu, fv, du, dv = [
            a + jnp.where(lane == 0, pltpu.roll(e, 107 - z, 1), down_y(b))
            for (a, b), e in zip(results, beyond)
        ]
        drag = friction if z == 0 else 0.0
        second[z] = stepped(first[z], load_u, fu, du, drag)
        second[LEVELS + z] = stepped(first[LEVELS + z], load_v, fv, dv, drag)

    levels(
        first,
        lambda z, value: joined(value, edge_u, 84 + z),
        lambda z, value: joined(value, edge_v, 84 + z),
        lambda z: hard[z],
        main_inv2,
        finish,
    )
    for c in range(2):
        for z in range(LEVELS):
            out_v[c, z] = second[c * LEVELS + z, 2:6, :]
    leaving = [pltpu.make_async_copy(out_v, out_v_to, leaves.at[0])]
    leaving[0].start()
    for c in range(2):
        for l in range(LAYERS):
            at = c * LEVELS + l
            means[8 * (c * LAYERS + l) : 8 * (c * LAYERS + l) + 8, :] = 0.5 * (
                second[at] + second[at + 1]
            )
    send[...] = jnp.zeros(send.shape, f32)
    for v in range(2):
        from_x = origin[8 * v : 8 * v + 8]
        from_y = origin[16 + 8 * v : 24 + 8 * v]
        here = [from_x == x for x in range(4)]
        for part in range(4):
            values = [jnp.zeros((8, 128), f32)] * 10
            for x in range(4):
                for i in range(10):
                    at = 8 * (i // 5 * LAYERS + 5 * part + i % 5) + 2 + x
                    values[i] = jnp.where(here[x], lanes_of(row_of(means, at, 8), from_y), values[i])
            for l in range(5):
                even, odd = halves(values[l], values[5 + l], lane)
                start = part * 256 + 128 * v + l
                send[pl.ds(start, 8, stride=16), :] = even
                send[pl.ds(start + 8, 8, stride=16), :] = odd
        for part in range(4):
            span = slice(256 * part + 128 * v, 256 * part + 128 * v + 128)
            copy = pltpu.make_async_copy(send.at[span], send_to.at[span], leaves.at[1 + 4 * v + part])
            copy.start()
            leaving.append(copy)
    for copy in leaving:
        copy.wait()


def prepare_kernel(donor, shaft, origin, counts, left, hot):
    row256 = iota((256, 128), 0).astype(bf16)
    row16 = iota((16, 128), 0).astype(bf16)
    one = jnp.ones((), bf16)
    zero = jnp.zeros((), bf16)
    for g in range(4):
        ids = joined_rows(donor.at[0, g])
        for t in range(16):
            span = slice(2048 * g + 128 * t, 2048 * g + 128 * t + 128)
            cell = ids[t : t + 1]
            low = jnp.broadcast_to(cell & 255, (256, 128)).astype(bf16)
            hot[:, span] = jnp.where(row256 == low, one, zero)
            high = jnp.broadcast_to(cell >> 8, (16, 128)).astype(bf16)
            left[:, span] = jnp.where(row16 == high, one, zero)
    counts[...] = lax.dot_general(
        left[...], hot[...], (((1,), (1,)), ((), ())), preferred_element_type=f32
    )
    slot_row = iota((16, 128), 0)
    place = iota((16, 128), 1).astype(f32)
    low_row = iota((128, 128), 0)
    where_from = jnp.zeros((32, 128), f32)
    for x in range(4):
        slot = shaft[x : x + 1, :]
        here = slot_row == jnp.broadcast_to(slot >> 7, (16, 128))
        left = jnp.concatenate(
            [jnp.where(here, float(x), 0.0), jnp.where(here, place, 0.0)], axis=0
        )
        right = jnp.where(low_row == jnp.broadcast_to(slot & 127, (128, 128)), 1.0, 0.0)
        where_from = where_from + lax.dot_general(
            left.astype(bf16),
            right.astype(bf16),
            (((1,), (1,)), ((), ())),
            preferred_element_type=f32,
        )
    origin[...] = where_from.astype(jnp.int32) & 127


def total_kernel(arrived, donor, counts, out, left, hot, rows, sums):
    lane = iota((8, 128), 1)
    row256 = iota((256, 128), 0).astype(bf16)
    blocks = [((iota((16, 128), 0) + 16 * t) // 20).astype(bf16) for t in range(20)]
    one = jnp.ones((), bf16)
    zero = jnp.zeros((), bf16)
    ids = [joined_rows(donor.at[0, g]) for g in range(4)]
    result = jnp.zeros((320, 256), f32)
    for step in range(STEPS):
        for part in range(64 // STEPS):
            chunk = 64 // STEPS * step + part
            span = slice(128 * chunk, 128 * chunk + 128)
            cell = ids[chunk // 16][chunk % 16 : chunk % 16 + 1]
            high = jnp.broadcast_to(cell >> 8, (16, 128)).astype(bf16)
            low = jnp.broadcast_to(cell & 255, (256, 128)).astype(bf16)
            hot[:, span] = jnp.where(row256 == low, one, zero)
            x = arrived[16 * chunk : 16 * chunk + 16, :]
            at = 40 * chunk
            for c, value in enumerate(halves(x[:8], x[8:], lane)):
                value = value[:5]
                big = value.astype(bf16).astype(f32)
                for i, piece in enumerate((big, value - big)):
                    start = at + 10 * i + 5 * c
                    rows[start : start + 5, :] = piece
                    rows[start + 20 : start + 25, :] = piece
            tiles = [rows[at + o : at + o + 16, :].astype(bf16) for o in (0, 16, 12, 8, 4)]
            for t in range(20):
                left[16 * t : 16 * t + 16, span] = jnp.where(high == blocks[t], tiles[t % 5], zero)
        span = slice(8192 // STEPS * step, 8192 // STEPS * (step + 1))
        result = result + lax.dot_general(
            left[:, span], hot[:, span], (((1,), (1,)), ((), ())), preferred_element_type=f32
        )
    sums[...] = result
    for h in range(16):
        total = sums[20 * h : 20 * h + 10, :] + sums[20 * h + 10 : 20 * h + 20, :]
        total = total / jnp.maximum(counts[h : h + 1, :], 1.0)
        span = slice(256 * h, 256 * h + 256)
        for l in range(5):
            out[l, 0:1, span] = total[l : l + 1]
            out[l, 1:2, span] = total[5 + l : 6 + l]


def shape(*sizes):
    return jax.ShapeDtypeStruct(sizes, f32)


def near_pairs(count):
    even = [(i, i ^ 1) for i in range(count)]
    odd = []
    for i in range(1, count - 1, 2):
        odd += [(i, i + 1), (i + 1, i)]
    return even, odd


def shards(
    ice_depth,
    heat_state,
    elevation_slope_components,
    sliding_drag,
    adjacent_polygons,
    edge_timing_ratio,
    edge_average_normal_speed,
    tier_edge_normal_speed,
    position_donor_polygons,
    shaft_holding_position,
    prior_node_motion,
):
    ice = ice_depth.reshape(32, 128)
    drag = sliding_drag.reshape(32, 128)
    outgoing, near_out, far_out, own = pl.pallas_call(
        pack_kernel,
        out_shape=(
            shape(32 * BLOCK_ROWS, 128),
            shape(MSG_ROWS, 128),
            shape(MSG_ROWS, 128),
            shape(6, 32, 128),
        ),
        in_specs=[pl.BlockSpec(memory_space=pltpu.HBM)] * 7,
        out_specs=[pl.BlockSpec(memory_space=pltpu.HBM)] * 4,
        scratch_shapes=[
            pltpu.VMEM((32, 128), f32),
            pltpu.VMEM((LAYERS, 4096), f32),
            pltpu.VMEM((2, 4096), f32),
            pltpu.VMEM((32, 128), f32),
            pltpu.VMEM((32, 64), jnp.int32),
            pltpu.VMEM((4, 128), jnp.int32),
            pltpu.VMEM((2, LEVELS, 4, 128), f32),
            pltpu.VMEM((32 * BLOCK_ROWS, 128), f32),
            pltpu.VMEM((MSG_ROWS, 128), f32),
            pltpu.VMEM((MSG_ROWS, 128), f32),
            pltpu.VMEM((6, 32, 128), f32),
            pltpu.SemaphoreType.DMA((7,)),
            pltpu.SemaphoreType.DMA((5,)),
        ],
        compiler_params=WIDE,
        name="pack",
    )(
        ice,
        heat_state,
        elevation_slope_components,
        drag,
        position_donor_polygons,
        shaft_holding_position,
        prior_node_motion,
    )
    arrived = lax.all_to_all(outgoing, "dom", split_axis=0, concat_axis=0, tiled=True)
    even, odd = near_pairs(lax.axis_size("dom"))
    near = lax.ppermute(near_out, "dom", even)
    far = lax.ppermute(far_out, "dom", odd)
    donor, shaft, near_out = lax.optimization_barrier(
        (position_donor_polygons, shaft_holding_position, near_out)
    )
    origin, counts = pl.pallas_call(
        prepare_kernel,
        out_shape=(jax.ShapeDtypeStruct((32, 128), jnp.int32), shape(16, 256)),
        scratch_shapes=[pltpu.VMEM((16, 8192), bf16), pltpu.VMEM((256, 8192), bf16)],
        compiler_params=PARAMS,
        name="prepare",
    )(donor, shaft)
    arrived, origin = lax.optimization_barrier((arrived, origin))
    geo, vext, edge = pl.pallas_call(
        column_kernel,
        out_shape=(shape(FIELDS, 8, 128), shape(2 * LEVELS, 8, 128), shape(56, 128)),
        scratch_shapes=[pltpu.VMEM((8, 128), jnp.int32)],
        compiler_params=PARAMS,
        name="columns",
    )(arrived, shaft_holding_position, near, far, prior_node_motion)
    even, odd = near_pairs(lax.axis_size("grp"))
    edge_near = lax.ppermute(edge, "grp", even)
    edge_far = lax.ppermute(edge, "grp", odd)
    partial = pl.pallas_call(
        inner_kernel,
        out_shape=shape(4 * LEVELS, 8, 128),
        compiler_params=PARAMS,
        name="inner",
    )(geo, vext)
    node_velocity, send = pl.pallas_call(
        ice_kernel,
        out_shape=(shape(2, LEVELS, 4, 128), shape(1024, 128)),
        scratch_shapes=[
            pltpu.VMEM((LAYERS, 8, 128), f32),
            pltpu.VMEM((2 * LEVELS, 8, 128), f32),
            pltpu.VMEM((2 * LEVELS, 8, 128), f32),
            pltpu.VMEM((2 * LAYERS * 8, 128), f32),
            pltpu.VMEM((2, LEVELS, 4, 128), f32),
            pltpu.VMEM((1024, 128), f32),
            pltpu.SemaphoreType.DMA((9,)),
        ],
        out_specs=[pl.BlockSpec(memory_space=pltpu.HBM)] * 2,
        compiler_params=PARAMS,
        name="velocity",
    )(geo, vext, partial, edge, edge_near, edge_far, origin)
    back = lax.all_to_all(send, ("grp", "dom"), split_axis=0, concat_axis=0, tiled=True)
    depth, heat = pl.pallas_call(
        advect_kernel,
        out_shape=(shape(32, 128), shape(5, 4096)),
        scratch_shapes=[pltpu.VMEM((6, 48, 128), f32)],
        compiler_params=PARAMS,
        name="advect",
    )(
        own,
        adjacent_polygons,
        edge_timing_ratio,
        edge_average_normal_speed,
        tier_edge_normal_speed,
        near,
        far,
    )
    tier_motion = pl.pallas_call(
        total_kernel,
        out_shape=shape(5, 2, 4096),
        scratch_shapes=[
            pltpu.VMEM((320, 8192), bf16),
            pltpu.VMEM((256, 8192), bf16),
            pltpu.VMEM((64 * 40, 128), f32),
            pltpu.VMEM((320, 256), f32),
        ],
        compiler_params=PARAMS,
        name="totals",
    )(back, position_donor_polygons, counts)
    return (depth.reshape(4096), heat, node_velocity, jnp.transpose(tier_motion, (1, 0, 2)))


def solution(mesh):
    in_specs = (
        P("dom"),
        P(None, "dom"),
        P(None, "dom"),
        P("dom"),
        P(None, "dom"),
        P(None, "dom"),
        P(None, "dom"),
        P("grp", None, "dom"),
        P("dom", None, None, None),
        P("dom", "grp"),
        P(None, None, "dom", "grp"),
    )
    out_specs = (P("dom"), P("grp", "dom"), P(None, None, "dom", "grp"), P(None, "grp", "dom"))
    return jax.shard_map(shards, mesh=mesh, in_specs=in_specs, out_specs=out_specs, check_vma=False)
```

```python
import math

import jax
import jax.numpy as jnp
from jax import lax
from jax.experimental import pallas as pl
from jax.experimental.pallas import tpu as pltpu
from jax.sharding import PartitionSpec as P

KAPPA = 1.0 / math.sqrt(3.0)
EPS_RATE = 0.01
LOG2E = math.log2(math.e)
SCALE = 4096.0
LAYERS = 20
LEVELS = 21
FIELDS = 24
PAIRS = 12
BLOCK_ROWS = 36
MSG_ROWS = 136
STEPS = 8
f32 = jnp.float32
bf16 = jnp.bfloat16
PARAMS = pltpu.CompilerParams(vmem_limit_bytes=32 * 1024 * 1024)
WIDE = pltpu.CompilerParams(vmem_limit_bytes=60 * 1024 * 1024)


def lanes_of(table, index):
    return jnp.take_along_axis(table, index, axis=1, mode="promise_in_bounds")


def iota(shape, dim):
    return lax.broadcasted_iota(jnp.int32, shape, dim)


def row_of(ref, row, rows):
    return jnp.broadcast_to(ref[pl.ds(row, 1), :], (rows, 128))


def halves(first, second, lane):
    even = jnp.where(lane < 64, first, pltpu.roll(second, 64, 1))
    odd = jnp.where(lane < 64, pltpu.roll(first, 64, 1), second)
    return even, odd


def joined_rows(rows):
    return jnp.concatenate([rows[pl.ds(0, 16, stride=2), :], rows[pl.ds(1, 16, stride=2), :]], axis=1)


def pack_kernel(
    ice_in, heat_in, slope_in, drag_in, donor_in, shaft_in, prior_in,
    out_to, near_to, far_to, own_to,
    ice, heat, slope, drag, donor, shaft, prior, out, near, far, own, arrivals, leaves,
):
    g = lax.axis_index("grp")
    d = lax.axis_index("dom")
    pairs = (
        (heat_in, heat),
        (donor_in.at[0, g], donor),
        (ice_in, ice),
        (slope_in, slope),
        (drag_in, drag),
        (shaft_in, shaft),
        (prior_in, prior),
    )
    copies = [pltpu.make_async_copy(a, b, arrivals.at[i]) for i, (a, b) in enumerate(pairs)]
    for copy in copies:
        copy.start()
    out[0:12, :] = jnp.zeros((12, 128), f32)
    out[31 * 36 + 24 : 31 * 36 + 36, :] = jnp.zeros((12, 128), f32)
    for copy in copies[:5]:
        copy.wait()
    leaving = []
    ids = jnp.maximum(joined_rows(donor), 0)
    high = ids >> 7
    low = ids & 127
    lane = iota((8, 128), 1)
    highs = [high[:8], high[8:]]
    lows = [low[:8], low[8:]]

    def table(field, k):
        if field == 0:
            part = ice[k : k + 1, :]
        elif field < 3:
            part = slope[field - 1 : field, 128 * k : 128 * k + 128]
        elif field == 3:
            part = drag[k : k + 1, :]
        else:
            part = heat[field - 4 : field - 3, 128 * k : 128 * k + 128]
        return jnp.broadcast_to(part, (8, 128))

    for v in range(2):
        found = [jnp.zeros((8, 128), f32)] * FIELDS
        for k in range(32):
            here = highs[v] == k
            for f in range(FIELDS):
                found[f] = jnp.where(here, lanes_of(table(f, k), lows[v]), found[f])
        at = 576 * v
        for p in range(PAIRS):
            even, odd = halves(found[p], found[p + PAIRS], lane)
            out[pl.ds(at + 12 + p, 8, stride=72), :] = even
            out[pl.ds(at + 36 + p, 8, stride=72), :] = even
            if v == 0:
                out[pl.ds(60 + p, 7, stride=72), :] = even[1:]
                out[pl.ds(72 + p, 8, stride=72), :] = odd
            else:
                out[pl.ds(at - 12 + p, 8, stride=72), :] = even
                out[pl.ds(at + 72 + p, 7, stride=72), :] = odd[:7]
            out[pl.ds(at + 48 + p, 8, stride=72), :] = odd
            out[pl.ds(at + 24 + p, 8, stride=72), :] = odd
        span = slice(0, 536) if v == 0 else slice(536, 1152)
        copy = pltpu.make_async_copy(out.at[span], out_to.at[span], leaves.at[3 + v])
        copy.start()
        leaving.append(copy)
    for copy in copies[5:]:
        copy.wait()
    own[0] = ice[...]
    for part in range(4):

        @pl.when(g == part)
        def _():
            for i in range(5):
                layer = 5 * part + i
                for k in range(32):
                    own[i + 1, k : k + 1, :] = heat[layer : layer + 1, 128 * k : 128 * k + 128]

    def message(msg, row0, chunk0):
        for c in range(2):
            for z in range(LEVELS):
                at = 2 * (c * LEVELS + z)
                msg[at : at + 2, :] = prior[c, z, row0 : row0 + 2, :]
        msg[84:86, :] = shaft[row0 : row0 + 2, :].astype(f32)
        msg[86:88, :] = jnp.zeros((2, 128), f32)
        for i in range(6):
            msg[88 + 8 * i : 96 + 8 * i, :] = own[i, chunk0 : chunk0 + 8, :]

    even_device = d % 2 == 0

    @pl.when(even_device)
    def _():
        message(near, 2, 24)
        message(far, 0, 0)

    @pl.when(jnp.logical_not(even_device))
    def _():
        message(near, 0, 0)
        message(far, 2, 24)

    for i, (a, b) in enumerate(((near, near_to), (far, far_to), (own, own_to))):
        copy = pltpu.make_async_copy(a, b, leaves.at[i])
        copy.start()
        leaving.append(copy)
    for copy in leaving:
        copy.wait()


def advect_kernel(own, adjacent, ratio, mean_speed, tier_speed, near, far, depth_out, heat_out, ext):
    d = lax.axis_index("dom")
    even_device = d % 2 == 0
    for i in range(6):
        a = near[88 + 8 * i : 96 + 8 * i, :]
        b = far[88 + 8 * i : 96 + 8 * i, :]
        ext[i, 0:8, :] = jnp.where(even_device, b, a)
        ext[i, 40:48, :] = jnp.where(even_device, a, b)
        ext[i, 8:40, :] = own[i]

    @pl.loop(0, 32)
    def _(k):
        span = pl.ds(pl.multiple_of(128 * k, 128), 128)
        cell = adjacent[:, span] - (d * 4096 - 1024)
        low = cell & 127
        turn = (cell >> 7) - k
        beside = [jnp.zeros((6, 128), f32) for _ in range(6)]
        for r in range(17):
            here = turn == r
            for i in range(6):
                rows = jnp.broadcast_to(ext[i, pl.ds(k + r, 1), :], (6, 128))
                beside[i] = jnp.where(here, lanes_of(rows, low), beside[i])
        weight = ratio[:, span]
        for i in range(6):
            here = ext[i, pl.ds(k + 8, 1), :]
            speed = mean_speed[:, span] if i == 0 else tier_speed[i - 1, :, span]
            flow = weight * (jnp.maximum(speed, 0.0) * here + jnp.minimum(speed, 0.0) * beside[i])
            result = here - jnp.sum(flow, axis=0, keepdims=True)
            if i == 0:
                depth_out[pl.ds(k, 1), :] = result
            else:
                heat_out[i - 1 : i, span] = result


def column_kernel(arrived, shaft, near, far, prior, geo, vext, edge, slots):
    d = lax.axis_index("dom")
    even_device = d % 2 == 0
    row = iota((8, 128), 0)
    lane = iota((8, 128), 1)

    def sides(start, count):
        a = near[start : start + count, :]
        b = far[start : start + count, :]
        return jnp.where(even_device, b, a), jnp.where(even_device, a, b)

    left, right = sides(84, 2)
    slots[0:2, :] = left.astype(jnp.int32)
    slots[2:6, :] = shaft[...]
    slots[6:8, :] = right.astype(jnp.int32)
    slot = slots[...]
    owner = slot >> 6
    low = slot & 63
    low2 = low + 64
    found = [jnp.zeros((8, 128), f32) for _ in range(FIELDS)]
    upper = row < 2
    middle = row < 6
    for p in range(32):
        here = owner == p
        for f in range(PAIRS):
            at = BLOCK_ROWS * p + f
            rows = jnp.where(
                upper,
                row_of(arrived, at, 8),
                jnp.where(middle, row_of(arrived, at + 12, 8), row_of(arrived, at + 24, 8)),
            )
            found[f] = jnp.where(here, lanes_of(rows, low), found[f])
            found[f + PAIRS] = jnp.where(here, lanes_of(rows, low2), found[f + PAIRS])
    first = jnp.where(d == 0, 2, 0)
    last = jnp.where(d == lax.axis_size("dom") - 1, 5, 7)
    inside = jnp.logical_and(row >= first, row <= last)
    found = [jnp.where(inside, value, 0.0) for value in found]
    load_u = -(found[0] * found[1]) * SCALE
    load_v = -(found[0] * found[2]) * SCALE
    friction = found[3] * SCALE
    geo[0] = found[0]
    geo[1] = load_u
    geo[2] = load_v
    geo[3] = friction
    for l in range(LAYERS):
        geo[4 + l] = found[4 + l]
    for cz in range(2 * LEVELS):
        left, right = sides(2 * cz, 2)
        vext[cz, 0:2, :] = left
        vext[cz, 2:6, :] = prior[cz // LEVELS, cz % LEVELS]
        vext[cz, 6:8, :] = right
    group = lane // LEVELS
    pick = jnp.where(group < 2, group, jnp.where(group < 4, 124 + group, 0))
    level = lane - group * LEVELS
    for c in range(2):
        value = jnp.zeros((8, 128), f32)
        for z in range(LEVELS):
            value = jnp.where(level == z, lanes_of(vext[c * LEVELS + z], pick), value)
        edge[8 * c : 8 * c + 8, :] = value
    value = jnp.zeros((8, 128), f32)
    for l in range(LAYERS):
        value = jnp.where(level == l, lanes_of(found[4 + l], pick), value)
    edge[16:24, :] = value
    edge[24:32, :] = lanes_of(found[0], pick)
    edge[32:40, :] = lanes_of(load_u, pick)
    edge[40:48, :] = lanes_of(load_v, pick)
    edge[48:56, :] = jnp.where(level == 0, lanes_of(friction, pick), 0.0)


def interpolate(a, b):
    diff = b - a
    total = a + b
    part = KAPPA * diff
    return diff, total - part, total + part


def spread(a, b):
    total = a + b
    part = KAPPA * (a - b)
    return total, part


def spread_square(a, b):
    total = (1.0 + KAPPA * KAPPA) * (a + b)
    part = (2.0 * KAPPA) * (a - b)
    return total + part, total - part


def up_x(value):
    return pltpu.roll(value, 7, 0)


def down_x(value):
    return pltpu.roll(value, 1, 0)


def level_terms(value, value_y):
    dy, ya, yb = interpolate(value, value_y)
    _, along_y0, along_y1 = interpolate(dy, up_x(dy))
    along_x0, z00, z10 = interpolate(ya, up_x(ya))
    along_x1, z01, z11 = interpolate(yb, up_x(yb))
    return [along_x0, along_x1, along_y0, along_y1, z00, z01, z10, z11]


def element(low_u, top_u, low_v, top_v, hard, inverse2, keep=None):
    def gradients(low, top):
        x = [interpolate(low[q], top[q])[1:] for q in (0, 1)]
        y = [interpolate(low[2 + q], top[2 + q])[1:] for q in (0, 1)]
        z = [top[4 + q] - low[4 + q] for q in range(4)]
        return x, y, z

    ux, uy, uz = gradients(low_u, top_u)
    vx, vy, vz = gradients(low_v, top_v)
    vertical = [
        (uz[q] * uz[q] + vz[q] * vz[q]) * (0.25 * inverse2) + EPS_RATE for q in range(4)
    ]
    vy2 = [[vy[a][b] * vy[a][b] for b in (0, 1)] for a in (0, 1)]
    ex, ey, ez = {}, {}, {}
    ev, eu, wx, wy = {}, {}, {}, {}

    def put(store, key, value):
        store[key] = value if key not in store else store[key] + value

    for qx in (0, 1):
        for qy in (0, 1):
            for qz in (0, 1):
                a = ux[qy][qz]
                b = vy[qx][qz]
                shear = uy[qx][qz] + vx[qy][qz]
                rate = (
                    a * (a + b) + vy2[qx][qz] + 0.25 * (shear * shear) + vertical[2 * qx + qy]
                )
                eta = jnp.exp2(hard - jnp.log2(rate) * (1.0 / 3.0))
                if keep is not None:
                    eta = jnp.where(keep, eta, 0.0)
                put(ex, (qy, qz), eta)
                put(ey, (qx, qz), eta)
                put(ez, 2 * qx + qy, eta)
                put(ev, (qy, qz), eta * b)
                put(eu, (qx, qz), eta * a)
                w = eta * shear
                put(wx, (qy, qz), w)
                put(wy, (qx, qz), w)
    ez = [ez[q] * inverse2 for q in range(4)]
    lows, tops = [], []

    def add_spread(a, b):
        total, part = spread(a, b)
        lows.append(total + part)
        tops.append(total - part)

    def flux(e, g, s):
        half = (g + g) * e + s
        return half + half

    for q in (0, 1):
        add_spread(*[flux(ex[q, z], ux[q][z], ev[q, z]) for z in (0, 1)])
    for q in (0, 1):
        add_spread(wy[q, 0], wy[q, 1])
    for q in range(4):
        value = ez[q] * uz[q]
        lows.append(-value)
        tops.append(value)
    for q in (0, 1):
        add_spread(wx[q, 0], wx[q, 1])
    for q in (0, 1):
        add_spread(*[flux(ey[q, z], vy[q][z], eu[q, z]) for z in (0, 1)])
    for q in range(4):
        value = ez[q] * vz[q]
        lows.append(-value)
        tops.append(value)
    for q in (0, 1):
        a, b = spread_square(ex[q, 0], ex[q, 1])
        lows.append(a)
        tops.append(b)
    for q in (0, 1):
        a, b = spread_square(ey[q, 0], ey[q, 1])
        lows.append(a)
        tops.append(b)
    lows += ez
    tops += ez
    return lows, tops


def node_parts(acc):
    results = []
    for c in (0, 1):
        x0, x1, y0, y1, z00, z01, z10, z11 = acc[8 * c : 8 * c + 8]
        total, part = spread(y0, y1)
        hd = (total + part) + down_x(total - part)
        both = []
        for along, a, b in ((x0, z00, z10), (x1, z01, z11)):
            total, part = spread(a, b)
            part = part - along
            both.append((total + part) + down_x(total - part))
        total, part = spread(both[0], both[1])
        part = part - hd
        results.append((total + part, total - part))
    x0, x1, y0, y1, z00, z01, z10, z11 = acc[16:24]
    hx = [x0 + down_x(x0), x1 + down_x(x1)]
    a, b = spread_square(y0, y1)
    hy = a + down_x(b)
    hz = []
    for za, zb in ((z00, z10), (z01, z11)):
        a, b = spread_square(za, zb)
        hz.append(a + down_x(b))
    a, b = spread_square(4.0 * hx[0] + hz[0], 4.0 * hx[1] + hz[1])
    results.append((a + hy, b + hy))
    hy4 = 4.0 * hy
    a, b = spread_square(hx[0] + hz[0], hx[1] + hz[1])
    results.append((a + hy4, b + hy4))
    return results


def corners(value, value_y):
    pair = value + value_y
    return pair + up_x(pair)


def geometry(depth4):
    dz = depth4 * (0.25 / LAYERS)
    dz = jnp.where(dz > 0.0, dz, 1.0)
    inverse = 0.25 / dz
    return jnp.log2(dz * 16.0), inverse * inverse


def hardness(log_depth, warmth4):
    return log_depth - (0.25 * LOG2E) * warmth4


def at_lane(value, index):
    return lanes_of(value, jnp.full((8, 128), index, jnp.int32))


def up_y(value):
    return pltpu.roll(value, 127, 1)


def down_y(value):
    return pltpu.roll(value, 1, 1)


def levels(source, next_u, next_v, hard, inverse2, finish):
    def terms(z):
        u = source[z]
        v = source[LEVELS + z]
        return level_terms(u, next_u(z, u)) + level_terms(v, next_v(z, v))

    def body(z, carry):
        low, tops = carry[:16], carry[16:]
        top = terms(z + 1)
        lows, next_tops = element(low[:8], top[:8], low[8:], top[8:], hard(z), inverse2)
        finish(z, node_parts([a + b for a, b in zip(lows, tops)]))
        return (*top, *next_tops)

    zero = jnp.zeros((8, 128), f32)
    carry = (*terms(0), *([zero] * 24))
    for z in range(LAYERS):
        carry = body(z, carry)
    finish(LAYERS, node_parts(list(carry[16:])))


def inner_kernel(geo, vext, partial):
    lane = iota((8, 128), 1)
    depth = geo[0]
    log_depth, inverse2 = geometry(corners(depth, up_y(depth)))

    def hard(z):
        warm = geo[4 + z]
        return hardness(log_depth, corners(warm, up_y(warm)))

    def beside(z, value):
        return up_y(value)

    def finish(z, results):
        for q, (a, b) in enumerate(results):
            partial[q * LEVELS + z] = jnp.where(lane == 127, 0.0, a) + jnp.where(
                lane == 0, 0.0, down_y(b)
            )

    levels(vext, beside, beside, hard, inverse2, finish)


def ice_kernel(
    geo, vext, partial, edge, edge_near, edge_far, origin, out_v_to, send_to,
    hard, first, second, means, out_v, send, leaves,
):
    g = lax.axis_index("grp")
    d = lax.axis_index("dom")
    groups = lax.axis_size("grp")
    domains = lax.axis_size("dom")
    row = iota((8, 128), 0)
    lane = iota((8, 128), 1)
    group = lane // LEVELS
    level = lane - group * LEVELS
    even_group = g % 2 == 0

    def edge_field(i):
        span = slice(8 * i, 8 * i + 8)
        own = edge[span, :]
        a = edge_near[span, :]
        b = edge_far[span, :]
        left = jnp.where(even_group, b, a)
        right = jnp.where(even_group, a, b)
        return jnp.where(
            lane < 42,
            pltpu.roll(left, 86, 1),
            jnp.where(
                lane < 63,
                pltpu.roll(own, 42, 1),
                jnp.where(lane < 84, own, pltpu.roll(right, 84, 1)),
            ),
        )

    edge_u, edge_v, edge_t, edge_h, edge_fu, edge_fv, edge_b = [edge_field(i) for i in range(7)]

    def edge_up(value):
        return pltpu.roll(value, 107, 1)

    def joined(value, beyond, index):
        return jnp.where(lane == 127, pltpu.roll(beyond, 127 - index, 1), up_y(value))

    edge_log, edge_inv2 = geometry(corners(edge_h, edge_up(edge_h)))
    edge_hard = hardness(edge_log, corners(edge_t, edge_up(edge_t)))
    depth = geo[0]
    main_log, main_inv2 = geometry(corners(depth, joined(depth, edge_h, 84)))
    for l in range(LAYERS):
        warm = geo[4 + l]
        hard[l] = hardness(main_log, corners(warm, joined(warm, edge_t, 84 + l)))

    load_u = geo[1]
    load_v = geo[2]
    friction = geo[3]
    keep = jnp.logical_and(level != LAYERS, lane < 6 * LEVELS)
    first_row = jnp.where(d == 0, 2, 1)
    last_row = jnp.where(d == domains - 1, 5, 6)
    inside = jnp.logical_and(row >= first_row, row <= last_row)
    edge_inside = jnp.logical_and(
        inside,
        jnp.logical_or(
            jnp.logical_and(group == 1, g > 0),
            jnp.logical_and(group == 4, g < groups - 1),
        ),
    )

    def edge_parts(u, v):
        low_u = level_terms(u, edge_up(u))
        low_v = level_terms(v, edge_up(v))
        top_u = [up_y(t) for t in low_u]
        top_v = [up_y(t) for t in low_v]
        lows, tops = element(low_u, top_u, low_v, top_v, edge_hard, edge_inv2, keep)
        return node_parts([a + down_y(b) for a, b in zip(lows, tops)])

    def stepped(value, load, force, diagonal, drag):
        return value + 0.5 * (load - force - drag * value) / (diagonal + drag)

    parts = edge_parts(edge_u, edge_v)
    for z in range(LEVELS):
        sums = []
        for q, (a, b) in enumerate(parts):
            rim = jnp.where(lane == 127, pltpu.roll(a, 64 - z, 1), 0.0)
            rim = jnp.where(lane == 0, pltpu.roll(b, 107 - z, 1), rim)
            sums.append(partial[q * LEVELS + z] + rim)
        fu, fv, du, dv = sums
        drag = friction if z == 0 else 0.0
        first[z] = jnp.where(inside, stepped(vext[z], load_u, fu, du, drag), 0.0)
        first[LEVELS + z] = jnp.where(inside, stepped(vext[LEVELS + z], load_v, fv, dv, drag), 0.0)

    def edge_final(c, value, load):
        (fa, fb), (da, db) = parts[c], parts[2 + c]
        force = fa + pltpu.roll(fb, LEVELS, 1)
        diagonal = da + pltpu.roll(db, LEVELS, 1)
        return jnp.where(edge_inside, stepped(value, load, force, diagonal, edge_b), 0.0)

    edge_u = edge_final(0, edge_u, edge_fu)
    edge_v = edge_final(1, edge_v, edge_fv)
    for z in range(LEVELS):
        here = lane == 42 + z
        edge_u = jnp.where(here, pltpu.roll(first[z], 42 + z, 1), edge_u)
        edge_v = jnp.where(here, pltpu.roll(first[LEVELS + z], 42 + z, 1), edge_v)
    beyond = [b for _, b in edge_parts(edge_u, edge_v)]

    def finish(z, results):
        fu, fv, du, dv = [
            a + jnp.where(lane == 0, pltpu.roll(e, 107 - z, 1), down_y(b))
            for (a, b), e in zip(results, beyond)
        ]
        drag = friction if z == 0 else 0.0
        second[z] = stepped(first[z], load_u, fu, du, drag)
        second[LEVELS + z] = stepped(first[LEVELS + z], load_v, fv, dv, drag)

    levels(
        first,
        lambda z, value: joined(value, edge_u, 84 + z),
        lambda z, value: joined(value, edge_v, 84 + z),
        lambda z: hard[z],
        main_inv2,
        finish,
    )
    for c in range(2):
        for z in range(LEVELS):
            out_v[c, z] = second[c * LEVELS + z, 2:6, :]
    leaving = [pltpu.make_async_copy(out_v, out_v_to, leaves.at[0])]
    leaving[0].start()
    for c in range(2):
        for l in range(LAYERS):
            at = c * LEVELS + l
            means[8 * (c * LAYERS + l) : 8 * (c * LAYERS + l) + 8, :] = 0.5 * (
                second[at] + second[at + 1]
            )
    send[...] = jnp.zeros(send.shape, f32)
    for v in range(2):
        from_x = origin[8 * v : 8 * v + 8]
        from_y = origin[16 + 8 * v : 24 + 8 * v]
        here = [from_x == x for x in range(4)]
        for part in range(4):
            values = [jnp.zeros((8, 128), f32)] * 10
            for x in range(4):
                for i in range(10):
                    at = 8 * (i // 5 * LAYERS + 5 * part + i % 5) + 2 + x
                    values[i] = jnp.where(here[x], lanes_of(row_of(means, at, 8), from_y), values[i])
            for l in range(5):
                even, odd = halves(values[l], values[5 + l], lane)
                start = part * 256 + 128 * v + l
                send[pl.ds(start, 8, stride=16), :] = even
                send[pl.ds(start + 8, 8, stride=16), :] = odd
        for part in range(4):
            span = slice(256 * part + 128 * v, 256 * part + 128 * v + 128)
            copy = pltpu.make_async_copy(send.at[span], send_to.at[span], leaves.at[1 + 4 * v + part])
            copy.start()
            leaving.append(copy)
    for copy in leaving:
        copy.wait()


def prepare_kernel(donor, shaft, origin, counts, left, hot):
    row256 = iota((256, 128), 0).astype(bf16)
    row16 = iota((16, 128), 0).astype(bf16)
    one = jnp.ones((), bf16)
    zero = jnp.zeros((), bf16)
    for g in range(4):
        ids = joined_rows(donor.at[0, g])
        for t in range(16):
            span = slice(2048 * g + 128 * t, 2048 * g + 128 * t + 128)
            cell = ids[t : t + 1]
            low = jnp.broadcast_to(cell & 255, (256, 128)).astype(bf16)
            hot[:, span] = jnp.where(row256 == low, one, zero)
            high = jnp.broadcast_to(cell >> 8, (16, 128)).astype(bf16)
            left[:, span] = jnp.where(row16 == high, one, zero)
    counts[...] = lax.dot_general(
        left[...], hot[...], (((1,), (1,)), ((), ())), preferred_element_type=f32
    )
    slot_row = iota((16, 128), 0)
    place = iota((16, 128), 1).astype(f32)
    low_row = iota((128, 128), 0)
    where_from = jnp.zeros((32, 128), f32)
    for x in range(4):
        slot = shaft[x : x + 1, :]
        here = slot_row == jnp.broadcast_to(slot >> 7, (16, 128))
        left = jnp.concatenate(
            [jnp.where(here, float(x), 0.0), jnp.where(here, place, 0.0)], axis=0
        )
        right = jnp.where(low_row == jnp.broadcast_to(slot & 127, (128, 128)), 1.0, 0.0)
        where_from = where_from + lax.dot_general(
            left.astype(bf16),
            right.astype(bf16),
            (((1,), (1,)), ((), ())),
            preferred_element_type=f32,
        )
    origin[...] = where_from.astype(jnp.int32) & 127


def total_kernel(arrived, donor, counts, out, left, hot, rows, sums):
    lane = iota((8, 128), 1)
    row256 = iota((256, 128), 0).astype(bf16)
    blocks = [((iota((16, 128), 0) + 16 * t) // 20).astype(bf16) for t in range(20)]
    one = jnp.ones((), bf16)
    zero = jnp.zeros((), bf16)
    ids = [joined_rows(donor.at[0, g]) for g in range(4)]
    result = jnp.zeros((320, 256), f32)
    for step in range(STEPS):
        for part in range(64 // STEPS):
            chunk = 64 // STEPS * step + part
            span = slice(128 * chunk, 128 * chunk + 128)
            cell = ids[chunk // 16][chunk % 16 : chunk % 16 + 1]
            high = jnp.broadcast_to(cell >> 8, (16, 128)).astype(bf16)
            low = jnp.broadcast_to(cell & 255, (256, 128)).astype(bf16)
            hot[:, span] = jnp.where(row256 == low, one, zero)
            x = arrived[16 * chunk : 16 * chunk + 16, :]
            at = 40 * chunk
            for c, value in enumerate(halves(x[:8], x[8:], lane)):
                value = value[:5]
                big = value.astype(bf16).astype(f32)
                for i, piece in enumerate((big, value - big)):
                    start = at + 10 * i + 5 * c
                    rows[start : start + 5, :] = piece
                    rows[start + 20 : start + 25, :] = piece
            tiles = [rows[at + o : at + o + 16, :].astype(bf16) for o in (0, 16, 12, 8, 4)]
            for t in range(20):
                left[16 * t : 16 * t + 16, span] = jnp.where(high == blocks[t], tiles[t % 5], zero)
        span = slice(8192 // STEPS * step, 8192 // STEPS * (step + 1))
        result = result + lax.dot_general(
            left[:, span], hot[:, span], (((1,), (1,)), ((), ())), preferred_element_type=f32
        )
    sums[...] = result
    for h in range(16):
        total = sums[20 * h : 20 * h + 10, :] + sums[20 * h + 10 : 20 * h + 20, :]
        total = total / jnp.maximum(counts[h : h + 1, :], 1.0)
        span = slice(256 * h, 256 * h + 256)
        for l in range(5):
            out[l, 0:1, span] = total[l : l + 1]
            out[l, 1:2, span] = total[5 + l : 6 + l]


def shape(*sizes):
    return jax.ShapeDtypeStruct(sizes, f32)


def near_pairs(count):
    even = [(i, i ^ 1) for i in range(count)]
    odd = []
    for i in range(1, count - 1, 2):
        odd += [(i, i + 1), (i + 1, i)]
    return even, odd


def shards(
    ice_depth,
    heat_state,
    elevation_slope_components,
    sliding_drag,
    adjacent_polygons,
    edge_timing_ratio,
    edge_average_normal_speed,
    tier_edge_normal_speed,
    position_donor_polygons,
    shaft_holding_position,
    prior_node_motion,
):
    ice = ice_depth.reshape(32, 128)
    drag = sliding_drag.reshape(32, 128)
    outgoing, near_out, far_out, own = pl.pallas_call(
        pack_kernel,
        out_shape=(
            shape(32 * BLOCK_ROWS, 128),
            shape(MSG_ROWS, 128),
            shape(MSG_ROWS, 128),
            shape(6, 32, 128),
        ),
        in_specs=[pl.BlockSpec(memory_space=pltpu.HBM)] * 7,
        out_specs=[pl.BlockSpec(memory_space=pltpu.HBM)] * 4,
        scratch_shapes=[
            pltpu.VMEM((32, 128), f32),
            pltpu.VMEM((LAYERS, 4096), f32),
            pltpu.VMEM((2, 4096), f32),
            pltpu.VMEM((32, 128), f32),
            pltpu.VMEM((32, 64), jnp.int32),
            pltpu.VMEM((4, 128), jnp.int32),
            pltpu.VMEM((2, LEVELS, 4, 128), f32),
            pltpu.VMEM((32 * BLOCK_ROWS, 128), f32),
            pltpu.VMEM((MSG_ROWS, 128), f32),
            pltpu.VMEM((MSG_ROWS, 128), f32),
            pltpu.VMEM((6, 32, 128), f32),
            pltpu.SemaphoreType.DMA((7,)),
            pltpu.SemaphoreType.DMA((5,)),
        ],
        compiler_params=WIDE,
        name="pack",
    )(
        ice,
        heat_state,
        elevation_slope_components,
        drag,
        position_donor_polygons,
        shaft_holding_position,
        prior_node_motion,
    )
    arrived = lax.all_to_all(
        outgoing.reshape(32, 1, BLOCK_ROWS * 128), "dom", split_axis=0, concat_axis=0, tiled=True
    ).reshape(32 * BLOCK_ROWS, 128)
    even, odd = near_pairs(lax.axis_size("dom"))
    near = lax.ppermute(near_out, "dom", even)
    far = lax.ppermute(far_out, "dom", odd)
    donor, shaft, near_out = lax.optimization_barrier(
        (position_donor_polygons, shaft_holding_position, near_out)
    )
    origin, counts = pl.pallas_call(
        prepare_kernel,
        out_shape=(jax.ShapeDtypeStruct((32, 128), jnp.int32), shape(16, 256)),
        scratch_shapes=[pltpu.VMEM((16, 8192), bf16), pltpu.VMEM((256, 8192), bf16)],
        compiler_params=PARAMS,
        name="prepare",
    )(donor, shaft)
    arrived, origin = lax.optimization_barrier((arrived, origin))
    geo, vext, edge = pl.pallas_call(
        column_kernel,
        out_shape=(shape(FIELDS, 8, 128), shape(2 * LEVELS, 8, 128), shape(56, 128)),
        scratch_shapes=[pltpu.VMEM((8, 128), jnp.int32)],
        compiler_params=PARAMS,
        name="columns",
    )(arrived, shaft_holding_position, near, far, prior_node_motion)
    even, odd = near_pairs(lax.axis_size("grp"))
    edge_near = lax.ppermute(edge, "grp", even)
    edge_far = lax.ppermute(edge, "grp", odd)
    partial = pl.pallas_call(
        inner_kernel,
        out_shape=shape(4 * LEVELS, 8, 128),
        compiler_params=PARAMS,
        name="inner",
    )(geo, vext)
    node_velocity, send = pl.pallas_call(
        ice_kernel,
        out_shape=(shape(2, LEVELS, 4, 128), shape(1024, 128)),
        scratch_shapes=[
            pltpu.VMEM((LAYERS, 8, 128), f32),
            pltpu.VMEM((2 * LEVELS, 8, 128), f32),
            pltpu.VMEM((2 * LEVELS, 8, 128), f32),
            pltpu.VMEM((2 * LAYERS * 8, 128), f32),
            pltpu.VMEM((2, LEVELS, 4, 128), f32),
            pltpu.VMEM((1024, 128), f32),
            pltpu.SemaphoreType.DMA((9,)),
        ],
        out_specs=[pl.BlockSpec(memory_space=pltpu.HBM)] * 2,
        compiler_params=PARAMS,
        name="velocity",
    )(geo, vext, partial, edge, edge_near, edge_far, origin)
    back = lax.all_to_all(send, ("grp", "dom"), split_axis=0, concat_axis=0, tiled=True)
    depth, heat = pl.pallas_call(
        advect_kernel,
        out_shape=(shape(32, 128), shape(5, 4096)),
        scratch_shapes=[pltpu.VMEM((6, 48, 128), f32)],
        compiler_params=PARAMS,
        name="advect",
    )(
        own,
        adjacent_polygons,
        edge_timing_ratio,
        edge_average_normal_speed,
        tier_edge_normal_speed,
        near,
        far,
    )
    tier_motion = pl.pallas_call(
        total_kernel,
        out_shape=shape(5, 2, 4096),
        scratch_shapes=[
            pltpu.VMEM((320, 8192), bf16),
            pltpu.VMEM((256, 8192), bf16),
            pltpu.VMEM((64 * 40, 128), f32),
            pltpu.VMEM((320, 256), f32),
        ],
        compiler_params=PARAMS,
        name="totals",
    )(back, position_donor_polygons, counts)
    return (depth.reshape(4096), heat, node_velocity, jnp.transpose(tier_motion, (1, 0, 2)))


def solution(mesh):
    in_specs = (
        P("dom"),
        P(None, "dom"),
        P(None, "dom"),
        P("dom"),
        P(None, "dom"),
        P(None, "dom"),
        P(None, "dom"),
        P("grp", None, "dom"),
        P("dom", None, None, None),
        P("dom", "grp"),
        P(None, None, "dom", "grp"),
    )
    out_specs = (P("dom"), P("grp", "dom"), P(None, None, "dom", "grp"), P(None, "grp", "dom"))
    return jax.shard_map(shards, mesh=mesh, in_specs=in_specs, out_specs=out_specs, check_vma=False)
```

```python
import math

import jax
import jax.numpy as jnp
from jax import lax
from jax.experimental import pallas as pl
from jax.experimental.pallas import tpu as pltpu
from jax.sharding import PartitionSpec as P

KAPPA = 1.0 / math.sqrt(3.0)
EPS_RATE = 0.01
LOG2E = math.log2(math.e)
SCALE = 4096.0
LAYERS = 20
LEVELS = 21
FIELDS = 24
PAIRS = 12
BLOCK_ROWS = 36
MSG_ROWS = 136
WIDTH = 256
f32 = jnp.float32
bf16 = jnp.bfloat16
PARAMS = pltpu.CompilerParams(vmem_limit_bytes=32 * 1024 * 1024)
WIDE = pltpu.CompilerParams(vmem_limit_bytes=60 * 1024 * 1024)


def lanes_of(table, index):
    return jnp.take_along_axis(table, index, axis=1, mode="promise_in_bounds")


def iota(shape, dim):
    return lax.broadcasted_iota(jnp.int32, shape, dim)


def row_of(ref, row, rows):
    return jnp.broadcast_to(ref[pl.ds(row, 1), :], (rows, 128))


def halves(first, second, lane):
    even = jnp.where(lane < 64, first, pltpu.roll(second, 64, 1))
    odd = jnp.where(lane < 64, pltpu.roll(first, 64, 1), second)
    return even, odd


def joined_rows(rows):
    return jnp.concatenate([rows[pl.ds(0, 16, stride=2), :], rows[pl.ds(1, 16, stride=2), :]], axis=1)


def pack_kernel(
    ice_in, heat_in, slope_in, drag_in, donor_in, shaft_in, prior_in,
    out_to, near_to, far_to, own_to,
    ice, heat, slope, drag, donor, shaft, prior, out, near, far, own, arrivals, leaves,
):
    g = lax.axis_index("grp")
    d = lax.axis_index("dom")
    pairs = (
        (heat_in, heat),
        (donor_in.at[0, g], donor),
        (ice_in, ice),
        (slope_in, slope),
        (drag_in, drag),
        (shaft_in, shaft),
        (prior_in, prior),
    )
    copies = [pltpu.make_async_copy(a, b, arrivals.at[i]) for i, (a, b) in enumerate(pairs)]
    for copy in copies:
        copy.start()
    out[0:12, :] = jnp.zeros((12, 128), f32)
    out[31 * 36 + 24 : 31 * 36 + 36, :] = jnp.zeros((12, 128), f32)
    for copy in copies[:5]:
        copy.wait()
    leaving = []
    ids = jnp.maximum(joined_rows(donor), 0)
    high = ids >> 7
    low = ids & 127
    lane = iota((8, 128), 1)
    highs = [high[:8], high[8:]]
    lows = [low[:8], low[8:]]

    def table(field, k):
        if field == 0:
            part = ice[k : k + 1, :]
        elif field < 3:
            part = slope[field - 1 : field, 128 * k : 128 * k + 128]
        elif field == 3:
            part = drag[k : k + 1, :]
        else:
            part = heat[field - 4 : field - 3, 128 * k : 128 * k + 128]
        return jnp.broadcast_to(part, (8, 128))

    for v in range(2):
        found = [jnp.zeros((8, 128), f32)] * FIELDS
        for k in range(32):
            here = highs[v] == k
            for f in range(FIELDS):
                found[f] = jnp.where(here, lanes_of(table(f, k), lows[v]), found[f])
        at = 576 * v
        for p in range(PAIRS):
            even, odd = halves(found[p], found[p + PAIRS], lane)
            out[pl.ds(at + 12 + p, 8, stride=72), :] = even
            out[pl.ds(at + 36 + p, 8, stride=72), :] = even
            if v == 0:
                out[pl.ds(60 + p, 7, stride=72), :] = even[1:]
                out[pl.ds(72 + p, 8, stride=72), :] = odd
            else:
                out[pl.ds(at - 12 + p, 8, stride=72), :] = even
                out[pl.ds(at + 72 + p, 7, stride=72), :] = odd[:7]
            out[pl.ds(at + 48 + p, 8, stride=72), :] = odd
            out[pl.ds(at + 24 + p, 8, stride=72), :] = odd
        span = slice(0, 536) if v == 0 else slice(536, 1152)
        copy = pltpu.make_async_copy(out.at[span], out_to.at[span], leaves.at[3 + v])
        copy.start()
        leaving.append(copy)
    for copy in copies[5:]:
        copy.wait()
    own[0] = ice[...]
    for part in range(4):

        @pl.when(g == part)
        def _():
            for i in range(5):
                layer = 5 * part + i
                for k in range(32):
                    own[i + 1, k : k + 1, :] = heat[layer : layer + 1, 128 * k : 128 * k + 128]

    def message(msg, row0, chunk0):
        for c in range(2):
            for z in range(LEVELS):
                at = 2 * (c * LEVELS + z)
                msg[at : at + 2, :] = prior[c, z, row0 : row0 + 2, :]
        msg[84:86, :] = shaft[row0 : row0 + 2, :].astype(f32)
        msg[86:88, :] = jnp.zeros((2, 128), f32)
        for i in range(6):
            msg[88 + 8 * i : 96 + 8 * i, :] = own[i, chunk0 : chunk0 + 8, :]

    even_device = d % 2 == 0

    @pl.when(even_device)
    def _():
        message(near, 2, 24)
        message(far, 0, 0)

    @pl.when(jnp.logical_not(even_device))
    def _():
        message(near, 0, 0)
        message(far, 2, 24)

    for i, (a, b) in enumerate(((near, near_to), (far, far_to), (own, own_to))):
        copy = pltpu.make_async_copy(a, b, leaves.at[i])
        copy.start()
        leaving.append(copy)
    for copy in leaving:
        copy.wait()


def advect_kernel(own, adjacent, ratio, mean_speed, tier_speed, near, far, depth_out, heat_out, ext):
    d = lax.axis_index("dom")
    even_device = d % 2 == 0
    for i in range(6):
        a = near[88 + 8 * i : 96 + 8 * i, :]
        b = far[88 + 8 * i : 96 + 8 * i, :]
        ext[i, 0:8, :] = jnp.where(even_device, b, a)
        ext[i, 40:48, :] = jnp.where(even_device, a, b)
        ext[i, 8:40, :] = own[i]

    @pl.loop(0, 32)
    def _(k):
        span = pl.ds(pl.multiple_of(128 * k, 128), 128)
        cell = adjacent[:, span] - (d * 4096 - 1024)
        low = cell & 127
        turn = (cell >> 7) - k
        beside = [jnp.zeros((6, 128), f32) for _ in range(6)]
        for r in range(17):
            here = turn == r
            for i in range(6):
                rows = jnp.broadcast_to(ext[i, pl.ds(k + r, 1), :], (6, 128))
                beside[i] = jnp.where(here, lanes_of(rows, low), beside[i])
        weight = ratio[:, span]
        for i in range(6):
            here = ext[i, pl.ds(k + 8, 1), :]
            speed = mean_speed[:, span] if i == 0 else tier_speed[i - 1, :, span]
            flow = weight * (jnp.maximum(speed, 0.0) * here + jnp.minimum(speed, 0.0) * beside[i])
            result = here - jnp.sum(flow, axis=0, keepdims=True)
            if i == 0:
                depth_out[pl.ds(k, 1), :] = result
            else:
                heat_out[i - 1 : i, span] = result


def column_kernel(arrived, shaft, near, far, prior, geo, vext, edge, slots):
    d = lax.axis_index("dom")
    even_device = d % 2 == 0
    row = iota((8, 128), 0)
    lane = iota((8, 128), 1)

    def sides(start, count):
        a = near[start : start + count, :]
        b = far[start : start + count, :]
        return jnp.where(even_device, b, a), jnp.where(even_device, a, b)

    left, right = sides(84, 2)
    slots[0:2, :] = left.astype(jnp.int32)
    slots[2:6, :] = shaft[...]
    slots[6:8, :] = right.astype(jnp.int32)
    slot = slots[...]
    owner = slot >> 6
    low = slot & 63
    low2 = low + 64
    found = [jnp.zeros((8, 128), f32) for _ in range(FIELDS)]
    upper = row < 2
    middle = row < 6
    for p in range(32):
        here = owner == p
        for f in range(PAIRS):
            at = BLOCK_ROWS * p + f
            rows = jnp.where(
                upper,
                row_of(arrived, at, 8),
                jnp.where(middle, row_of(arrived, at + 12, 8), row_of(arrived, at + 24, 8)),
            )
            found[f] = jnp.where(here, lanes_of(rows, low), found[f])
            found[f + PAIRS] = jnp.where(here, lanes_of(rows, low2), found[f + PAIRS])
    first = jnp.where(d == 0, 2, 0)
    last = jnp.where(d == lax.axis_size("dom") - 1, 5, 7)
    inside = jnp.logical_and(row >= first, row <= last)
    found = [jnp.where(inside, value, 0.0) for value in found]
    load_u = -(found[0] * found[1]) * SCALE
    load_v = -(found[0] * found[2]) * SCALE
    friction = found[3] * SCALE
    geo[0] = found[0]
    geo[1] = load_u
    geo[2] = load_v
    geo[3] = friction
    for l in range(LAYERS):
        geo[4 + l] = found[4 + l]
    for cz in range(2 * LEVELS):
        left, right = sides(2 * cz, 2)
        vext[cz, 0:2, :] = left
        vext[cz, 2:6, :] = prior[cz // LEVELS, cz % LEVELS]
        vext[cz, 6:8, :] = right
    group = lane // LEVELS
    pick = jnp.where(group < 2, group, jnp.where(group < 4, 124 + group, 0))
    level = lane - group * LEVELS
    for c in range(2):
        value = jnp.zeros((8, 128), f32)
        for z in range(LEVELS):
            value = jnp.where(level == z, lanes_of(vext[c * LEVELS + z], pick), value)
        edge[8 * c : 8 * c + 8, :] = value
    value = jnp.zeros((8, 128), f32)
    for l in range(LAYERS):
        value = jnp.where(level == l, lanes_of(found[4 + l], pick), value)
    edge[16:24, :] = value
    edge[24:32, :] = lanes_of(found[0], pick)
    edge[32:40, :] = lanes_of(load_u, pick)
    edge[40:48, :] = lanes_of(load_v, pick)
    edge[48:56, :] = jnp.where(level == 0, lanes_of(friction, pick), 0.0)


def interpolate(a, b):
    diff = b - a
    total = a + b
    part = KAPPA * diff
    return diff, total - part, total + part


def spread(a, b):
    total = a + b
    part = KAPPA * (a - b)
    return total, part


def spread_square(a, b):
    total = (1.0 + KAPPA * KAPPA) * (a + b)
    part = (2.0 * KAPPA) * (a - b)
    return total + part, total - part


def up_x(value):
    return pltpu.roll(value, 7, 0)


def down_x(value):
    return pltpu.roll(value, 1, 0)


def level_terms(value, value_y):
    dy, ya, yb = interpolate(value, value_y)
    _, along_y0, along_y1 = interpolate(dy, up_x(dy))
    along_x0, z00, z10 = interpolate(ya, up_x(ya))
    along_x1, z01, z11 = interpolate(yb, up_x(yb))
    return [along_x0, along_x1, along_y0, along_y1, z00, z01, z10, z11]


def element(low_u, top_u, low_v, top_v, hard, inverse2, keep=None):
    def gradients(low, top):
        x = [interpolate(low[q], top[q])[1:] for q in (0, 1)]
        y = [interpolate(low[2 + q], top[2 + q])[1:] for q in (0, 1)]
        z = [top[4 + q] - low[4 + q] for q in range(4)]
        return x, y, z

    ux, uy, uz = gradients(low_u, top_u)
    vx, vy, vz = gradients(low_v, top_v)
    vertical = [
        (uz[q] * uz[q] + vz[q] * vz[q]) * (0.25 * inverse2) + EPS_RATE for q in range(4)
    ]
    vy2 = [[vy[a][b] * vy[a][b] for b in (0, 1)] for a in (0, 1)]
    ex, ey, ez = {}, {}, {}
    ev, eu, wx, wy = {}, {}, {}, {}

    def put(store, key, value):
        store[key] = value if key not in store else store[key] + value

    for qx in (0, 1):
        for qy in (0, 1):
            for qz in (0, 1):
                a = ux[qy][qz]
                b = vy[qx][qz]
                shear = uy[qx][qz] + vx[qy][qz]
                rate = (
                    a * (a + b) + vy2[qx][qz] + 0.25 * (shear * shear) + vertical[2 * qx + qy]
                )
                eta = jnp.exp2(hard - jnp.log2(rate) * (1.0 / 3.0))
                if keep is not None:
                    eta = jnp.where(keep, eta, 0.0)
                put(ex, (qy, qz), eta)
                put(ey, (qx, qz), eta)
                put(ez, 2 * qx + qy, eta)
                put(ev, (qy, qz), eta * b)
                put(eu, (qx, qz), eta * a)
                w = eta * shear
                put(wx, (qy, qz), w)
                put(wy, (qx, qz), w)
    ez = [ez[q] * inverse2 for q in range(4)]
    lows, tops = [], []

    def add_spread(a, b):
        total, part = spread(a, b)
        lows.append(total + part)
        tops.append(total - part)

    def flux(e, g, s):
        half = (g + g) * e + s
        return half + half

    for q in (0, 1):
        add_spread(*[flux(ex[q, z], ux[q][z], ev[q, z]) for z in (0, 1)])
    for q in (0, 1):
        add_spread(wy[q, 0], wy[q, 1])
    for q in range(4):
        value = ez[q] * uz[q]
        lows.append(-value)
        tops.append(value)
    for q in (0, 1):
        add_spread(wx[q, 0], wx[q, 1])
    for q in (0, 1):
        add_spread(*[flux(ey[q, z], vy[q][z], eu[q, z]) for z in (0, 1)])
    for q in range(4):
        value = ez[q] * vz[q]
        lows.append(-value)
        tops.append(value)
    for q in (0, 1):
        a, b = spread_square(ex[q, 0], ex[q, 1])
        lows.append(a)
        tops.append(b)
    for q in (0, 1):
        a, b = spread_square(ey[q, 0], ey[q, 1])
        lows.append(a)
        tops.append(b)
    lows += ez
    tops += ez
    return lows, tops


def node_parts(acc):
    results = []
    for c in (0, 1):
        x0, x1, y0, y1, z00, z01, z10, z11 = acc[8 * c : 8 * c + 8]
        total, part = spread(y0, y1)
        hd = (total + part) + down_x(total - part)
        both = []
        for along, a, b in ((x0, z00, z10), (x1, z01, z11)):
            total, part = spread(a, b)
            part = part - along
            both.append((total + part) + down_x(total - part))
        total, part = spread(both[0], both[1])
        part = part - hd
        results.append((total + part, total - part))
    x0, x1, y0, y1, z00, z01, z10, z11 = acc[16:24]
    hx = [x0 + down_x(x0), x1 + down_x(x1)]
    a, b = spread_square(y0, y1)
    hy = a + down_x(b)
    hz = []
    for za, zb in ((z00, z10), (z01, z11)):
        a, b = spread_square(za, zb)
        hz.append(a + down_x(b))
    a, b = spread_square(4.0 * hx[0] + hz[0], 4.0 * hx[1] + hz[1])
    results.append((a + hy, b + hy))
    hy4 = 4.0 * hy
    a, b = spread_square(hx[0] + hz[0], hx[1] + hz[1])
    results.append((a + hy4, b + hy4))
    return results


def corners(value, value_y):
    pair = value + value_y
    return pair + up_x(pair)


def geometry(depth4):
    dz = depth4 * (0.25 / LAYERS)
    dz = jnp.where(dz > 0.0, dz, 1.0)
    inverse = 0.25 / dz
    return jnp.log2(dz * 16.0), inverse * inverse


def hardness(log_depth, warmth4):
    return log_depth - (0.25 * LOG2E) * warmth4


def at_lane(value, index):
    return lanes_of(value, jnp.full((8, 128), index, jnp.int32))


def up_y(value):
    return pltpu.roll(value, 127, 1)


def down_y(value):
    return pltpu.roll(value, 1, 1)


def levels(source, next_u, next_v, hard, inverse2, finish):
    def terms(z):
        u = source[z]
        v = source[LEVELS + z]
        return level_terms(u, next_u(z, u)) + level_terms(v, next_v(z, v))

    def body(z, carry):
        low, tops = carry[:16], carry[16:]
        top = terms(z + 1)
        lows, next_tops = element(low[:8], top[:8], low[8:], top[8:], hard(z), inverse2)
        finish(z, node_parts([a + b for a, b in zip(lows, tops)]))
        return (*top, *next_tops)

    zero = jnp.zeros((8, 128), f32)
    carry = (*terms(0), *([zero] * 24))
    for z in range(LAYERS):
        carry = body(z, carry)
    finish(LAYERS, node_parts(list(carry[16:])))


def inner_kernel(geo, vext, partial):
    lane = iota((8, 128), 1)
    depth = geo[0]
    log_depth, inverse2 = geometry(corners(depth, up_y(depth)))

    def hard(z):
        warm = geo[4 + z]
        return hardness(log_depth, corners(warm, up_y(warm)))

    def beside(z, value):
        return up_y(value)

    def finish(z, results):
        for q, (a, b) in enumerate(results):
            partial[q * LEVELS + z] = jnp.where(lane == 127, 0.0, a) + jnp.where(
                lane == 0, 0.0, down_y(b)
            )

    levels(vext, beside, beside, hard, inverse2, finish)


def ice_kernel(
    geo, vext, partial, edge, edge_near, edge_far, origin, out_v_to, send_to,
    hard, first, second, means, out_v, send, leaves,
):
    g = lax.axis_index("grp")
    d = lax.axis_index("dom")
    groups = lax.axis_size("grp")
    domains = lax.axis_size("dom")
    row = iota((8, 128), 0)
    lane = iota((8, 128), 1)
    group = lane // LEVELS
    level = lane - group * LEVELS
    even_group = g % 2 == 0

    def edge_field(i):
        span = slice(8 * i, 8 * i + 8)
        own = edge[span, :]
        a = edge_near[span, :]
        b = edge_far[span, :]
        left = jnp.where(even_group, b, a)
        right = jnp.where(even_group, a, b)
        return jnp.where(
            lane < 42,
            pltpu.roll(left, 86, 1),
            jnp.where(
                lane < 63,
                pltpu.roll(own, 42, 1),
                jnp.where(lane < 84, own, pltpu.roll(right, 84, 1)),
            ),
        )

    edge_u, edge_v, edge_t, edge_h, edge_fu, edge_fv, edge_b = [edge_field(i) for i in range(7)]

    def edge_up(value):
        return pltpu.roll(value, 107, 1)

    def joined(value, beyond, index):
        return jnp.where(lane == 127, pltpu.roll(beyond, 127 - index, 1), up_y(value))

    edge_log, edge_inv2 = geometry(corners(edge_h, edge_up(edge_h)))
    edge_hard = hardness(edge_log, corners(edge_t, edge_up(edge_t)))
    depth = geo[0]
    main_log, main_inv2 = geometry(corners(depth, joined(depth, edge_h, 84)))
    for l in range(LAYERS):
        warm = geo[4 + l]
        hard[l] = hardness(main_log, corners(warm, joined(warm, edge_t, 84 + l)))

    load_u = geo[1]
    load_v = geo[2]
    friction = geo[3]
    keep = jnp.logical_and(level != LAYERS, lane < 6 * LEVELS)
    first_row = jnp.where(d == 0, 2, 1)
    last_row = jnp.where(d == domains - 1, 5, 6)
    inside = jnp.logical_and(row >= first_row, row <= last_row)
    edge_inside = jnp.logical_and(
        inside,
        jnp.logical_or(
            jnp.logical_and(group == 1, g > 0),
            jnp.logical_and(group == 4, g < groups - 1),
        ),
    )

    def edge_parts(u, v):
        low_u = level_terms(u, edge_up(u))
        low_v = level_terms(v, edge_up(v))
        top_u = [up_y(t) for t in low_u]
        top_v = [up_y(t) for t in low_v]
        lows, tops = element(low_u, top_u, low_v, top_v, edge_hard, edge_inv2, keep)
        return node_parts([a + down_y(b) for a, b in zip(lows, tops)])

    def stepped(value, load, force, diagonal, drag):
        return value + 0.5 * (load - force - drag * value) / (diagonal + drag)

    parts = edge_parts(edge_u, edge_v)
    for z in range(LEVELS):
        sums = []
        for q, (a, b) in enumerate(parts):
            rim = jnp.where(lane == 127, pltpu.roll(a, 64 - z, 1), 0.0)
            rim = jnp.where(lane == 0, pltpu.roll(b, 107 - z, 1), rim)
            sums.append(partial[q * LEVELS + z] + rim)
        fu, fv, du, dv = sums
        drag = friction if z == 0 else 0.0
        first[z] = jnp.where(inside, stepped(vext[z], load_u, fu, du, drag), 0.0)
        first[LEVELS + z] = jnp.where(inside, stepped(vext[LEVELS + z], load_v, fv, dv, drag), 0.0)

    def edge_final(c, value, load):
        (fa, fb), (da, db) = parts[c], parts[2 + c]
        force = fa + pltpu.roll(fb, LEVELS, 1)
        diagonal = da + pltpu.roll(db, LEVELS, 1)
        return jnp.where(edge_inside, stepped(value, load, force, diagonal, edge_b), 0.0)

    edge_u = edge_final(0, edge_u, edge_fu)
    edge_v = edge_final(1, edge_v, edge_fv)
    for z in range(LEVELS):
        here = lane == 42 + z
        edge_u = jnp.where(here, pltpu.roll(first[z], 42 + z, 1), edge_u)
        edge_v = jnp.where(here, pltpu.roll(first[LEVELS + z], 42 + z, 1), edge_v)
    beyond = [b for _, b in edge_parts(edge_u, edge_v)]

    def finish(z, results):
        fu, fv, du, dv = [
            a + jnp.where(lane == 0, pltpu.roll(e, 107 - z, 1), down_y(b))
            for (a, b), e in zip(results, beyond)
        ]
        drag = friction if z == 0 else 0.0
        second[z] = stepped(first[z], load_u, fu, du, drag)
        second[LEVELS + z] = stepped(first[LEVELS + z], load_v, fv, dv, drag)

    levels(
        first,
        lambda z, value: joined(value, edge_u, 84 + z),
        lambda z, value: joined(value, edge_v, 84 + z),
        lambda z: hard[z],
        main_inv2,
        finish,
    )
    for c in range(2):
        for z in range(LEVELS):
            out_v[c, z] = second[c * LEVELS + z, 2:6, :]
    leaving = [pltpu.make_async_copy(out_v, out_v_to, leaves.at[0])]
    leaving[0].start()
    for c in range(2):
        for l in range(LAYERS):
            at = c * LEVELS + l
            means[8 * (c * LAYERS + l) : 8 * (c * LAYERS + l) + 8, :] = 0.5 * (
                second[at] + second[at + 1]
            )
    send[...] = jnp.zeros(send.shape, f32)
    for v in range(2):
        from_x = origin[8 * v : 8 * v + 8]
        from_y = origin[16 + 8 * v : 24 + 8 * v]
        here = [from_x == x for x in range(4)]
        for part in range(4):
            values = [jnp.zeros((8, 128), f32)] * 10
            for x in range(4):
                for i in range(10):
                    at = 8 * (i // 5 * LAYERS + 5 * part + i % 5) + 2 + x
                    values[i] = jnp.where(here[x], lanes_of(row_of(means, at, 8), from_y), values[i])
            for l in range(5):
                even, odd = halves(values[l], values[5 + l], lane)
                start = part * 256 + 128 * v + l
                send[pl.ds(start, 8, stride=16), :] = even
                send[pl.ds(start + 8, 8, stride=16), :] = odd
        for part in range(4):
            span = slice(256 * part + 128 * v, 256 * part + 128 * v + 128)
            copy = pltpu.make_async_copy(send.at[span], send_to.at[span], leaves.at[1 + 4 * v + part])
            copy.start()
            leaving.append(copy)
    for copy in leaving:
        copy.wait()


def prepare_kernel(donor, shaft, origin, counts, left, hot):
    row256 = iota((256, 128), 0).astype(bf16)
    row16 = iota((16, 128), 0).astype(bf16)
    one = jnp.ones((), bf16)
    zero = jnp.zeros((), bf16)
    for g in range(4):
        ids = joined_rows(donor.at[0, g])
        for t in range(16):
            span = slice(2048 * g + 128 * t, 2048 * g + 128 * t + 128)
            cell = ids[t : t + 1]
            low = jnp.broadcast_to(cell & 255, (256, 128)).astype(bf16)
            hot[:, span] = jnp.where(row256 == low, one, zero)
            high = jnp.broadcast_to(cell >> 8, (16, 128)).astype(bf16)
            left[:, span] = jnp.where(row16 == high, one, zero)
    counts[...] = lax.dot_general(
        left[...], hot[...], (((1,), (1,)), ((), ())), preferred_element_type=f32
    )
    slot_row = iota((16, 128), 0)
    place = iota((16, 128), 1).astype(f32)
    low_row = iota((128, 128), 0)
    where_from = jnp.zeros((32, 128), f32)
    for x in range(4):
        slot = shaft[x : x + 1, :]
        here = slot_row == jnp.broadcast_to(slot >> 7, (16, 128))
        left = jnp.concatenate(
            [jnp.where(here, float(x), 0.0), jnp.where(here, place, 0.0)], axis=0
        )
        right = jnp.where(low_row == jnp.broadcast_to(slot & 127, (128, 128)), 1.0, 0.0)
        where_from = where_from + lax.dot_general(
            left.astype(bf16),
            right.astype(bf16),
            (((1,), (1,)), ((), ())),
            preferred_element_type=f32,
        )
    origin[...] = where_from.astype(jnp.int32) & 127


def total_kernel(arrived, donor, counts, out, rows, sums):
    lane = iota((8, 128), 1)
    row256 = iota((256, WIDTH), 0).astype(bf16)
    blocks = [((iota((16, WIDTH), 0) + 16 * t) // 20).astype(bf16) for t in range(20)]
    one = jnp.ones((), bf16)
    zero = jnp.zeros((), bf16)
    ids = [joined_rows(donor.at[0, g]) for g in range(4)]
    result = jnp.zeros((320, 256), f32)
    for step in range(8192 // WIDTH):
        cells = []
        for part in range(WIDTH // 128):
            chunk = WIDTH // 128 * step + part
            cells.append(ids[chunk // 16][chunk % 16 : chunk % 16 + 1])
            x = arrived[16 * chunk : 16 * chunk + 16, :]
            span = slice(128 * part, 128 * part + 128)
            for c, value in enumerate(halves(x[:8], x[8:], lane)):
                value = value[:5]
                big = value.astype(bf16).astype(f32)
                for i, piece in enumerate((big, value - big)):
                    start = 40 * step + 10 * i + 5 * c
                    rows[start : start + 5, span] = piece
                    rows[start + 20 : start + 25, span] = piece
        cell = jnp.concatenate(cells, axis=1)
        high = jnp.broadcast_to(cell >> 8, (16, WIDTH)).astype(bf16)
        low = jnp.broadcast_to(cell & 255, (256, WIDTH)).astype(bf16)
        hot = jnp.where(row256 == low, one, zero)
        tiles = [rows[40 * step + o : 40 * step + o + 16, :].astype(bf16) for o in (0, 16, 12, 8, 4)]
        left = jnp.concatenate(
            [jnp.where(high == blocks[t], tiles[t % 5], zero) for t in range(20)], axis=0
        )
        result = result + lax.dot_general(
            left, hot, (((1,), (1,)), ((), ())), preferred_element_type=f32
        )
    sums[...] = result
    for h in range(16):
        total = sums[20 * h : 20 * h + 10, :] + sums[20 * h + 10 : 20 * h + 20, :]
        total = total / jnp.maximum(counts[h : h + 1, :], 1.0)
        span = slice(256 * h, 256 * h + 256)
        for l in range(5):
            out[l, 0:1, span] = total[l : l + 1]
            out[l, 1:2, span] = total[5 + l : 6 + l]


def shape(*sizes):
    return jax.ShapeDtypeStruct(sizes, f32)


def near_pairs(count):
    even = [(i, i ^ 1) for i in range(count)]
    odd = []
    for i in range(1, count - 1, 2):
        odd += [(i, i + 1), (i + 1, i)]
    return even, odd


def shards(
    ice_depth,
    heat_state,
    elevation_slope_components,
    sliding_drag,
    adjacent_polygons,
    edge_timing_ratio,
    edge_average_normal_speed,
    tier_edge_normal_speed,
    position_donor_polygons,
    shaft_holding_position,
    prior_node_motion,
):
    ice = ice_depth.reshape(32, 128)
    drag = sliding_drag.reshape(32, 128)
    outgoing, near_out, far_out, own = pl.pallas_call(
        pack_kernel,
        out_shape=(
            shape(32 * BLOCK_ROWS, 128),
            shape(MSG_ROWS, 128),
            shape(MSG_ROWS, 128),
            shape(6, 32, 128),
        ),
        in_specs=[pl.BlockSpec(memory_space=pltpu.HBM)] * 7,
        out_specs=[pl.BlockSpec(memory_space=pltpu.HBM)] * 4,
        scratch_shapes=[
            pltpu.VMEM((32, 128), f32),
            pltpu.VMEM((LAYERS, 4096), f32),
            pltpu.VMEM((2, 4096), f32),
            pltpu.VMEM((32, 128), f32),
            pltpu.VMEM((32, 64), jnp.int32),
            pltpu.VMEM((4, 128), jnp.int32),
            pltpu.VMEM((2, LEVELS, 4, 128), f32),
            pltpu.VMEM((32 * BLOCK_ROWS, 128), f32),
            pltpu.VMEM((MSG_ROWS, 128), f32),
            pltpu.VMEM((MSG_ROWS, 128), f32),
            pltpu.VMEM((6, 32, 128), f32),
            pltpu.SemaphoreType.DMA((7,)),
            pltpu.SemaphoreType.DMA((5,)),
        ],
        compiler_params=WIDE,
        name="pack",
    )(
        ice,
        heat_state,
        elevation_slope_components,
        drag,
        position_donor_polygons,
        shaft_holding_position,
        prior_node_motion,
    )
    arrived = lax.all_to_all(
        outgoing.reshape(32, 1, BLOCK_ROWS * 128), "dom", split_axis=0, concat_axis=0, tiled=True
    ).reshape(32 * BLOCK_ROWS, 128)
    even, odd = near_pairs(lax.axis_size("dom"))
    near = lax.ppermute(near_out, "dom", even)
    far = lax.ppermute(far_out, "dom", odd)
    donor, shaft, near_out = lax.optimization_barrier(
        (position_donor_polygons, shaft_holding_position, near_out)
    )
    origin, counts = pl.pallas_call(
        prepare_kernel,
        out_shape=(jax.ShapeDtypeStruct((32, 128), jnp.int32), shape(16, 256)),
        scratch_shapes=[pltpu.VMEM((16, 8192), bf16), pltpu.VMEM((256, 8192), bf16)],
        compiler_params=PARAMS,
        name="prepare",
    )(donor, shaft)
    arrived, origin = lax.optimization_barrier((arrived, origin))
    geo, vext, edge = pl.pallas_call(
        column_kernel,
        out_shape=(shape(FIELDS, 8, 128), shape(2 * LEVELS, 8, 128), shape(56, 128)),
        scratch_shapes=[pltpu.VMEM((8, 128), jnp.int32)],
        compiler_params=PARAMS,
        name="columns",
    )(arrived, shaft_holding_position, near, far, prior_node_motion)
    even, odd = near_pairs(lax.axis_size("grp"))
    edge_near = lax.ppermute(edge, "grp", even)
    edge_far = lax.ppermute(edge, "grp", odd)
    partial = pl.pallas_call(
        inner_kernel,
        out_shape=shape(4 * LEVELS, 8, 128),
        compiler_params=PARAMS,
        name="inner",
    )(geo, vext)
    node_velocity, send = pl.pallas_call(
        ice_kernel,
        out_shape=(shape(2, LEVELS, 4, 128), shape(1024, 128)),
        scratch_shapes=[
            pltpu.VMEM((LAYERS, 8, 128), f32),
            pltpu.VMEM((2 * LEVELS, 8, 128), f32),
            pltpu.VMEM((2 * LEVELS, 8, 128), f32),
            pltpu.VMEM((2 * LAYERS * 8, 128), f32),
            pltpu.VMEM((2, LEVELS, 4, 128), f32),
            pltpu.VMEM((1024, 128), f32),
            pltpu.SemaphoreType.DMA((9,)),
        ],
        out_specs=[pl.BlockSpec(memory_space=pltpu.HBM)] * 2,
        compiler_params=PARAMS,
        name="velocity",
    )(geo, vext, partial, edge, edge_near, edge_far, origin)
    back = lax.all_to_all(send, ("grp", "dom"), split_axis=0, concat_axis=0, tiled=True)
    depth, heat = pl.pallas_call(
        advect_kernel,
        out_shape=(shape(32, 128), shape(5, 4096)),
        scratch_shapes=[pltpu.VMEM((6, 48, 128), f32)],
        compiler_params=PARAMS,
        name="advect",
    )(
        own,
        adjacent_polygons,
        edge_timing_ratio,
        edge_average_normal_speed,
        tier_edge_normal_speed,
        near,
        far,
    )
    tier_motion = pl.pallas_call(
        total_kernel,
        out_shape=shape(5, 2, 4096),
        scratch_shapes=[
            pltpu.VMEM((8192 // WIDTH * 40, WIDTH), f32),
            pltpu.VMEM((320, 256), f32),
        ],
        compiler_params=PARAMS,
        name="totals",
    )(back, position_donor_polygons, counts)
    return (depth.reshape(4096), heat, node_velocity, jnp.transpose(tier_motion, (1, 0, 2)))


def solution(mesh):
    in_specs = (
        P("dom"),
        P(None, "dom"),
        P(None, "dom"),
        P("dom"),
        P(None, "dom"),
        P(None, "dom"),
        P(None, "dom"),
        P("grp", None, "dom"),
        P("dom", None, None, None),
        P("dom", "grp"),
        P(None, None, "dom", "grp"),
    )
    out_specs = (P("dom"), P("grp", "dom"), P(None, None, "dom", "grp"), P(None, "grp", "dom"))
    return jax.shard_map(shards, mesh=mesh, in_specs=in_specs, out_specs=out_specs, check_vma=False)
```

```python
import math

import jax
import jax.numpy as jnp
from jax import lax
from jax.experimental import pallas as pl
from jax.experimental.pallas import tpu as pltpu
from jax.sharding import PartitionSpec as P

KAPPA = 1.0 / math.sqrt(3.0)
EPS_RATE = 0.01
LOG2E = math.log2(math.e)
SCALE = 4096.0
LAYERS = 20
LEVELS = 21
FIELDS = 24
PAIRS = 12
BLOCK_ROWS = 36
MSG_ROWS = 88
RIM_ROWS = 48
WIDTH = 256
f32 = jnp.float32
bf16 = jnp.bfloat16
PARAMS = pltpu.CompilerParams(vmem_limit_bytes=32 * 1024 * 1024)
WIDE = pltpu.CompilerParams(vmem_limit_bytes=60 * 1024 * 1024)


def lanes_of(table, index):
    return jnp.take_along_axis(table, index, axis=1, mode="promise_in_bounds")


def iota(shape, dim):
    return lax.broadcasted_iota(jnp.int32, shape, dim)


def row_of(ref, row, rows):
    return jnp.broadcast_to(ref[pl.ds(row, 1), :], (rows, 128))


def halves(first, second, lane):
    even = jnp.where(lane < 64, first, pltpu.roll(second, 64, 1))
    odd = jnp.where(lane < 64, pltpu.roll(first, 64, 1), second)
    return even, odd


def joined_rows(rows):
    return jnp.concatenate([rows[pl.ds(0, 16, stride=2), :], rows[pl.ds(1, 16, stride=2), :]], axis=1)


def pack_kernel(
    ice_in, heat_in, slope_in, drag_in, donor_in, shaft_in, prior_in,
    out_to, near_to, far_to, own_to, near_rim_to, far_rim_to,
    ice, heat, slope, drag, donor, shaft, prior, out, near, far, own, near_rim, far_rim, arrivals, leaves,
):
    g = lax.axis_index("grp")
    d = lax.axis_index("dom")
    pairs = (
        (heat_in, heat),
        (donor_in.at[0, g], donor),
        (ice_in, ice),
        (slope_in, slope),
        (drag_in, drag),
        (shaft_in, shaft),
        (prior_in, prior),
    )
    copies = [pltpu.make_async_copy(a, b, arrivals.at[i]) for i, (a, b) in enumerate(pairs)]
    for copy in copies:
        copy.start()
    out[0:12, :] = jnp.zeros((12, 128), f32)
    out[31 * 36 + 24 : 31 * 36 + 36, :] = jnp.zeros((12, 128), f32)
    for copy in copies[:5]:
        copy.wait()
    leaving = []
    ids = jnp.maximum(joined_rows(donor), 0)
    high = ids >> 7
    low = ids & 127
    lane = iota((8, 128), 1)
    highs = [high[:8], high[8:]]
    lows = [low[:8], low[8:]]

    def table(field, k):
        if field == 0:
            part = ice[k : k + 1, :]
        elif field < 3:
            part = slope[field - 1 : field, 128 * k : 128 * k + 128]
        elif field == 3:
            part = drag[k : k + 1, :]
        else:
            part = heat[field - 4 : field - 3, 128 * k : 128 * k + 128]
        return jnp.broadcast_to(part, (8, 128))

    for v in range(2):
        found = [jnp.zeros((8, 128), f32)] * FIELDS
        for k in range(32):
            here = highs[v] == k
            for f in range(FIELDS):
                found[f] = jnp.where(here, lanes_of(table(f, k), lows[v]), found[f])
        at = 576 * v
        for p in range(PAIRS):
            even, odd = halves(found[p], found[p + PAIRS], lane)
            out[pl.ds(at + 12 + p, 8, stride=72), :] = even
            out[pl.ds(at + 36 + p, 8, stride=72), :] = even
            if v == 0:
                out[pl.ds(60 + p, 7, stride=72), :] = even[1:]
                out[pl.ds(72 + p, 8, stride=72), :] = odd
            else:
                out[pl.ds(at - 12 + p, 8, stride=72), :] = even
                out[pl.ds(at + 72 + p, 7, stride=72), :] = odd[:7]
            out[pl.ds(at + 48 + p, 8, stride=72), :] = odd
            out[pl.ds(at + 24 + p, 8, stride=72), :] = odd
        span = slice(0, 536) if v == 0 else slice(536, 1152)
        copy = pltpu.make_async_copy(out.at[span], out_to.at[span], leaves.at[5 + v])
        copy.start()
        leaving.append(copy)
    for copy in copies[5:]:
        copy.wait()
    own[0] = ice[...]
    for part in range(4):

        @pl.when(g == part)
        def _():
            for i in range(5):
                layer = 5 * part + i
                for k in range(32):
                    own[i + 1, k : k + 1, :] = heat[layer : layer + 1, 128 * k : 128 * k + 128]

    def message(msg, rim, row0, chunk0):
        for c in range(2):
            for z in range(LEVELS):
                at = 2 * (c * LEVELS + z)
                msg[at : at + 2, :] = prior[c, z, row0 : row0 + 2, :]
        msg[84:86, :] = shaft[row0 : row0 + 2, :].astype(f32)
        msg[86:88, :] = jnp.zeros((2, 128), f32)
        for i in range(6):
            rim[8 * i : 8 * i + 8, :] = own[i, chunk0 : chunk0 + 8, :]

    even_device = d % 2 == 0

    @pl.when(even_device)
    def _():
        message(near, near_rim, 2, 24)
        message(far, far_rim, 0, 0)

    @pl.when(jnp.logical_not(even_device))
    def _():
        message(near, near_rim, 0, 0)
        message(far, far_rim, 2, 24)

    for i, (a, b) in enumerate(
        (
            (near, near_to),
            (far, far_to),
            (own, own_to),
            (near_rim, near_rim_to),
            (far_rim, far_rim_to),
        )
    ):
        copy = pltpu.make_async_copy(a, b, leaves.at[i])
        copy.start()
        leaving.append(copy)
    for copy in leaving:
        copy.wait()


def advect_kernel(own, adjacent, ratio, mean_speed, tier_speed, near, far, depth_out, heat_out, ext):
    d = lax.axis_index("dom")
    even_device = d % 2 == 0
    for i in range(6):
        a = near[8 * i : 8 * i + 8, :]
        b = far[8 * i : 8 * i + 8, :]
        ext[i, 0:8, :] = jnp.where(even_device, b, a)
        ext[i, 40:48, :] = jnp.where(even_device, a, b)
        ext[i, 8:40, :] = own[i]

    @pl.loop(0, 32)
    def _(k):
        span = pl.ds(pl.multiple_of(128 * k, 128), 128)
        cell = adjacent[:, span] - (d * 4096 - 1024)
        low = cell & 127
        turn = (cell >> 7) - k
        beside = [jnp.zeros((6, 128), f32) for _ in range(6)]
        for r in range(17):
            here = turn == r
            for i in range(6):
                rows = jnp.broadcast_to(ext[i, pl.ds(k + r, 1), :], (6, 128))
                beside[i] = jnp.where(here, lanes_of(rows, low), beside[i])
        weight = ratio[:, span]
        for i in range(6):
            here = ext[i, pl.ds(k + 8, 1), :]
            speed = mean_speed[:, span] if i == 0 else tier_speed[i - 1, :, span]
            flow = weight * (jnp.maximum(speed, 0.0) * here + jnp.minimum(speed, 0.0) * beside[i])
            result = here - jnp.sum(flow, axis=0, keepdims=True)
            if i == 0:
                depth_out[pl.ds(k, 1), :] = result
            else:
                heat_out[i - 1 : i, span] = result


def column_kernel(arrived, shaft, near, far, prior, geo, vext, edge, slots):
    d = lax.axis_index("dom")
    even_device = d % 2 == 0
    row = iota((8, 128), 0)
    lane = iota((8, 128), 1)

    def sides(start, count):
        a = near[start : start + count, :]
        b = far[start : start + count, :]
        return jnp.where(even_device, b, a), jnp.where(even_device, a, b)

    left, right = sides(84, 2)
    slots[0:2, :] = left.astype(jnp.int32)
    slots[2:6, :] = shaft[...]
    slots[6:8, :] = right.astype(jnp.int32)
    slot = slots[...]
    owner = slot >> 6
    low = slot & 63
    low2 = low + 64
    found = [jnp.zeros((8, 128), f32) for _ in range(FIELDS)]
    upper = row < 2
    middle = row < 6
    for p in range(32):
        here = owner == p
        for f in range(PAIRS):
            at = BLOCK_ROWS * p + f
            rows = jnp.where(
                upper,
                row_of(arrived, at, 8),
                jnp.where(middle, row_of(arrived, at + 12, 8), row_of(arrived, at + 24, 8)),
            )
            found[f] = jnp.where(here, lanes_of(rows, low), found[f])
            found[f + PAIRS] = jnp.where(here, lanes_of(rows, low2), found[f + PAIRS])
    first = jnp.where(d == 0, 2, 0)
    last = jnp.where(d == lax.axis_size("dom") - 1, 5, 7)
    inside = jnp.logical_and(row >= first, row <= last)
    found = [jnp.where(inside, value, 0.0) for value in found]
    load_u = -(found[0] * found[1]) * SCALE
    load_v = -(found[0] * found[2]) * SCALE
    friction = found[3] * SCALE
    geo[0] = found[0]
    geo[1] = load_u
    geo[2] = load_v
    geo[3] = friction
    for l in range(LAYERS):
        geo[4 + l] = found[4 + l]
    for cz in range(2 * LEVELS):
        left, right = sides(2 * cz, 2)
        vext[cz, 0:2, :] = left
        vext[cz, 2:6, :] = prior[cz // LEVELS, cz % LEVELS]
        vext[cz, 6:8, :] = right
    group = lane // LEVELS
    pick = jnp.where(group < 2, group, jnp.where(group < 4, 124 + group, 0))
    level = lane - group * LEVELS
    for c in range(2):
        value = jnp.zeros((8, 128), f32)
        for z in range(LEVELS):
            value = jnp.where(level == z, lanes_of(vext[c * LEVELS + z], pick), value)
        edge[8 * c : 8 * c + 8, :] = value
    value = jnp.zeros((8, 128), f32)
    for l in range(LAYERS):
        value = jnp.where(level == l, lanes_of(found[4 + l], pick), value)
    edge[16:24, :] = value
    edge[24:32, :] = lanes_of(found[0], pick)
    edge[32:40, :] = lanes_of(load_u, pick)
    edge[40:48, :] = lanes_of(load_v, pick)
    edge[48:56, :] = jnp.where(level == 0, lanes_of(friction, pick), 0.0)


def interpolate(a, b):
    diff = b - a
    total = a + b
    part = KAPPA * diff
    return diff, total - part, total + part


def spread(a, b):
    total = a + b
    part = KAPPA * (a - b)
    return total, part


def spread_square(a, b):
    total = (1.0 + KAPPA * KAPPA) * (a + b)
    part = (2.0 * KAPPA) * (a - b)
    return total + part, total - part


def up_x(value):
    return pltpu.roll(value, 7, 0)


def down_x(value):
    return pltpu.roll(value, 1, 0)


def level_terms(value, value_y):
    dy, ya, yb = interpolate(value, value_y)
    _, along_y0, along_y1 = interpolate(dy, up_x(dy))
    along_x0, z00, z10 = interpolate(ya, up_x(ya))
    along_x1, z01, z11 = interpolate(yb, up_x(yb))
    return [along_x0, along_x1, along_y0, along_y1, z00, z01, z10, z11]


def element(low_u, top_u, low_v, top_v, hard, inverse2, keep=None):
    def gradients(low, top):
        x = [interpolate(low[q], top[q])[1:] for q in (0, 1)]
        y = [interpolate(low[2 + q], top[2 + q])[1:] for q in (0, 1)]
        z = [top[4 + q] - low[4 + q] for q in range(4)]
        return x, y, z

    ux, uy, uz = gradients(low_u, top_u)
    vx, vy, vz = gradients(low_v, top_v)
    vertical = [
        (uz[q] * uz[q] + vz[q] * vz[q]) * (0.25 * inverse2) + EPS_RATE for q in range(4)
    ]
    vy2 = [[vy[a][b] * vy[a][b] for b in (0, 1)] for a in (0, 1)]
    ex, ey, ez = {}, {}, {}
    ev, eu, wx, wy = {}, {}, {}, {}

    def put(store, key, value):
        store[key] = value if key not in store else store[key] + value

    for qx in (0, 1):
        for qy in (0, 1):
            for qz in (0, 1):
                a = ux[qy][qz]
                b = vy[qx][qz]
                shear = uy[qx][qz] + vx[qy][qz]
                rate = (
                    a * (a + b) + vy2[qx][qz] + 0.25 * (shear * shear) + vertical[2 * qx + qy]
                )
                eta = jnp.exp2(hard - jnp.log2(rate) * (1.0 / 3.0))
                if keep is not None:
                    eta = jnp.where(keep, eta, 0.0)
                put(ex, (qy, qz), eta)
                put(ey, (qx, qz), eta)
                put(ez, 2 * qx + qy, eta)
                put(ev, (qy, qz), eta * b)
                put(eu, (qx, qz), eta * a)
                w = eta * shear
                put(wx, (qy, qz), w)
                put(wy, (qx, qz), w)
    ez = [ez[q] * inverse2 for q in range(4)]
    lows, tops = [], []

    def add_spread(a, b):
        total, part = spread(a, b)
        lows.append(total + part)
        tops.append(total - part)

    def flux(e, g, s):
        half = (g + g) * e + s
        return half + half

    for q in (0, 1):
        add_spread(*[flux(ex[q, z], ux[q][z], ev[q, z]) for z in (0, 1)])
    for q in (0, 1):
        add_spread(wy[q, 0], wy[q, 1])
    for q in range(4):
        value = ez[q] * uz[q]
        lows.append(-value)
        tops.append(value)
    for q in (0, 1):
        add_spread(wx[q, 0], wx[q, 1])
    for q in (0, 1):
        add_spread(*[flux(ey[q, z], vy[q][z], eu[q, z]) for z in (0, 1)])
    for q in range(4):
        value = ez[q] * vz[q]
        lows.append(-value)
        tops.append(value)
    for q in (0, 1):
        a, b = spread_square(ex[q, 0], ex[q, 1])
        lows.append(a)
        tops.append(b)
    for q in (0, 1):
        a, b = spread_square(ey[q, 0], ey[q, 1])
        lows.append(a)
        tops.append(b)
    lows += ez
    tops += ez
    return lows, tops


def node_parts(acc):
    results = []
    for c in (0, 1):
        x0, x1, y0, y1, z00, z01, z10, z11 = acc[8 * c : 8 * c + 8]
        total, part = spread(y0, y1)
        hd = (total + part) + down_x(total - part)
        both = []
        for along, a, b in ((x0, z00, z10), (x1, z01, z11)):
            total, part = spread(a, b)
            part = part - along
            both.append((total + part) + down_x(total - part))
        total, part = spread(both[0], both[1])
        part = part - hd
        results.append((total + part, total - part))
    x0, x1, y0, y1, z00, z01, z10, z11 = acc[16:24]
    hx = [x0 + down_x(x0), x1 + down_x(x1)]
    a, b = spread_square(y0, y1)
    hy = a + down_x(b)
    hz = []
    for za, zb in ((z00, z10), (z01, z11)):
        a, b = spread_square(za, zb)
        hz.append(a + down_x(b))
    a, b = spread_square(4.0 * hx[0] + hz[0], 4.0 * hx[1] + hz[1])
    results.append((a + hy, b + hy))
    hy4 = 4.0 * hy
    a, b = spread_square(hx[0] + hz[0], hx[1] + hz[1])
    results.append((a + hy4, b + hy4))
    return results


def corners(value, value_y):
    pair = value + value_y
    return pair + up_x(pair)


def geometry(depth4):
    dz = depth4 * (0.25 / LAYERS)
    dz = jnp.where(dz > 0.0, dz, 1.0)
    inverse = 0.25 / dz
    return jnp.log2(dz * 16.0), inverse * inverse


def hardness(log_depth, warmth4):
    return log_depth - (0.25 * LOG2E) * warmth4


def at_lane(value, index):
    return lanes_of(value, jnp.full((8, 128), index, jnp.int32))


def up_y(value):
    return pltpu.roll(value, 127, 1)


def down_y(value):
    return pltpu.roll(value, 1, 1)


def levels(source, next_u, next_v, hard, inverse2, finish):
    def terms(z):
        u = source[z]
        v = source[LEVELS + z]
        return level_terms(u, next_u(z, u)) + level_terms(v, next_v(z, v))

    def body(z, carry):
        low, tops = carry[:16], carry[16:]
        top = terms(z + 1)
        lows, next_tops = element(low[:8], top[:8], low[8:], top[8:], hard(z), inverse2)
        finish(z, node_parts([a + b for a, b in zip(lows, tops)]))
        return (*top, *next_tops)

    zero = jnp.zeros((8, 128), f32)
    carry = (*terms(0), *([zero] * 24))
    for z in range(LAYERS):
        carry = body(z, carry)
    finish(LAYERS, node_parts(list(carry[16:])))


def inner_kernel(geo, vext, partial):
    lane = iota((8, 128), 1)
    depth = geo[0]
    log_depth, inverse2 = geometry(corners(depth, up_y(depth)))

    def hard(z):
        warm = geo[4 + z]
        return hardness(log_depth, corners(warm, up_y(warm)))

    def beside(z, value):
        return up_y(value)

    def finish(z, results):
        for q, (a, b) in enumerate(results):
            partial[q * LEVELS + z] = jnp.where(lane == 127, 0.0, a) + jnp.where(
                lane == 0, 0.0, down_y(b)
            )

    levels(vext, beside, beside, hard, inverse2, finish)


def ice_kernel(
    geo, vext, partial, edge, edge_near, edge_far, origin, out_v_to, send_to,
    hard, first, second, means, out_v, send, leaves,
):
    g = lax.axis_index("grp")
    d = lax.axis_index("dom")
    groups = lax.axis_size("grp")
    domains = lax.axis_size("dom")
    row = iota((8, 128), 0)
    lane = iota((8, 128), 1)
    group = lane // LEVELS
    level = lane - group * LEVELS
    even_group = g % 2 == 0

    def edge_field(i):
        span = slice(8 * i, 8 * i + 8)
        own = edge[span, :]
        a = edge_near[span, :]
        b = edge_far[span, :]
        left = jnp.where(even_group, b, a)
        right = jnp.where(even_group, a, b)
        return jnp.where(
            lane < 42,
            pltpu.roll(left, 86, 1),
            jnp.where(
                lane < 63,
                pltpu.roll(own, 42, 1),
                jnp.where(lane < 84, own, pltpu.roll(right, 84, 1)),
            ),
        )

    edge_u, edge_v, edge_t, edge_h, edge_fu, edge_fv, edge_b = [edge_field(i) for i in range(7)]

    def edge_up(value):
        return pltpu.roll(value, 107, 1)

    def joined(value, beyond, index):
        return jnp.where(lane == 127, pltpu.roll(beyond, 127 - index, 1), up_y(value))

    edge_log, edge_inv2 = geometry(corners(edge_h, edge_up(edge_h)))
    edge_hard = hardness(edge_log, corners(edge_t, edge_up(edge_t)))
    depth = geo[0]
    main_log, main_inv2 = geometry(corners(depth, joined(depth, edge_h, 84)))
    for l in range(LAYERS):
        warm = geo[4 + l]
        hard[l] = hardness(main_log, corners(warm, joined(warm, edge_t, 84 + l)))

    load_u = geo[1]
    load_v = geo[2]
    friction = geo[3]
    keep = jnp.logical_and(level != LAYERS, lane < 6 * LEVELS)
    first_row = jnp.where(d == 0, 2, 1)
    last_row = jnp.where(d == domains - 1, 5, 6)
    inside = jnp.logical_and(row >= first_row, row <= last_row)
    edge_inside = jnp.logical_and(
        inside,
        jnp.logical_or(
            jnp.logical_and(group == 1, g > 0),
            jnp.logical_and(group == 4, g < groups - 1),
        ),
    )

    def edge_parts(u, v):
        low_u = level_terms(u, edge_up(u))
        low_v = level_terms(v, edge_up(v))
        top_u = [up_y(t) for t in low_u]
        top_v = [up_y(t) for t in low_v]
        lows, tops = element(low_u, top_u, low_v, top_v, edge_hard, edge_inv2, keep)
        return node_parts([a + down_y(b) for a, b in zip(lows, tops)])

    def stepped(value, load, force, diagonal, drag):
        return value + 0.5 * (load - force - drag * value) / (diagonal + drag)

    parts = edge_parts(edge_u, edge_v)
    for z in range(LEVELS):
        sums = []
        for q, (a, b) in enumerate(parts):
            rim = jnp.where(lane == 127, pltpu.roll(a, 64 - z, 1), 0.0)
            rim = jnp.where(lane == 0, pltpu.roll(b, 107 - z, 1), rim)
            sums.append(partial[q * LEVELS + z] + rim)
        fu, fv, du, dv = sums
        drag = friction if z == 0 else 0.0
        first[z] = jnp.where(inside, stepped(vext[z], load_u, fu, du, drag), 0.0)
        first[LEVELS + z] = jnp.where(inside, stepped(vext[LEVELS + z], load_v, fv, dv, drag), 0.0)

    def edge_final(c, value, load):
        (fa, fb), (da, db) = parts[c], parts[2 + c]
        force = fa + pltpu.roll(fb, LEVELS, 1)
        diagonal = da + pltpu.roll(db, LEVELS, 1)
        return jnp.where(edge_inside, stepped(value, load, force, diagonal, edge_b), 0.0)

    edge_u = edge_final(0, edge_u, edge_fu)
    edge_v = edge_final(1, edge_v, edge_fv)
    for z in range(LEVELS):
        here = lane == 42 + z
        edge_u = jnp.where(here, pltpu.roll(first[z], 42 + z, 1), edge_u)
        edge_v = jnp.where(here, pltpu.roll(first[LEVELS + z], 42 + z, 1), edge_v)
    beyond = [b for _, b in edge_parts(edge_u, edge_v)]

    def finish(z, results):
        fu, fv, du, dv = [
            a + jnp.where(lane == 0, pltpu.roll(e, 107 - z, 1), down_y(b))
            for (a, b), e in zip(results, beyond)
        ]
        drag = friction if z == 0 else 0.0
        second[z] = stepped(first[z], load_u, fu, du, drag)
        second[LEVELS + z] = stepped(first[LEVELS + z], load_v, fv, dv, drag)

    levels(
        first,
        lambda z, value: joined(value, edge_u, 84 + z),
        lambda z, value: joined(value, edge_v, 84 + z),
        lambda z: hard[z],
        main_inv2,
        finish,
    )
    for c in range(2):
        for z in range(LEVELS):
            out_v[c, z] = second[c * LEVELS + z, 2:6, :]
    leaving = [pltpu.make_async_copy(out_v, out_v_to, leaves.at[0])]
    leaving[0].start()
    for c in range(2):
        for l in range(LAYERS):
            at = c * LEVELS + l
            means[8 * (c * LAYERS + l) : 8 * (c * LAYERS + l) + 8, :] = 0.5 * (
                second[at] + second[at + 1]
            )
    send[...] = jnp.zeros(send.shape, f32)
    for v in range(2):
        from_x = origin[8 * v : 8 * v + 8]
        from_y = origin[16 + 8 * v : 24 + 8 * v]
        here = [from_x == x for x in range(4)]
        for part in range(4):
            values = [jnp.zeros((8, 128), f32)] * 10
            for x in range(4):
                for i in range(10):
                    at = 8 * (i // 5 * LAYERS + 5 * part + i % 5) + 2 + x
                    values[i] = jnp.where(here[x], lanes_of(row_of(means, at, 8), from_y), values[i])
            for l in range(5):
                even, odd = halves(values[l], values[5 + l], lane)
                start = part * 256 + 128 * v + l
                send[pl.ds(start, 8, stride=16), :] = even
                send[pl.ds(start + 8, 8, stride=16), :] = odd
        for part in range(4):
            span = slice(256 * part + 128 * v, 256 * part + 128 * v + 128)
            copy = pltpu.make_async_copy(send.at[span], send_to.at[span], leaves.at[1 + 4 * v + part])
            copy.start()
            leaving.append(copy)
    for copy in leaving:
        copy.wait()


def prepare_kernel(donor, shaft, origin, counts, left, hot):
    row256 = iota((256, 128), 0).astype(bf16)
    row16 = iota((16, 128), 0).astype(bf16)
    one = jnp.ones((), bf16)
    zero = jnp.zeros((), bf16)
    for g in range(4):
        ids = joined_rows(donor.at[0, g])
        for t in range(16):
            span = slice(2048 * g + 128 * t, 2048 * g + 128 * t + 128)
            cell = ids[t : t + 1]
            low = jnp.broadcast_to(cell & 255, (256, 128)).astype(bf16)
            hot[:, span] = jnp.where(row256 == low, one, zero)
            high = jnp.broadcast_to(cell >> 8, (16, 128)).astype(bf16)
            left[:, span] = jnp.where(row16 == high, one, zero)
    counts[...] = lax.dot_general(
        left[...], hot[...], (((1,), (1,)), ((), ())), preferred_element_type=f32
    )
    slot_row = iota((16, 128), 0)
    place = iota((16, 128), 1).astype(f32)
    low_row = iota((128, 128), 0)
    where_from = jnp.zeros((32, 128), f32)
    for x in range(4):
        slot = shaft[x : x + 1, :]
        here = slot_row == jnp.broadcast_to(slot >> 7, (16, 128))
        left = jnp.concatenate(
            [jnp.where(here, float(x), 0.0), jnp.where(here, place, 0.0)], axis=0
        )
        right = jnp.where(low_row == jnp.broadcast_to(slot & 127, (128, 128)), 1.0, 0.0)
        where_from = where_from + lax.dot_general(
            left.astype(bf16),
            right.astype(bf16),
            (((1,), (1,)), ((), ())),
            preferred_element_type=f32,
        )
    origin[...] = where_from.astype(jnp.int32) & 127


def total_kernel(arrived, donor, counts, out, rows, sums):
    lane = iota((8, 128), 1)
    row256 = iota((256, WIDTH), 0).astype(bf16)
    blocks = [((iota((16, WIDTH), 0) + 16 * t) // 20).astype(bf16) for t in range(20)]
    one = jnp.ones((), bf16)
    zero = jnp.zeros((), bf16)
    ids = [joined_rows(donor.at[0, g]) for g in range(4)]
    result = jnp.zeros((320, 256), f32)
    for step in range(8192 // WIDTH):
        cells = []
        for part in range(WIDTH // 128):
            chunk = WIDTH // 128 * step + part
            cells.append(ids[chunk // 16][chunk % 16 : chunk % 16 + 1])
            x = arrived[16 * chunk : 16 * chunk + 16, :]
            span = slice(128 * part, 128 * part + 128)
            for c, value in enumerate(halves(x[:8], x[8:], lane)):
                value = value[:5]
                big = value.astype(bf16).astype(f32)
                for i, piece in enumerate((big, value - big)):
                    start = 40 * step + 10 * i + 5 * c
                    rows[start : start + 5, span] = piece
                    rows[start + 20 : start + 25, span] = piece
        cell = jnp.concatenate(cells, axis=1)
        high = jnp.broadcast_to(cell >> 8, (16, WIDTH)).astype(bf16)
        low = jnp.broadcast_to(cell & 255, (256, WIDTH)).astype(bf16)
        hot = jnp.where(row256 == low, one, zero)
        tiles = [rows[40 * step + o : 40 * step + o + 16, :].astype(bf16) for o in (0, 16, 12, 8, 4)]
        left = jnp.concatenate(
            [jnp.where(high == blocks[t], tiles[t % 5], zero) for t in range(20)], axis=0
        )
        result = result + lax.dot_general(
            left, hot, (((1,), (1,)), ((), ())), preferred_element_type=f32
        )
    sums[...] = result
    for h in range(16):
        total = sums[20 * h : 20 * h + 10, :] + sums[20 * h + 10 : 20 * h + 20, :]
        total = total / jnp.maximum(counts[h : h + 1, :], 1.0)
        span = slice(256 * h, 256 * h + 256)
        for l in range(5):
            out[l, 0:1, span] = total[l : l + 1]
            out[l, 1:2, span] = total[5 + l : 6 + l]


def shape(*sizes):
    return jax.ShapeDtypeStruct(sizes, f32)


def near_pairs(count):
    even = [(i, i ^ 1) for i in range(count)]
    odd = []
    for i in range(1, count - 1, 2):
        odd += [(i, i + 1), (i + 1, i)]
    return even, odd


def shards(
    ice_depth,
    heat_state,
    elevation_slope_components,
    sliding_drag,
    adjacent_polygons,
    edge_timing_ratio,
    edge_average_normal_speed,
    tier_edge_normal_speed,
    position_donor_polygons,
    shaft_holding_position,
    prior_node_motion,
):
    ice = ice_depth.reshape(32, 128)
    drag = sliding_drag.reshape(32, 128)
    outgoing, near_out, far_out, own, near_rim, far_rim = pl.pallas_call(
        pack_kernel,
        out_shape=(
            shape(32 * BLOCK_ROWS, 128),
            shape(MSG_ROWS, 128),
            shape(MSG_ROWS, 128),
            shape(6, 32, 128),
            shape(RIM_ROWS, 128),
            shape(RIM_ROWS, 128),
        ),
        in_specs=[pl.BlockSpec(memory_space=pltpu.HBM)] * 7,
        out_specs=[pl.BlockSpec(memory_space=pltpu.HBM)] * 6,
        scratch_shapes=[
            pltpu.VMEM((32, 128), f32),
            pltpu.VMEM((LAYERS, 4096), f32),
            pltpu.VMEM((2, 4096), f32),
            pltpu.VMEM((32, 128), f32),
            pltpu.VMEM((32, 64), jnp.int32),
            pltpu.VMEM((4, 128), jnp.int32),
            pltpu.VMEM((2, LEVELS, 4, 128), f32),
            pltpu.VMEM((32 * BLOCK_ROWS, 128), f32),
            pltpu.VMEM((MSG_ROWS, 128), f32),
            pltpu.VMEM((MSG_ROWS, 128), f32),
            pltpu.VMEM((6, 32, 128), f32),
            pltpu.VMEM((RIM_ROWS, 128), f32),
            pltpu.VMEM((RIM_ROWS, 128), f32),
            pltpu.SemaphoreType.DMA((7,)),
            pltpu.SemaphoreType.DMA((7,)),
        ],
        compiler_params=WIDE,
        name="pack",
    )(
        ice,
        heat_state,
        elevation_slope_components,
        drag,
        position_donor_polygons,
        shaft_holding_position,
        prior_node_motion,
    )
    arrived = lax.all_to_all(
        outgoing.reshape(32, 1, BLOCK_ROWS * 128), "dom", split_axis=0, concat_axis=0, tiled=True
    ).reshape(32 * BLOCK_ROWS, 128)
    even, odd = near_pairs(lax.axis_size("dom"))
    near = lax.ppermute(near_out, "dom", even)
    far = lax.ppermute(far_out, "dom", odd)
    donor, shaft, near_out = lax.optimization_barrier(
        (position_donor_polygons, shaft_holding_position, near_out)
    )
    origin, counts = pl.pallas_call(
        prepare_kernel,
        out_shape=(jax.ShapeDtypeStruct((32, 128), jnp.int32), shape(16, 256)),
        scratch_shapes=[pltpu.VMEM((16, 8192), bf16), pltpu.VMEM((256, 8192), bf16)],
        compiler_params=PARAMS,
        name="prepare",
    )(donor, shaft)
    arrived, origin = lax.optimization_barrier((arrived, origin))
    geo, vext, edge = pl.pallas_call(
        column_kernel,
        out_shape=(shape(FIELDS, 8, 128), shape(2 * LEVELS, 8, 128), shape(56, 128)),
        scratch_shapes=[pltpu.VMEM((8, 128), jnp.int32)],
        compiler_params=PARAMS,
        name="columns",
    )(arrived, shaft_holding_position, near, far, prior_node_motion)
    rims = near_pairs(lax.axis_size("dom"))
    even, odd = near_pairs(lax.axis_size("grp"))
    edge_near = lax.ppermute(edge, "grp", even)
    edge_far = lax.ppermute(edge, "grp", odd)
    partial = pl.pallas_call(
        inner_kernel,
        out_shape=shape(4 * LEVELS, 8, 128),
        compiler_params=PARAMS,
        name="inner",
    )(geo, vext)
    node_velocity, send = pl.pallas_call(
        ice_kernel,
        out_shape=(shape(2, LEVELS, 4, 128), shape(1024, 128)),
        scratch_shapes=[
            pltpu.VMEM((LAYERS, 8, 128), f32),
            pltpu.VMEM((2 * LEVELS, 8, 128), f32),
            pltpu.VMEM((2 * LEVELS, 8, 128), f32),
            pltpu.VMEM((2 * LAYERS * 8, 128), f32),
            pltpu.VMEM((2, LEVELS, 4, 128), f32),
            pltpu.VMEM((1024, 128), f32),
            pltpu.SemaphoreType.DMA((9,)),
        ],
        out_specs=[pl.BlockSpec(memory_space=pltpu.HBM)] * 2,
        compiler_params=PARAMS,
        name="velocity",
    )(geo, vext, partial, edge, edge_near, edge_far, origin)
    back = lax.all_to_all(send, ("grp", "dom"), split_axis=0, concat_axis=0, tiled=True)
    near_rim, far_rim, send = lax.optimization_barrier((near_rim, far_rim, send))
    near_rim = lax.ppermute(near_rim, "dom", rims[0])
    far_rim = lax.ppermute(far_rim, "dom", rims[1])
    depth, heat = pl.pallas_call(
        advect_kernel,
        out_shape=(shape(32, 128), shape(5, 4096)),
        scratch_shapes=[pltpu.VMEM((6, 48, 128), f32)],
        compiler_params=PARAMS,
        name="advect",
    )(
        own,
        adjacent_polygons,
        edge_timing_ratio,
        edge_average_normal_speed,
        tier_edge_normal_speed,
        near_rim,
        far_rim,
    )
    tier_motion = pl.pallas_call(
        total_kernel,
        out_shape=shape(5, 2, 4096),
        scratch_shapes=[
            pltpu.VMEM((8192 // WIDTH * 40, WIDTH), f32),
            pltpu.VMEM((320, 256), f32),
        ],
        compiler_params=PARAMS,
        name="totals",
    )(back, position_donor_polygons, counts)
    return (depth.reshape(4096), heat, node_velocity, jnp.transpose(tier_motion, (1, 0, 2)))


def solution(mesh):
    in_specs = (
        P("dom"),
        P(None, "dom"),
        P(None, "dom"),
        P("dom"),
        P(None, "dom"),
        P(None, "dom"),
        P(None, "dom"),
        P("grp", None, "dom"),
        P("dom", None, None, None),
        P("dom", "grp"),
        P(None, None, "dom", "grp"),
    )
    out_specs = (P("dom"), P("grp", "dom"), P(None, None, "dom", "grp"), P(None, "grp", "dom"))
    return jax.shard_map(shards, mesh=mesh, in_specs=in_specs, out_specs=out_specs, check_vma=False)
```
